32 devices in a mesh: ctx: 8 (over y, x, core), head: 4 (over z).
Axes of the slice: x: 2, y: 2, z: 4, core: 2. Of those that a mesh axis runs over, the one named last changes fastest.
Arguments:
- queries: bfloat16 [1024, 128, 128], P('ctx', 'head'), may hold values from -64 to 64
- key_states: bfloat16 [1024, 8, 128], P('ctx', 'head'), may hold values from -4 to 4
- value_vector_states: bfloat16 [1024, 8, 128], P('ctx', 'head'), may hold values from -6 to 6
- map_query: float32 [128, 128, 64], P('head'), may hold values from -0.5 to 0.5
- map_key: float32 [128, 128, 64], P('head'), may hold values from -0.5 to 0.5
Outputs:
- grad_map_query: float32 [128, 128, 64], P('head')
- grad_map_key: float32 [128, 128, 64], P('head')
The draws below stay inside these ranges and needn't reach their ends.
All inputs are finite; a program needn't handle non-finite values.
Results may differ from the reference program's by a relative error of at most 0.0012.
Values may be sent and summed in bfloat16 or wider, within the bound.
No kernel may reach another device: no remote copies, remote signals or barrier semaphores. Data moves between devices by JAX's collectives and lax.ppermute only.
A program may use at most 192 MiB of HBM per device.

```python
import math
import jax
import jax.numpy as jnp
from jax import lax

QUERY_HEADS = 128
KEY_VALUE_HEADS = 8
HEAD_SIZE = 128
F = 64
TOK_DEV = 128
SEQUENCE_TOKENS = 1024


def attention_pair(key):
    seed_query = jax.random.fold_in(key, 101)
    random_key_seeds = jax.random.fold_in(key, 202)
    queries = jnp.clip(2.0 * jax.random.normal(seed_query, (SEQUENCE_TOKENS, QUERY_HEADS, HEAD_SIZE), jnp.float32), -8.0, 8.0)
    key_row_vectors = jnp.clip(jax.random.normal(random_key_seeds, (SEQUENCE_TOKENS, KEY_VALUE_HEADS, HEAD_SIZE), jnp.float32), -4.0, 4.0)
    return (queries, key_row_vectors)


def draw_queries(key, part):
    return attention_pair(key)[0].astype(jnp.bfloat16)


def draw_key_states(key, part):
    return attention_pair(key)[1].astype(jnp.bfloat16)


def steps_of(stream_key, extent, shards, least, high):
    level, own = 1.0, jax.random.fold_in(stream_key, 6)
    for axis_at, parts in shards:
        draws = jnp.exp(jax.random.uniform(jax.random.fold_in(own, axis_at), (parts,), jnp.float32, least / len(shards), high / len(shards)))
        level = level * jnp.repeat(draws, extent[axis_at] // parts).reshape([-1 if axis == axis_at else 1 for axis in range(len(extent))])
    return level


def scatter_about(key, dims, width, reach, shards=(), held_as=jnp.bfloat16):
    drawn = width * jax.random.normal(key, dims, jnp.float32)
    if shards:
        drawn = drawn * steps_of(key, dims, shards, -0.22, 0.18)
    return jnp.clip(drawn, -reach, reach).astype(held_as)


def setup_inputs(seed: int = 0) -> dict:
    key_list = jax.random.split(jax.random.key(seed), 6)
    return {
        "queries": draw_queries(jax.random.fold_in(key_list[5], 71), 0),
        "key_states": draw_key_states(jax.random.fold_in(key_list[5], 71), 0),
        "value_vector_states": scatter_about(key_list[2], (SEQUENCE_TOKENS, KEY_VALUE_HEADS, HEAD_SIZE), 1.0, 6.0, ((0, 8), (1, 4))),
        "map_query": scatter_about(key_list[3], (QUERY_HEADS, HEAD_SIZE, F), HEAD_SIZE ** -0.5, 0.5, ((0, 4),), jnp.float32),
        "map_key": scatter_about(key_list[4], (QUERY_HEADS, HEAD_SIZE, F), HEAD_SIZE ** -0.5, 0.5, ((0, 4),), jnp.float32),
    }


HIGHEST = lax.Precision.HIGHEST

def feature(values):
    return jnp.concatenate([jax.nn.elu(values) + 1.0, jax.nn.elu(-values) + 1.0], axis=-1)

def teacher_rows(query_rows, key_row_vectors, value_rows):
    score_scale = 1.0 / math.sqrt(HEAD_SIZE)
    scores = jnp.dot(query_rows, key_row_vectors.T, precision=HIGHEST) * score_scale
    causal = jnp.arange(SEQUENCE_TOKENS, dtype=jnp.int32)[None, :] <= jnp.arange(SEQUENCE_TOKENS, dtype=jnp.int32)[:, None]
    scores = jnp.where(causal, scores, -1e+30)
    row_top = lax.optimization_barrier(jnp.max(scores, axis=1, keepdims=True))
    weights = jnp.where(causal, jnp.exp(scores - row_top), 0.0)
    row_total = lax.optimization_barrier(jnp.sum(weights, axis=1, keepdims=True))
    rounded = lax.optimization_barrier(weights.astype(jnp.bfloat16)).astype(jnp.float32)
    return jnp.dot(rounded, value_rows, precision=HIGHEST) / row_total

def head_error(weights, query_rows, key_row_vectors, value_rows, target):
    weight_query, weight_key = weights
    phi_query = feature(jnp.dot(query_rows, weight_query, precision=HIGHEST))
    phi_key = feature(jnp.dot(key_row_vectors, weight_key, precision=HIGHEST))
    blocks = SEQUENCE_TOKENS // TOK_DEV
    feature_width = phi_query.shape[1]
    causal = (jnp.arange(TOK_DEV, dtype=jnp.int32)[None, :] <= jnp.arange(TOK_DEV, dtype=jnp.int32)[:, None]).astype(jnp.float32)

    def advance(carried, inputs):
        state_sum, norm_sum = carried
        block_query, block_key, block_value, block_target = inputs
        inner_scores = jnp.dot(block_query, block_key.T, precision=HIGHEST) * causal
        numerator = jnp.dot(inner_scores, block_value, precision=HIGHEST) + jnp.dot(block_query, state_sum, precision=HIGHEST)
        denominator = lax.optimization_barrier(jnp.sum(inner_scores, axis=1)) + jnp.dot(block_query, norm_sum, precision=HIGHEST)
        student = numerator / denominator[:, None]
        state_sum = state_sum + jnp.dot(block_key.T, block_value, precision=HIGHEST)
        norm_sum = norm_sum + lax.optimization_barrier(jnp.sum(block_key, axis=0))
        mismatch = student - block_target
        return ((state_sum, norm_sum), jnp.sum(mismatch * mismatch))
    initial = (jnp.zeros((feature_width, HEAD_SIZE), jnp.float32), jnp.zeros((feature_width,), jnp.float32))
    stacked = (phi_query.reshape(blocks, TOK_DEV, feature_width), phi_key.reshape(blocks, TOK_DEV, feature_width), value_rows.reshape(blocks, TOK_DEV, HEAD_SIZE), target.reshape(blocks, TOK_DEV, HEAD_SIZE))
    last_state, errors = lax.scan(advance, initial, stacked)
    return jnp.sum(errors)

def reference(queries, key_states, value_vector_states, map_query, map_key):
    query_group_count = QUERY_HEADS // KEY_VALUE_HEADS
    query_major = jnp.transpose(queries.astype(jnp.float32), (1, 0, 2))
    key_major = jnp.transpose(key_states.astype(jnp.float32), (1, 0, 2))
    value_major = jnp.transpose(value_vector_states.astype(jnp.float32), (1, 0, 2))
    head_numbers = jnp.arange(QUERY_HEADS, dtype=jnp.int32)

    def teacher_head(inputs):
        query_rows, head_number = inputs
        group_index = (head_number // query_group_count).astype(jnp.int32)
        key_row_vectors = lax.dynamic_index_in_dim(key_major, group_index, 0, keepdims=False)
        value_rows = lax.dynamic_index_in_dim(value_major, group_index, 0, keepdims=False)
        return teacher_rows(query_rows, key_row_vectors, value_rows)
    teacher = lax.map(teacher_head, (query_major, head_numbers))
    energy = jnp.sum(teacher * teacher)

    def student_grad(inputs):
        query_rows, head_number, weight_query, weight_key, target = inputs
        group_index = (head_number // query_group_count).astype(jnp.int32)
        key_row_vectors = lax.dynamic_index_in_dim(key_major, group_index, 0, keepdims=False)
        value_rows = lax.dynamic_index_in_dim(value_major, group_index, 0, keepdims=False)
        return jax.grad(head_error)((weight_query, weight_key), query_rows, key_row_vectors, value_rows, target)
    grad_query, grad_key = lax.map(student_grad, (query_major, head_numbers, map_query, map_key, teacher))
    factor = QUERY_HEADS / energy
    return (grad_query * factor, grad_key * factor)
```

```python
import functools
import math

import jax
import jax.numpy as jnp
import numpy as np
from jax import lax
from jax.experimental import pallas as pl
from jax.experimental.pallas import tpu as pltpu
from jax.sharding import PartitionSpec as P

F32 = jnp.float32
BF16 = jnp.bfloat16
F16 = jnp.float16
VMEM_LIMIT = 56 * 1024 * 1024
TAIL = 16


def dot(a, b):
    return lax.dot_general(a, b, (((1,), (0,)), ((), ())), preferred_element_type=F32)


def dot_nt(a, b):
    return lax.dot_general(a, b, (((1,), (1,)), ((), ())), preferred_element_type=F32)


def halves(x):
    high = x.astype(BF16)
    return high, (x - high.astype(F32)).astype(BF16)


def beside(*parts):
    return jnp.concatenate(parts, axis=1)


def below(*parts):
    return jnp.concatenate(parts, axis=0)


def feature_and_slope(logit):
    grown = jnp.exp(jnp.minimum(logit, 0.0))
    positive = logit > 0
    return jnp.where(positive, logit + 1.0, grown), jnp.where(positive, 1.0, grown)


def causal(rows, columns, shift):
    row = lax.broadcasted_iota(jnp.int32, (rows, columns), 0)
    column = lax.broadcasted_iota(jnp.int32, (rows, columns), 1)
    return column <= row + shift


def teacher_kernel(scale, rows, q_ref, k_ref, v_ref, out_ref, energy_ref, scores_ref):
    blocks, _, chunk, dim = q_ref.shape
    per_row = rows // chunk
    steps = blocks // per_row
    power = scale * math.log2(math.e)
    mask = causal(rows, rows, 0)

    def finish(r, weighted, total):
        teacher = weighted / total
        for i in range(per_row):
            out_ref[r * per_row + i, 0] = teacher[i * chunk : (i + 1) * chunk]
        return jnp.sum((teacher * teacher).reshape(rows // 8, 8, dim), axis=0)

    def take(ref, r, count=1):
        return ref[pl.ds(r * per_row, count * per_row), 0].reshape(count * rows, dim)

    if steps <= 8:
        energy = jnp.zeros((8, dim), F32)
        for r in range(steps):
            q = take(q_ref, r)
            keys = take(k_ref, 0, r + 1)
            scores = dot_nt(q, keys)
            last = jnp.where(mask, scores[:, r * rows :], -1e30)
            scores = beside(scores[:, : r * rows], last) if r else last
            top = jnp.max(scores, axis=1, keepdims=True)
            weights = jnp.exp2((scores - top) * power)
            total = jnp.sum(weights, axis=1, keepdims=True)
            weighted = dot(weights.astype(BF16), take(v_ref, 0, r + 1))
            energy = energy + finish(r, weighted, total)
    else:

        def one_row(r, energy):
            q = take(q_ref, r)

            def look(j, top):
                scores = dot_nt(q, take(k_ref, j))
                scores = jnp.where((j < r) | mask, scores, -1e30)
                scores_ref[j] = scores
                return jnp.maximum(top, jnp.max(scores, axis=1, keepdims=True))

            top = lax.fori_loop(0, r + 1, look, jnp.full((rows, 1), -1e30, F32))

            def add(j, state):
                weighted, total = state
                weights = jnp.exp2((scores_ref[j] - top) * power)
                total = total + jnp.sum(weights, axis=1, keepdims=True)
                return weighted + dot(weights.astype(BF16), take(v_ref, j)), total

            weighted, total = lax.fori_loop(
                0, r + 1, add, (jnp.zeros((rows, dim), F32), jnp.zeros((rows, 1), F32))
            )
            return energy + finish(r, weighted, total)

        energy = lax.fori_loop(0, steps, one_row, jnp.zeros((8, dim), F32))
    energy_ref[0] = energy


def teacher_call(x, heads):
    blocks, _, chunk, dim = x.shape
    rows = 2 * chunk if blocks % 2 == 0 else chunk
    steps = blocks * chunk // rows
    held = (steps, rows, rows) if steps > 8 else (1, 8, 128)
    return pl.pallas_call(
        functools.partial(teacher_kernel, 1.0 / math.sqrt(dim), rows),
        grid=(heads,),
        in_specs=[
            pl.BlockSpec((blocks, 1, chunk, dim), lambda h: (0, h, 0, 0)),
            pl.BlockSpec((blocks, 1, chunk, dim), lambda h: (0, heads, 0, 0)),
            pl.BlockSpec((blocks, 1, chunk, dim), lambda h: (0, heads + 1, 0, 0)),
        ],
        out_specs=[
            pl.BlockSpec((blocks, 1, chunk, dim), lambda h: (0, h, 0, 0)),
            pl.BlockSpec((1, 8, dim), lambda h: (h, 0, 0)),
        ],
        out_shape=[
            jax.ShapeDtypeStruct((blocks, heads, chunk, dim), F32),
            jax.ShapeDtypeStruct((heads, 8, dim), F32),
        ],
        scratch_shapes=[pltpu.VMEM(held, F32)],
        compiler_params=pltpu.CompilerParams(vmem_limit_bytes=VMEM_LIMIT),
        cost_estimate=pl.CostEstimate(
            flops=2 * heads * (blocks * chunk) ** 2 * dim,
            bytes_accessed=8 * heads * blocks * chunk * dim,
            transcendentals=heads * (blocks * chunk) ** 2 // 2,
        ),
    )(x, x, x)


def student_kernel(
    heads,
    x_ref,
    teacher_ref,
    mq_ref,
    mk_ref,
    grad_ref,
    top_ref,
    wq_ref,
    wk_ref,
    state_ref,
    local_ref,
    slope_ref,
    back_ref,
    sum_q_ref,
    sum_k_ref,
):
    blocks, _, chunk, dim = x_ref.shape
    features = mq_ref.shape[1]
    both = 2 * features

    for h in range(heads):
        rows = pl.ds(h * both, both)
        for source, target in ((mq_ref, wq_ref), (mk_ref, wk_ref)):
            high, low = halves(source[h])
            target[rows, :] = below(beside(high, low), beside(-high, -low))
    state_ref[...] = jnp.zeros_like(state_ref)
    sum_q_ref[...] = jnp.zeros_like(sum_q_ref)
    sum_k_ref[...] = jnp.zeros_like(sum_k_ref)
    mask = causal(chunk, chunk, 0)
    ones = jnp.ones((chunk, dim), BF16)

    def forward(r, carry):
        k, v = x_ref[r, heads], x_ref[r, heads + 1]
        wide = beside(v, ones)
        wide = below(wide, wide)
        twice = beside(v, v)
        phi_k, slope_k = feature_and_slope(dot_nt(wk_ref[...], beside(k, k)))
        slope_ref[r] = slope_k
        k_high, k_low = halves(phi_k)
        for h in range(heads):
            rows = pl.ds(h * both, both)
            at = slice(h * both, (h + 1) * both)
            q = x_ref[r, h]
            qq = beside(q, q)
            weight = wq_ref[rows, :]
            phi, _ = feature_and_slope(dot_nt(qq, weight))
            phi_t, slope_t = feature_and_slope(dot_nt(weight, qq))
            q_high, q_low = halves(phi)
            t_high, t_low = halves(phi_t)
            q_pair = beside(q_high, q_low)
            kh, kl = k_high[at], k_low[at]
            pair = beside(kh, kl)
            inner = dot(q_pair, below(pair, pair))
            inner = jnp.where(mask, inner[:, :chunk] + inner[:, chunk:], 0.0)
            state = state_ref[rows, :]
            s_high, s_low = halves(state)
            out = (
                dot(beside(*halves(inner)), wide)
                + dot(q_pair, below(s_high, s_high))
                + dot(q_high, s_low)
            )
            inverse = 1.0 / out[:, dim:]
            student = out[:, :dim] * inverse
            error = student - teacher_ref[r, h]
            numer = error * inverse
            denom = -jnp.sum(error * student, axis=1, keepdims=True) * inverse
            n_high, n_low = halves(numer)
            d_high, d_low = halves(denom)
            inner_grad = jnp.where(
                mask, dot_nt(beside(n_high, n_low), twice) + denom[:, :chunk], 0.0
            )
            i_high, i_low = halves(inner_grad)
            back_ref[r, rows, :] = dot(
                beside(t_high, t_high), below(beside(n_high, d_high), beside(n_low, d_low))
            )
            grad_t = (
                dot_nt(pair, beside(i_high, i_high))
                + dot_nt(beside(kh, s_high[:, :dim]), beside(i_low, n_high))
                + dot_nt(
                    beside(s_high[:, :dim], s_high[:, dim:] * (1.0 / dim)), beside(n_low, d_high)
                )
                + dot_nt(
                    beside(s_low[:, :dim], s_low[:, dim:] * (1.0 / dim)), beside(n_high, d_high)
                )
            )
            sum_q_ref[rows, :] += dot(beside(*halves(grad_t * slope_t)), below(q, q))
            local_ref[r, rows, :] = dot(beside(t_high, t_low), below(i_high, i_high)) + dot(
                t_high, i_low
            )
        state_ref[...] += dot(beside(k_high, k_low), wide)
        return carry

    lax.fori_loop(0, blocks, forward, 0)
    state_ref[...] = jnp.zeros_like(state_ref)

    def backward(i, carry):
        r = blocks - 1 - i
        k, v = x_ref[r, heads], x_ref[r, heads + 1]
        later = state_ref[...]
        high, low = halves(later[:, :dim])
        grad_t = local_ref[r] + dot_nt(beside(high, low), beside(v, v)) + later[:, dim:]
        sum_k_ref[...] += dot(beside(*halves(grad_t * slope_ref[r])), below(k, k))
        state_ref[...] = later + back_ref[r]
        return carry

    lax.fori_loop(0, blocks, backward, 0)
    for h in range(heads):
        base = h * both
        for i, total in enumerate((sum_q_ref, sum_k_ref)):
            part = total[pl.ds(base, features), :] - total[pl.ds(base + features, features), :]
            grad_ref[pl.ds(base + i * features, features), :] = part
        top = jnp.max(jnp.abs(grad_ref[pl.ds(base, both), :]), axis=0, keepdims=True)
        top_ref[pl.ds(h, 1), :] = top


def student_call(x, teacher, map_query, map_key):
    blocks, _, chunk, dim = x.shape
    heads, features, _ = map_query.shape
    rows = heads * 2 * features
    whole = pl.BlockSpec(memory_space=pltpu.VMEM)
    return pl.pallas_call(
        functools.partial(student_kernel, heads),
        in_specs=[whole] * 4,
        out_specs=[whole] * 2,
        out_shape=[
            jax.ShapeDtypeStruct((rows, dim), F32),
            jax.ShapeDtypeStruct((heads, dim), F32),
        ],
        scratch_shapes=[
            pltpu.VMEM((rows, 2 * dim), BF16),
            pltpu.VMEM((rows, 2 * dim), BF16),
            pltpu.VMEM((rows, 2 * dim), F32),
            pltpu.VMEM((blocks, rows, chunk), F32),
            pltpu.VMEM((blocks, rows, chunk), F32),
            pltpu.VMEM((blocks, rows, 2 * dim), F32),
            pltpu.VMEM((rows, dim), F32),
            pltpu.VMEM((rows, dim), F32),
        ],
        compiler_params=pltpu.CompilerParams(vmem_limit_bytes=VMEM_LIMIT),
        cost_estimate=pl.CostEstimate(
            flops=40 * rows * blocks * chunk * dim,
            bytes_accessed=12 * heads * blocks * chunk * dim,
            transcendentals=3 * rows * blocks * chunk,
        ),
    )(x, teacher, map_query, map_key)


def on_device(queries, key_states, value_vector_states, map_query, map_key):
    places = lax.axis_size("ctx")
    planes = lax.axis_size("head")
    place = lax.axis_index("ctx")
    tokens, query_heads, dim = queries.shape
    key_heads = key_states.shape[1]
    features = map_query.shape[2]
    group = query_heads // key_heads
    heads = min(d for d in range(1, group + 1) if group % d == 0 and d * places >= query_heads)
    padding = heads * places - query_heads
    key_of = np.minimum(np.arange(places) * heads, query_heads - 1) // group

    def padded(a, axis):
        width = [(0, padding if i == axis else 0) for i in range(a.ndim)]
        return jnp.pad(a, width) if padding else a

    by_head = padded(queries, 1).transpose(1, 0, 2).reshape(places, heads, tokens, dim)
    keys = jnp.stack([key_states[:, g] for g in key_of])[:, None]
    values = jnp.stack([value_vector_states[:, g] for g in key_of])[:, None]
    parts = jnp.concatenate([by_head, keys, values], axis=1)
    x = lax.all_to_all(parts, "ctx", 0, 0)

    def own(weights):
        weights = padded(weights, 0).transpose(0, 2, 1)
        return lax.dynamic_slice_in_dim(weights, place * heads, heads, 0)

    teacher, energy = teacher_call(x, heads)
    live = place * heads + jnp.arange(heads) < query_heads
    energy = jnp.sum(jnp.where(live[:, None, None], energy, 0.0)).reshape(1, 1)
    shifted = [
        lax.ppermute(energy, "head", [(i, (i + k) % planes) for i in range(planes)])
        for k in range(1, planes)
    ]
    energy = sum(shifted, energy)[0, 0]
    grads, top = student_call(x, teacher, own(map_query), own(map_key))

    def exponent(v):
        return jnp.clip(jnp.round(jnp.log2(jnp.maximum(v, 1e-30))), -100.0, 126.0)

    power = exponent(jnp.max(top, axis=1))
    energy_power = exponent(energy)
    near_one = energy * jnp.exp2(-energy_power)
    first = near_one.astype(F16)
    second = ((near_one - first.astype(F32)) * 1024.0).astype(F16)
    tail = jnp.concatenate([power.astype(F16), jnp.stack([energy_power.astype(F16), first, second])])
    tail = jnp.pad(jnp.broadcast_to(tail[:, None], (heads + 3, dim)), ((0, TAIL - heads - 3), (0, 0)))
    rows = heads * 2 * features
    scaled = (grads.reshape(heads, -1, dim) * jnp.exp2(-power)[:, None, None]).astype(F16)
    sent = jnp.concatenate([scaled.reshape(rows, dim), tail])
    gathered = lax.all_gather(sent, "ctx").astype(F32)
    tails = gathered[:, rows:, 0]
    power = tails[:, :heads]
    energies = (tails[:, heads + 1] + tails[:, heads + 2] * (1.0 / 1024.0)) * jnp.exp2(tails[:, heads])
    factor = jnp.exp2(power) * (2.0 * query_heads * planes / jnp.sum(energies))
    result = gathered[:, :rows].reshape(places, heads, 2, features, dim)
    result = result * factor[:, :, None, None, None]
    result = result.reshape(places * heads, 2, features, dim)[:query_heads].transpose(1, 0, 3, 2)
    return (result[0], result[1])


def solution(mesh):
    placed = (
        P("ctx", "head", None),
        P("ctx", "head", None),
        P("ctx", "head", None),
        P("head", None, None),
        P("head", None, None),
    )
    return jax.shard_map(
        on_device,
        mesh=mesh,
        in_specs=placed,
        out_specs=(P("head", None, None), P("head", None, None)),
        check_vma=False,
    )
```

```python
import functools
import math

import jax
import jax.numpy as jnp
import numpy as np
from jax import lax
from jax.experimental import pallas as pl
from jax.experimental.pallas import tpu as pltpu
from jax.sharding import PartitionSpec as P

F32 = jnp.float32
BF16 = jnp.bfloat16
F16 = jnp.float16
VMEM_LIMIT = 56 * 1024 * 1024
TAIL = 16


def dot(a, b):
    return lax.dot_general(a, b, (((1,), (0,)), ((), ())), preferred_element_type=F32)


def dot_nt(a, b):
    return lax.dot_general(a, b, (((1,), (1,)), ((), ())), preferred_element_type=F32)


def halves(x):
    high = x.astype(BF16)
    return high, (x - high.astype(F32)).astype(BF16)


def beside(*parts):
    return jnp.concatenate(parts, axis=1)


def below(*parts):
    return jnp.concatenate(parts, axis=0)


def feature(logit):
    return jnp.where(logit > 0, logit + 1.0, jnp.exp(jnp.minimum(logit, 0.0)))


def causal(rows, columns, shift):
    row = lax.broadcasted_iota(jnp.int32, (rows, columns), 0)
    column = lax.broadcasted_iota(jnp.int32, (rows, columns), 1)
    return column <= row + shift


def teacher_kernel(scale, rows, q_ref, k_ref, v_ref, out_ref, energy_ref, scores_ref):
    blocks, _, chunk, dim = q_ref.shape
    per_row = rows // chunk
    steps = blocks // per_row
    power = scale * math.log2(math.e)
    mask = causal(rows, rows, 0)

    def finish(r, weighted, total):
        teacher = weighted / total
        for i in range(per_row):
            out_ref[r * per_row + i, 0] = teacher[i * chunk : (i + 1) * chunk]
        return jnp.sum((teacher * teacher).reshape(rows // 8, 8, dim), axis=0)

    def take(ref, r, count=1):
        return ref[pl.ds(r * per_row, count * per_row), 0].reshape(count * rows, dim)

    if steps <= 8:
        energy = jnp.zeros((8, dim), F32)
        for r in range(steps):
            q = take(q_ref, r)
            keys = take(k_ref, 0, r + 1)
            scores = dot_nt(q, keys)
            last = jnp.where(mask, scores[:, r * rows :], -1e30)
            scores = beside(scores[:, : r * rows], last) if r else last
            top = jnp.max(scores, axis=1, keepdims=True)
            weights = jnp.exp2((scores - top) * power)
            total = jnp.sum(weights, axis=1, keepdims=True)
            weighted = dot(weights.astype(BF16), take(v_ref, 0, r + 1))
            energy = energy + finish(r, weighted, total)
    else:

        def one_row(r, energy):
            q = take(q_ref, r)

            def look(j, top):
                scores = dot_nt(q, take(k_ref, j))
                scores = jnp.where((j < r) | mask, scores, -1e30)
                scores_ref[j] = scores
                return jnp.maximum(top, jnp.max(scores, axis=1, keepdims=True))

            top = lax.fori_loop(0, r + 1, look, jnp.full((rows, 1), -1e30, F32))

            def add(j, state):
                weighted, total = state
                weights = jnp.exp2((scores_ref[j] - top) * power)
                total = total + jnp.sum(weights, axis=1, keepdims=True)
                return weighted + dot(weights.astype(BF16), take(v_ref, j)), total

            weighted, total = lax.fori_loop(
                0, r + 1, add, (jnp.zeros((rows, dim), F32), jnp.zeros((rows, 1), F32))
            )
            return energy + finish(r, weighted, total)

        energy = lax.fori_loop(0, steps, one_row, jnp.zeros((8, dim), F32))
    energy_ref[0] = energy


def teacher_call(x, heads):
    blocks, _, chunk, dim = x.shape
    rows = 2 * chunk if blocks % 2 == 0 else chunk
    steps = blocks * chunk // rows
    held = (steps, rows, rows) if steps > 8 else (1, 8, 128)
    return pl.pallas_call(
        functools.partial(teacher_kernel, 1.0 / math.sqrt(dim), rows),
        grid=(heads,),
        in_specs=[
            pl.BlockSpec((blocks, 1, chunk, dim), lambda h: (0, h, 0, 0)),
            pl.BlockSpec((blocks, 1, chunk, dim), lambda h: (0, heads, 0, 0)),
            pl.BlockSpec((blocks, 1, chunk, dim), lambda h: (0, heads + 1, 0, 0)),
        ],
        out_specs=[
            pl.BlockSpec((blocks, 1, chunk, dim), lambda h: (0, h, 0, 0)),
            pl.BlockSpec((1, 8, dim), lambda h: (h, 0, 0)),
        ],
        out_shape=[
            jax.ShapeDtypeStruct((blocks, heads, chunk, dim), F32),
            jax.ShapeDtypeStruct((heads, 8, dim), F32),
        ],
        scratch_shapes=[pltpu.VMEM(held, F32)],
        compiler_params=pltpu.CompilerParams(vmem_limit_bytes=VMEM_LIMIT),
        cost_estimate=pl.CostEstimate(
            flops=2 * heads * (blocks * chunk) ** 2 * dim,
            bytes_accessed=8 * heads * blocks * chunk * dim,
            transcendentals=heads * (blocks * chunk) ** 2 // 2,
        ),
    )(x, x, x)


def student_kernel(
    heads,
    x_ref,
    teacher_ref,
    mq_ref,
    mk_ref,
    grad_ref,
    top_ref,
    wq_ref,
    wk_ref,
    q_ref,
    t_ref,
    k_ref,
    before_ref,
    norm_ref,
    state_ref,
    local_ref,
    back_ref,
    sum_q_ref,
    sum_k_ref,
):
    blocks, _, chunk, dim = x_ref.shape
    features = mq_ref.shape[1]
    both = 2 * features
    at = [slice(h * both, (h + 1) * both) for h in range(heads)]
    per = 2 if blocks % 2 == 0 else 1

    for h in range(heads):
        for source, target in ((mq_ref, wq_ref), (mk_ref, wk_ref)):
            high, low = halves(source[h])
            target[at[h], :] = below(beside(high, low), beside(-high, -low))
    state_ref[...] = jnp.zeros_like(state_ref)
    sum_q_ref[...] = jnp.zeros_like(sum_q_ref)
    sum_k_ref[...] = jnp.zeros_like(sum_k_ref)
    mask = causal(chunk, chunk, 0)
    ones = jnp.ones((chunk, dim), BF16)

    def query_features(i, carry):
        for h in range(heads):
            for j in range(per):
                r = i * per + j
                q = x_ref[r, h]
                high, low = halves(feature(dot_nt(beside(q, q), wq_ref[at[h], :])))
                q_ref[r, at[h], :] = beside(high, low)
                t_ref[r, at[h], :] = beside(high.T, low.T)
        return carry

    def key_features(r, carry):
        k, v = x_ref[r, heads], x_ref[r, heads + 1]
        wide = beside(v, ones)
        pair = beside(*halves(feature(dot_nt(wk_ref[...], beside(k, k)))))
        k_ref[r] = pair
        state = state_ref[...]
        before_ref[r] = beside(*halves(state))
        norm_ref[r] = state[:, dim:]
        state_ref[...] = state + dot(pair, below(wide, wide))
        return carry

    lax.fori_loop(0, blocks // per, query_features, 0)
    lax.fori_loop(0, blocks, key_features, 0)

    def forward(i, carry):
        chunks = [i * per + j for j in range(per)]
        pairs = [(r, h) for r in chunks for h in range(heads)]

        def stacked(parts):
            return [below(*parts[j * heads : (j + 1) * heads]) for j in range(per)]

        def split(parts):
            return [part[s] for part in parts for s in at]

        def weigh(r, h):
            k = k_ref[r, at[h], :]
            both_ways = dot(q_ref[r, at[h], :], below(k, k))
            return jnp.where(mask, both_ways[:, :chunk] + both_ways[:, chunk:], 0.0)

        def from_before(r, h):
            q = q_ref[r, at[h], :both]
            s = before_ref[r, at[h], :]
            return dot(beside(q, q), below(s[:, : 2 * dim], s[:, 2 * dim :]))

        inner = stacked([weigh(r, h) for r, h in pairs])
        values = [x_ref[r, heads + 1] for r in chunks]
        wide = [beside(v, ones) for v in values]
        state_part = stacked([from_before(r, h) for r, h in pairs])
        out = [
            dot(beside(*halves(a)), below(w, w)) + b for a, w, b in zip(inner, wide, state_part)
        ]
        inverse = [1.0 / o[:, dim:] for o in out]
        student = [o[:, :dim] * n for o, n in zip(out, inverse)]
        error = [s - below(*[teacher_ref[r, h] for h in range(heads)]) for s, r in zip(student, chunks)]
        numer = [e * n for e, n in zip(error, inverse)]
        denom = [
            -jnp.sum(e * s, axis=1, keepdims=True) * n for e, s, n in zip(error, student, inverse)
        ]
        numer_pair = [beside(*halves(n)) for n in numer]
        denom_pair = [beside(*halves(d)) for d in denom]
        spread = [dot_nt(n, beside(v, v)) for n, v in zip(numer_pair, values)]
        mask_all = below(*[mask] * heads)
        inner_grad = [
            jnp.where(mask_all, s + d[:, :chunk], 0.0) for s, d in zip(spread, denom)
        ]
        grad_pair = [beside(*halves(g)) for g in inner_grad]
        numer_pair, denom_pair = split(numer_pair), split(denom_pair)
        grad_pair, denom = split(grad_pair), split(denom)
        for (r, h), n, d, g, d_full in zip(pairs, numer_pair, denom_pair, grad_pair, denom):
            t, k, s = t_ref[r, at[h], :], k_ref[r, at[h], :], before_ref[r, at[h], :]
            t_high, k_high = t[:, :chunk], k[:, :chunk]
            g_high, g_low = g[:, :chunk], g[:, chunk:]
            n_high, n_low = n[:, :dim], n[:, dim:]
            s_high, s_low = s[:, :dim], s[:, 2 * dim : 3 * dim]
            back_ref[r, at[h], :] = dot(
                beside(t_high, t_high), below(beside(n_high, d[:, :dim]), beside(n_low, d[:, dim:]))
            )
            local_ref[r, at[h], :] = dot(beside(t, t_high), below(g_high, g_high, g_low))
            grad_t = dot_nt(
                beside(k, k_high, s_high, s_high, s_low),
                beside(g_high, g_high, g_low, n_high, n_low, n_high),
            )
            grad_t = grad_t + norm_ref[r, at[h], :] * d_full.T
            slope = jnp.minimum(t_high.astype(F32) + t[:, chunk:].astype(F32), 1.0)
            q = x_ref[r, h]
            sum_q_ref[at[h], :] += dot(beside(*halves(grad_t * slope)), below(q, q))
        return carry

    lax.fori_loop(0, blocks // per, forward, 0)
    state_ref[...] = jnp.zeros_like(state_ref)

    def backward(i, carry):
        r = blocks - 1 - i
        k, v = x_ref[r, heads], x_ref[r, heads + 1]
        later = state_ref[...]
        high, low = halves(later[:, :dim])
        grad_t = local_ref[r] + dot_nt(beside(high, low), beside(v, v)) + later[:, dim:]
        pair = k_ref[r]
        slope = jnp.minimum(pair[:, :chunk].astype(F32) + pair[:, chunk:].astype(F32), 1.0)
        sum_k_ref[...] += dot(beside(*halves(grad_t * slope)), below(k, k))
        state_ref[...] = later + back_ref[r]
        return carry

    lax.fori_loop(0, blocks, backward, 0)
    for h in range(heads):
        base = h * both
        for i, total in enumerate((sum_q_ref, sum_k_ref)):
            part = total[pl.ds(base, features), :] - total[pl.ds(base + features, features), :]
            grad_ref[pl.ds(base + i * features, features), :] = part
        top = jnp.max(jnp.abs(grad_ref[pl.ds(base, both), :]), axis=0, keepdims=True)
        top_ref[pl.ds(h, 1), :] = top


def student_call(x, teacher, map_query, map_key):
    blocks, _, chunk, dim = x.shape
    heads, features, _ = map_query.shape
    rows = heads * 2 * features
    whole = pl.BlockSpec(memory_space=pltpu.VMEM)
    return pl.pallas_call(
        functools.partial(student_kernel, heads),
        in_specs=[whole] * 4,
        out_specs=[whole] * 2,
        out_shape=[
            jax.ShapeDtypeStruct((rows, dim), F32),
            jax.ShapeDtypeStruct((heads, dim), F32),
        ],
        scratch_shapes=[
            pltpu.VMEM((rows, 2 * dim), BF16),
            pltpu.VMEM((rows, 2 * dim), BF16),
            pltpu.VMEM((blocks, rows, 2 * chunk), BF16),
            pltpu.VMEM((blocks, rows, 2 * chunk), BF16),
            pltpu.VMEM((blocks, rows, 2 * chunk), BF16),
            pltpu.VMEM((blocks, rows, 4 * dim), BF16),
            pltpu.VMEM((blocks, rows, dim), F32),
            pltpu.VMEM((rows, 2 * dim), F32),
            pltpu.VMEM((blocks, rows, chunk), F32),
            pltpu.VMEM((blocks, rows, 2 * dim), F32),
            pltpu.VMEM((rows, dim), F32),
            pltpu.VMEM((rows, dim), F32),
        ],
        compiler_params=pltpu.CompilerParams(vmem_limit_bytes=VMEM_LIMIT),
        cost_estimate=pl.CostEstimate(
            flops=40 * rows * blocks * chunk * dim,
            bytes_accessed=12 * heads * blocks * chunk * dim,
            transcendentals=3 * rows * blocks * chunk,
        ),
    )(x, teacher, map_query, map_key)


def on_device(queries, key_states, value_vector_states, map_query, map_key):
    places = lax.axis_size("ctx")
    planes = lax.axis_size("head")
    place = lax.axis_index("ctx")
    tokens, query_heads, dim = queries.shape
    key_heads = key_states.shape[1]
    features = map_query.shape[2]
    group = query_heads // key_heads
    heads = min(d for d in range(1, group + 1) if group % d == 0 and d * places >= query_heads)
    padding = heads * places - query_heads
    key_of = np.minimum(np.arange(places) * heads, query_heads - 1) // group

    def padded(a, axis):
        width = [(0, padding if i == axis else 0) for i in range(a.ndim)]
        return jnp.pad(a, width) if padding else a

    by_head = padded(queries, 1).transpose(1, 0, 2).reshape(places, heads, tokens, dim)
    keys = jnp.stack([key_states[:, g] for g in key_of])[:, None]
    values = jnp.stack([value_vector_states[:, g] for g in key_of])[:, None]
    parts = jnp.concatenate([by_head, keys, values], axis=1)
    x = lax.all_to_all(parts, "ctx", 0, 0)

    def own(weights):
        weights = padded(weights, 0).transpose(0, 2, 1)
        return lax.dynamic_slice_in_dim(weights, place * heads, heads, 0)

    teacher, energy = teacher_call(x, heads)
    live = place * heads + jnp.arange(heads) < query_heads
    energy = jnp.sum(jnp.where(live[:, None, None], energy, 0.0)).reshape(1, 1)
    shifted = [
        lax.ppermute(energy, "head", [(i, (i + k) % planes) for i in range(planes)])
        for k in range(1, planes)
    ]
    energy = sum(shifted, energy)[0, 0]
    grads, top = student_call(x, teacher, own(map_query), own(map_key))

    def exponent(v):
        return jnp.clip(jnp.round(jnp.log2(jnp.maximum(v, 1e-30))), -100.0, 126.0)

    power = exponent(jnp.max(top, axis=1))
    energy_power = exponent(energy)
    near_one = energy * jnp.exp2(-energy_power)
    first = near_one.astype(F16)
    second = ((near_one - first.astype(F32)) * 1024.0).astype(F16)
    tail = jnp.concatenate([power.astype(F16), jnp.stack([energy_power.astype(F16), first, second])])
    tail = jnp.pad(jnp.broadcast_to(tail[:, None], (heads + 3, dim)), ((0, TAIL - heads - 3), (0, 0)))
    rows = heads * 2 * features
    scaled = (grads.reshape(heads, -1, dim) * jnp.exp2(-power)[:, None, None]).astype(F16)
    sent = jnp.concatenate([scaled.reshape(rows, dim), tail])
    gathered = lax.all_gather(sent, "ctx").astype(F32)
    tails = gathered[:, rows:, 0]
    power = tails[:, :heads]
    energies = (tails[:, heads + 1] + tails[:, heads + 2] * (1.0 / 1024.0)) * jnp.exp2(tails[:, heads])
    factor = jnp.exp2(power) * (2.0 * query_heads * planes / jnp.sum(energies))
    result = gathered[:, :rows].reshape(places, heads, 2, features, dim)
    result = result * factor[:, :, None, None, None]
    result = result.reshape(places * heads, 2, features, dim)[:query_heads].transpose(1, 0, 3, 2)
    return (result[0], result[1])


def solution(mesh):
    placed = (
        P("ctx", "head", None),
        P("ctx", "head", None),
        P("ctx", "head", None),
        P("head", None, None),
        P("head", None, None),
    )
    return jax.shard_map(
        on_device,
        mesh=mesh,
        in_specs=placed,
        out_specs=(P("head", None, None), P("head", None, None)),
        check_vma=False,
    )
```

```python
import functools
import math

import jax
import jax.numpy as jnp
import numpy as np
from jax import lax
from jax.experimental import pallas as pl
from jax.experimental.pallas import tpu as pltpu
from jax.sharding import PartitionSpec as P

F32 = jnp.float32
BF16 = jnp.bfloat16
F16 = jnp.float16
VMEM_LIMIT = 44 * 1024 * 1024


def dot(a, b):
    return lax.dot_general(a, b, (((1,), (0,)), ((), ())), preferred_element_type=F32)


def dot_nt(a, b):
    return lax.dot_general(a, b, (((1,), (1,)), ((), ())), preferred_element_type=F32)


def halves(x):
    high = x.astype(BF16)
    return high, (x - high.astype(F32)).astype(BF16)


def beside(*parts):
    return jnp.concatenate(parts, axis=1)


def below(*parts):
    return jnp.concatenate(parts, axis=0)


def feature(logit):
    return jnp.where(logit > 0, logit + 1.0, jnp.exp(jnp.minimum(logit, 0.0)))


def power_of(top):
    return jnp.clip(jnp.round(jnp.log2(jnp.maximum(top, 1e-30))), -100.0, 126.0)


def causal(rows, columns, shift):
    row = lax.broadcasted_iota(jnp.int32, (rows, columns), 0)
    column = lax.broadcasted_iota(jnp.int32, (rows, columns), 1)
    return column <= row + shift


def teacher_kernel(heads, rows, scale, x_ref, out_ref, energy_ref, scores_ref):
    blocks, _, chunk, dim = x_ref.shape
    per_row = rows // chunk
    steps = blocks // per_row
    power = scale * math.log2(math.e)
    mask = causal(rows, rows, 0)

    def finish(h, r, weighted, total):
        teacher = weighted / total
        for i in range(per_row):
            out_ref[r * per_row + i, h] = teacher[i * chunk : (i + 1) * chunk]
        return jnp.sum((teacher * teacher).reshape(rows // 8, 8, dim), axis=0)

    def take(h, r, count=1):
        return x_ref[pl.ds(r * per_row, count * per_row), h].reshape(count * rows, dim)

    def one_head(h, energy):
        parts, tops, done = [], [], []
        for r in range(steps):
            scores = dot_nt(take(h, r), take(heads, 0, r + 1))
            last = jnp.where(mask, scores[:, r * rows :], -1e30)
            scores = beside(scores[:, : r * rows], last) if r else last
            parts.append(scores)
            tops.append(jnp.max(scores, axis=1, keepdims=True))
        for r in range(steps):
            weights = jnp.exp2((parts[r] - tops[r]) * power)
            total = jnp.sum(weights, axis=1, keepdims=True)
            done.append((dot(weights.astype(BF16), take(heads + 1, 0, r + 1)), total))
        for r in range(steps):
            energy = energy + finish(h, r, *done[r])
        return energy

    def one_long_head(h, energy):
        def one_row(r, energy):
            q = take(h, r)

            def look(j, top):
                scores = dot_nt(q, take(heads, j))
                scores = jnp.where((j < r) | mask, scores, -1e30)
                scores_ref[j] = scores
                return jnp.maximum(top, jnp.max(scores, axis=1, keepdims=True))

            top = lax.fori_loop(0, r + 1, look, jnp.full((rows, 1), -1e30, F32))

            def add(j, state):
                weighted, total = state
                weights = jnp.exp2((scores_ref[j] - top) * power)
                total = total + jnp.sum(weights, axis=1, keepdims=True)
                return weighted + dot(weights.astype(BF16), take(heads + 1, j)), total

            weighted, total = lax.fori_loop(
                0, r + 1, add, (jnp.zeros((rows, dim), F32), jnp.zeros((rows, 1), F32))
            )
            return energy + finish(h, r, weighted, total)

        return lax.fori_loop(0, steps, one_row, energy)

    body = one_head if steps <= 8 else one_long_head
    energy = lax.fori_loop(0, heads, body, jnp.zeros((8, dim), F32))
    energy = jnp.sum(jnp.sum(energy, axis=0, keepdims=True), axis=1, keepdims=True)
    energy_ref[...] = jnp.broadcast_to(energy, energy_ref.shape)


def teacher_call(x, heads):
    blocks, _, chunk, dim = x.shape
    rows = 2 * chunk if blocks % 2 == 0 else chunk
    steps = blocks * chunk // rows
    held = (steps, rows, rows) if steps > 8 else (1, 8, 128)
    whole = pl.BlockSpec(memory_space=pltpu.VMEM)
    return pl.pallas_call(
        functools.partial(teacher_kernel, heads, rows, 1.0 / math.sqrt(dim)),
        in_specs=[whole],
        out_specs=[whole, whole],
        out_shape=[
            pltpu.VMEM((blocks, heads, chunk, dim), F32),
            jax.ShapeDtypeStruct((8, dim), F32),
        ],
        scratch_shapes=[pltpu.VMEM(held, F32)],
        compiler_params=pltpu.CompilerParams(vmem_limit_bytes=VMEM_LIMIT),
        cost_estimate=pl.CostEstimate(
            flops=2 * heads * (blocks * chunk) ** 2 * dim,
            bytes_accessed=8 * heads * blocks * chunk * dim,
            transcendentals=heads * (blocks * chunk) ** 2 // 2,
        ),
    )(x)


def student_kernel(
    heads,
    x_ref,
    teacher_ref,
    mq_ref,
    mk_ref,
    grad_ref,
    wq_ref,
    wk_ref,
    q_ref,
    t_ref,
    k_ref,
    before_ref,
    norm_ref,
    state_ref,
    bias_ref,
    later_ref,
    sum_q_ref,
    sum_k_ref,
):
    blocks, _, chunk, dim = x_ref.shape
    features = mq_ref.shape[1]
    both = 2 * features
    spare = grad_ref.shape[0] - heads * both
    at = [slice(h * both, (h + 1) * both) for h in range(heads)]
    per = next(p for p in (4, 2, 1) if blocks % p == 0)

    for h in range(heads):
        for source, target in ((mq_ref, wq_ref), (mk_ref, wk_ref)):
            high, low = halves(source[h])
            target[at[h], :] = below(beside(high, low), beside(-high, -low))
    state_ref[...] = jnp.zeros_like(state_ref)
    sum_q_ref[...] = jnp.zeros_like(sum_q_ref)
    sum_k_ref[...] = jnp.zeros_like(sum_k_ref)
    mask = causal(chunk, chunk, 0)
    mask_all = below(*[mask] * heads)
    ones = jnp.ones((chunk, dim), BF16)

    def features_of(i, carry):
        chunks = [i * per + j for j in range(per)]
        keys = [x_ref[r, heads] for r in chunks]
        pairs = [
            beside(*halves(feature(dot_nt(wk_ref[...], beside(k, k))))) for k in keys
        ]
        wide = [beside(x_ref[r, heads + 1], ones) for r in chunks]
        added = [dot(p, below(w, w)) for p, w in zip(pairs, wide)]
        for r in chunks:
            for h in range(heads):
                q = x_ref[r, h]
                high, low = halves(feature(dot_nt(beside(q, q), wq_ref[at[h], :])))
                q_ref[r, at[h], :] = beside(high, low)
                t_ref[r, at[h], :] = beside(high.T, low.T)
        state = state_ref[...]
        for r, p, a in zip(chunks, pairs, added):
            k_ref[r] = p
            before_ref[r] = beside(*halves(state))
            norm_ref[r] = state[:, dim:]
            state = state + a
        state_ref[...] = state
        return carry

    lax.fori_loop(0, blocks // per, features_of, 0)
    bias_ref[...] = jnp.zeros_like(bias_ref)
    later_ref[...] = jnp.zeros_like(later_ref)

    def gradients(i, carry):
        chunks = [blocks - 1 - i * per - j for j in range(per)]
        pairs = [(r, h) for r in chunks for h in range(heads)]

        def stacked(parts):
            return [below(*parts[j * heads : (j + 1) * heads]) for j in range(per)]

        def split(parts):
            return [part[s] for part in parts for s in at]

        def weigh(r, h):
            k = k_ref[r, at[h], :]
            both_ways = dot(q_ref[r, at[h], :], below(k, k))
            return jnp.where(mask, both_ways[:, :chunk] + both_ways[:, chunk:], 0.0)

        def from_before(r, h):
            q = q_ref[r, at[h], :both]
            s = before_ref[r, at[h], :]
            return dot(beside(q, q), below(s[:, : 2 * dim], s[:, 2 * dim :]))

        inner = stacked([weigh(r, h) for r, h in pairs])
        values = [x_ref[r, heads + 1] for r in chunks]
        wide = [beside(v, ones) for v in values]
        state_part = stacked([from_before(r, h) for r, h in pairs])
        out = [
            dot(beside(*halves(a)), below(w, w)) + b for a, w, b in zip(inner, wide, state_part)
        ]
        inverse = [1.0 / o[:, dim:] for o in out]
        student = [o[:, :dim] * n for o, n in zip(out, inverse)]
        error = [s - below(*[teacher_ref[r, h] for h in range(heads)]) for s, r in zip(student, chunks)]
        numer = [e * n for e, n in zip(error, inverse)]
        denom = [
            -jnp.sum(e * s, axis=1, keepdims=True) * n for e, s, n in zip(error, student, inverse)
        ]
        numer_pair = [beside(*halves(n)) for n in numer]
        spread = [dot_nt(n, beside(v, v)) for n, v in zip(numer_pair, values)]
        inner_grad = [
            jnp.where(mask_all, s + d[:, :chunk], 0.0) for s, d in zip(spread, denom)
        ]
        grad_pair = [beside(*halves(g)) for g in inner_grad]
        numer_pair, grad_pair, denom = split(numer_pair), split(grad_pair), split(denom)
        query_side, from_later, later_bias = [], [], []
        for (r, h), n, g, d_full in zip(pairs, numer_pair, grad_pair, denom):
            t, k, s = t_ref[r, at[h], :], k_ref[r, at[h], :], before_ref[r, at[h], :]
            t_high, k_high = t[:, :chunk], k[:, :chunk]
            g_high, g_low = g[:, :chunk], g[:, chunk:]
            n_high, n_low = n[:, :dim], n[:, dim:]
            s_high, s_low = s[:, :dim], s[:, 2 * dim : 3 * dim]
            first = beside(n_high, g_high)
            from_later.append(dot(beside(t, t_high), below(first, first, beside(n_low, g_low))))
            grad_t = dot_nt(
                beside(k, k_high, s_high, s_high, s_low),
                beside(g_high, g_high, g_low, n_high, n_low, n_high),
            )
            d_row = d_full.T
            phi = t_high.astype(F32) + t[:, chunk:].astype(F32)
            later_bias.append(jnp.sum(phi * d_row, axis=1, keepdims=True))
            grad_t = grad_t + norm_ref[r, at[h], :] * d_row
            query_side.append(beside(*halves(grad_t * jnp.minimum(phi, 1.0))))
        for h in range(heads):
            left = beside(*[query_side[j * heads + h] for j in range(per)])
            right = below(*[x_ref[r, h] for r in chunks for _ in range(2)])
            sum_q_ref[at[h], :] += dot(left, right)
        later = later_ref[...]
        bias = bias_ref[...]
        key_side = []
        for j, (r, v) in enumerate(zip(chunks, values)):
            own = below(*from_later[j * heads : (j + 1) * heads])
            grad_t = own[:, dim:] + dot_nt(beside(*halves(later)), beside(v, v)) + bias
            pair = k_ref[r]
            slope = jnp.minimum(pair[:, :chunk].astype(F32) + pair[:, chunk:].astype(F32), 1.0)
            key_side.append(beside(*halves(grad_t * slope)))
            later = later + own[:, :dim]
            bias = bias + below(*later_bias[j * heads : (j + 1) * heads])
        sum_k_ref[...] += dot(
            beside(*key_side), below(*[x_ref[r, heads] for r in chunks for _ in range(2)])
        )
        later_ref[...] = later
        bias_ref[...] = jnp.broadcast_to(bias, bias_ref.shape)
        return carry

    lax.fori_loop(0, blocks // per, gradients, 0)
    grad_ref[pl.ds(heads * both, spare), :] = jnp.zeros((spare, dim), F32)
    for h in range(heads):
        base = h * both
        parts = [
            total[pl.ds(base, features), :] - total[pl.ds(base + features, features), :]
            for total in (sum_q_ref, sum_k_ref)
        ]
        grads = below(*parts)
        top = jnp.max(jnp.abs(grads), axis=0, keepdims=True)
        top = jnp.max(top, axis=1, keepdims=True)
        power = power_of(top)
        grad_ref[at[h], :] = grads * jnp.exp2(-power)
        grad_ref[pl.ds(heads * both + h, 1), :] = jnp.broadcast_to(power, (1, dim))


def student_call(x, teacher, map_query, map_key):
    blocks, _, chunk, dim = x.shape
    heads, features, _ = map_query.shape
    rows = heads * 2 * features
    whole = pl.BlockSpec(memory_space=pltpu.VMEM)
    return pl.pallas_call(
        functools.partial(student_kernel, heads),
        in_specs=[whole] * 4,
        out_specs=whole,
        out_shape=jax.ShapeDtypeStruct((rows + (heads + 7) // 8 * 8, dim), F32),
        scratch_shapes=[
            pltpu.VMEM((rows, 2 * dim), BF16),
            pltpu.VMEM((rows, 2 * dim), BF16),
            pltpu.VMEM((blocks, rows, 2 * chunk), BF16),
            pltpu.VMEM((blocks, rows, 2 * chunk), BF16),
            pltpu.VMEM((blocks, rows, 2 * chunk), BF16),
            pltpu.VMEM((blocks, rows, 4 * dim), BF16),
            pltpu.VMEM((blocks, rows, dim), F32),
            pltpu.VMEM((rows, 2 * dim), F32),
            pltpu.VMEM((rows, chunk), F32),
            pltpu.VMEM((rows, dim), F32),
            pltpu.VMEM((rows, dim), F32),
            pltpu.VMEM((rows, dim), F32),
        ],
        compiler_params=pltpu.CompilerParams(vmem_limit_bytes=VMEM_LIMIT),
        cost_estimate=pl.CostEstimate(
            flops=40 * rows * blocks * chunk * dim,
            bytes_accessed=12 * heads * blocks * chunk * dim,
            transcendentals=3 * rows * blocks * chunk,
        ),
    )(x, teacher, map_query, map_key)


def on_device(queries, key_states, value_vector_states, map_query, map_key):
    places = lax.axis_size("ctx")
    planes = lax.axis_size("head")
    place = lax.axis_index("ctx")
    tokens, query_heads, dim = queries.shape
    key_heads = key_states.shape[1]
    features = map_query.shape[2]
    group = query_heads // key_heads
    heads = min(d for d in range(1, group + 1) if group % d == 0 and d * places >= query_heads)
    padding = heads * places - query_heads
    key_of = np.minimum(np.arange(places) * heads, query_heads - 1) // group

    def padded(a, axis):
        width = [(0, padding if i == axis else 0) for i in range(a.ndim)]
        return jnp.pad(a, width) if padding else a

    by_head = padded(queries, 1).transpose(1, 0, 2).reshape(places, heads, tokens, dim)
    flat = [a.reshape(tokens, key_heads * dim) for a in (key_states, value_vector_states)]
    keyed = [jnp.stack([a[:, g * dim : (g + 1) * dim] for a in flat]) for g in key_of]
    parts = jnp.concatenate([by_head, jnp.stack(keyed)], axis=1)
    x = lax.all_to_all(parts, "ctx", 0, 0)
    x = pltpu.with_memory_space_constraint(x, pltpu.VMEM)

    def own(weights):
        weights = padded(weights, 0).transpose(0, 2, 1)
        return lax.dynamic_slice_in_dim(weights, place * heads, heads, 0)

    teacher, energy = teacher_call(x, heads)
    energy = jnp.where(place * heads < query_heads, energy, 0.0)
    shifted = [
        lax.ppermute(energy, "head", [(i, (i + k) % planes) for i in range(planes)])
        for k in range(1, planes)
    ]
    teacher = pltpu.with_memory_space_constraint(teacher, pltpu.VMEM)
    grads = student_call(x, teacher, own(map_query), own(map_key))
    energy = sum(shifted, energy)
    power = power_of(energy)
    near_one = energy * jnp.exp2(-power)
    first = lax.reduce_precision(near_one, 5, 10)
    row = lax.broadcasted_iota(jnp.int32, energy.shape, 0)
    tail = jnp.where(row == 0, power, jnp.where(row == 1, first, (near_one - first) * 1024.0))
    gathered = lax.all_gather(jnp.concatenate([grads, tail]).astype(F16), "ctx")
    rows = heads * 2 * features
    power = gathered[:, rows : rows + heads].astype(F32)
    tail = gathered[:, -8:-5].astype(F32)
    energy = jnp.sum((tail[:, 1] + tail[:, 2] * (1.0 / 1024.0)) * jnp.exp2(tail[:, 0]), axis=0)
    factor = (jnp.exp2(power) * (2.0 * query_heads * planes / energy))[:, :, None]

    def unpacked(i):
        part = gathered[:, :rows].reshape(places, heads, 2, features, dim)[:, :, i]
        part = (part.astype(F32) * factor).reshape(places * heads, features, dim)
        return part[:query_heads].transpose(0, 2, 1)

    return (unpacked(0), unpacked(1))


def solution(mesh):
    placed = (
        P("ctx", "head", None),
        P("ctx", "head", None),
        P("ctx", "head", None),
        P("head", None, None),
        P("head", None, None),
    )
    return jax.shard_map(
        on_device,
        mesh=mesh,
        in_specs=placed,
        out_specs=(P("head", None, None), P("head", None, None)),
        check_vma=False,
    )
```

```python
import functools
import math

import jax
import jax.numpy as jnp
from jax import lax
from jax.experimental import pallas as pl
from jax.experimental.pallas import tpu as pltpu
from jax.sharding import PartitionSpec as P

F32 = jnp.float32
BF16 = jnp.bfloat16
F16 = jnp.float16
VMEM_LIMIT = 44 * 1024 * 1024


def dot(a, b):
    return lax.dot_general(a, b, (((1,), (0,)), ((), ())), preferred_element_type=F32)


def dot_nt(a, b):
    return lax.dot_general(a, b, (((1,), (1,)), ((), ())), preferred_element_type=F32)


def halves(x):
    high = x.astype(BF16)
    return high, (x - high.astype(F32)).astype(BF16)


def beside(*parts):
    return jnp.concatenate(parts, axis=1)


def below(*parts):
    return jnp.concatenate(parts, axis=0)


def feature(logit):
    return jnp.where(logit > 0, logit + 1.0, jnp.exp(jnp.minimum(logit, 0.0)))


def power_of(top):
    return jnp.clip(jnp.round(jnp.log2(jnp.maximum(top, 1e-30))), -100.0, 126.0)


def causal(rows, columns, shift):
    row = lax.broadcasted_iota(jnp.int32, (rows, columns), 0)
    column = lax.broadcasted_iota(jnp.int32, (rows, columns), 1)
    return column <= row + shift


def teacher_kernel(shape, rows, scale, source_of, place_ref, *refs):
    places, cores, heads, with_keys = shape
    chips = places // cores
    pieces, refs = refs[:chips], refs[chips:]
    if with_keys:
        keys, refs = refs[:cores], refs[cores:]
        x_ref, kv_ref, out_ref, energy_ref, scores_ref = refs
    else:
        kv_ref, before_ref, x_ref, out_ref, energy_ref, scores_ref = refs
    blocks, _, chunk, dim = x_ref.shape
    per_row = rows // chunk
    steps = blocks // per_row
    power = scale * math.log2(math.e)
    mask = causal(rows, rows, 0)
    place = place_ref[0]
    core = place % cores
    for j, piece in enumerate(pieces):
        base = source_of(place // cores, j) * cores
        for i in range(cores):
            block = base + (core if i == 0 else 1 - core)
            x_ref[block] = piece[i]
            if with_keys:
                kv_ref[block] = keys[i][j]

    def finish(h, r, weighted, total):
        teacher = weighted / total
        for i in range(per_row):
            out_ref[r * per_row + i, h] = teacher[i * chunk : (i + 1) * chunk]
        return jnp.sum((teacher * teacher).reshape(rows // 8, 8, dim), axis=0)

    def take(h, r):
        return x_ref[pl.ds(r * per_row, per_row), h].reshape(rows, dim)

    def keyed(i, r, count=1):
        return kv_ref[pl.ds(r * per_row, count * per_row), i].reshape(count * rows, dim)

    def one_head(h, energy):
        parts, tops, done = [], [], []
        for r in range(steps):
            scores = dot_nt(take(h, r), keyed(0, 0, r + 1))
            last = jnp.where(mask, scores[:, r * rows :], -1e30)
            scores = beside(scores[:, : r * rows], last) if r else last
            parts.append(scores)
            tops.append(jnp.max(scores, axis=1, keepdims=True))
        for r in range(steps):
            weights = jnp.exp2((parts[r] - tops[r]) * power)
            total = jnp.sum(weights, axis=1, keepdims=True)
            done.append((dot(weights.astype(BF16), keyed(1, 0, r + 1)), total))
        for r in range(steps):
            energy = energy + finish(h, r, *done[r])
        return energy

    def one_long_head(h, energy):
        def one_row(r, energy):
            q = take(h, r)

            def look(j, top):
                scores = dot_nt(q, keyed(0, j))
                scores = jnp.where((j < r) | mask, scores, -1e30)
                scores_ref[j] = scores
                return jnp.maximum(top, jnp.max(scores, axis=1, keepdims=True))

            top = lax.fori_loop(0, r + 1, look, jnp.full((rows, 1), -1e30, F32))

            def add(j, state):
                weighted, total = state
                weights = jnp.exp2((scores_ref[j] - top) * power)
                total = total + jnp.sum(weights, axis=1, keepdims=True)
                return weighted + dot(weights.astype(BF16), keyed(1, j)), total

            weighted, total = lax.fori_loop(
                0, r + 1, add, (jnp.zeros((rows, dim), F32), jnp.zeros((rows, 1), F32))
            )
            return energy + finish(h, r, weighted, total)

        return lax.fori_loop(0, steps, one_row, energy)

    body = one_head if steps <= 8 else one_long_head
    energy = lax.fori_loop(0, heads, body, jnp.zeros((8, dim), F32))
    energy = jnp.sum(jnp.sum(energy, axis=0, keepdims=True), axis=1, keepdims=True)
    energy = jnp.broadcast_to(energy, energy_ref.shape)
    energy_ref[...] = energy if with_keys else energy + before_ref[...]


def in_vmem(a):
    return pltpu.with_memory_space_constraint(a, pltpu.VMEM)


def teacher_call(place, pieces, kv, keys, before, places, source_of):
    cores, heads, chunk, dim = pieces[0].shape
    with_keys = kv is None
    rows = 2 * chunk if places % 2 == 0 else chunk
    steps = places * chunk // rows
    held = (steps, rows, rows) if steps > 8 else (1, 8, 128)
    whole = pl.BlockSpec(memory_space=pltpu.VMEM)
    operands = [in_vmem(p) for p in pieces + (keys if with_keys else [kv])]
    operands += [] if with_keys else [before]
    return pl.pallas_call(
        functools.partial(
            teacher_kernel,
            (places, cores, heads, with_keys),
            rows,
            1.0 / math.sqrt(dim),
            source_of,
        ),
        in_specs=[pl.BlockSpec(memory_space=pltpu.SMEM)] + [whole] * len(operands),
        out_specs=[whole] * (3 + with_keys),
        out_shape=[pltpu.VMEM((places, heads, chunk, dim), BF16)]
        + [pltpu.VMEM((places, 2, chunk, dim), BF16)] * with_keys
        + [
            pltpu.VMEM((places, heads, chunk, dim), F32),
            jax.ShapeDtypeStruct((8, dim), F32),
        ],
        scratch_shapes=[pltpu.VMEM(held, F32)],
        compiler_params=pltpu.CompilerParams(vmem_limit_bytes=VMEM_LIMIT),
        cost_estimate=pl.CostEstimate(
            flops=10 * heads * (places * chunk) ** 2 * dim,
            bytes_accessed=8 * heads * places * chunk * dim,
            transcendentals=heads * (places * chunk) ** 2 // 2,
        ),
    )(place, *operands)


def student_kernel(
    start,
    heads,
    x_ref,
    kv_ref,
    teacher_ref,
    mq_ref,
    mk_ref,
    grad_ref,
    wq_ref,
    wk_ref,
    q_ref,
    t_ref,
    k_ref,
    before_ref,
    norm_ref,
    state_ref,
    bias_ref,
    later_ref,
    sum_q_ref,
    sum_k_ref,
):
    blocks, _, chunk, dim = x_ref.shape
    features = mq_ref.shape[1]
    both = 2 * features
    spare = grad_ref.shape[0] - heads * both
    at = [slice(h * both, (h + 1) * both) for h in range(heads)]
    per = next(p for p in (8, 4, 2, 1) if blocks % p == 0 and (p * heads <= 16 or p == 1))

    for h in range(heads):
        for source, target in ((mq_ref, wq_ref), (mk_ref, wk_ref)):
            high, low = halves(source[start + h])
            target[at[h], :] = below(beside(high, low), beside(-high, -low))
    state_ref[...] = jnp.zeros_like(state_ref)
    sum_q_ref[...] = jnp.zeros_like(sum_q_ref)
    sum_k_ref[...] = jnp.zeros_like(sum_k_ref)
    mask = causal(chunk, chunk, 0)
    mask_all = below(*[mask] * heads)
    ones = jnp.ones((chunk, dim), BF16)

    def features_of(i, carry):
        chunks = [i * per + j for j in range(per)]
        keys = [kv_ref[r, 0] for r in chunks]
        pairs = [
            beside(*halves(feature(dot_nt(wk_ref[...], beside(k, k))))) for k in keys
        ]
        wide = [beside(kv_ref[r, 1], ones) for r in chunks]
        added = [dot(p, below(w, w)) for p, w in zip(pairs, wide)]
        for r in chunks:
            for h in range(heads):
                q = x_ref[r, h]
                high, low = halves(feature(dot_nt(beside(q, q), wq_ref[at[h], :])))
                q_ref[r, at[h], :] = beside(high, low)
                t_ref[r, at[h], :] = beside(high.T, low.T)
        state = state_ref[...]
        for r, p, a in zip(chunks, pairs, added):
            k_ref[r] = p
            before_ref[r] = beside(*halves(state))
            norm_ref[r] = state[:, dim:]
            state = state + a
        state_ref[...] = state
        return carry

    lax.fori_loop(0, blocks // per, features_of, 0)
    bias_ref[...] = jnp.zeros_like(bias_ref)
    later_ref[...] = jnp.zeros_like(later_ref)

    def gradients(i, carry):
        chunks = [blocks - 1 - i * per - j for j in range(per)]
        pairs = [(r, h) for r in chunks for h in range(heads)]

        def stacked(parts):
            return [below(*parts[j * heads : (j + 1) * heads]) for j in range(per)]

        def split(parts):
            return [part[s] for part in parts for s in at]

        def weigh(r, h):
            k = k_ref[r, at[h], :]
            both_ways = dot(q_ref[r, at[h], :], below(k, k))
            return jnp.where(mask, both_ways[:, :chunk] + both_ways[:, chunk:], 0.0)

        def from_before(r, h):
            q = q_ref[r, at[h], :both]
            s = before_ref[r, at[h], :]
            return dot(beside(q, q), below(s[:, : 2 * dim], s[:, 2 * dim :]))

        inner = stacked([weigh(r, h) for r, h in pairs])
        values = [kv_ref[r, 1] for r in chunks]
        wide = [beside(v, ones) for v in values]
        state_part = stacked([from_before(r, h) for r, h in pairs])
        out = [
            dot(beside(*halves(a)), below(w, w)) + b for a, w, b in zip(inner, wide, state_part)
        ]
        inverse = [1.0 / o[:, dim:] for o in out]
        student = [o[:, :dim] * n for o, n in zip(out, inverse)]
        error = [s - below(*[teacher_ref[r, h] for h in range(heads)]) for s, r in zip(student, chunks)]
        numer = [e * n for e, n in zip(error, inverse)]
        denom = [
            -jnp.sum(e * s, axis=1, keepdims=True) * n for e, s, n in zip(error, student, inverse)
        ]
        numer_pair = [beside(*halves(n)) for n in numer]
        spread = [dot_nt(n, beside(v, v)) for n, v in zip(numer_pair, values)]
        inner_grad = [
            jnp.where(mask_all, s + d[:, :chunk], 0.0) for s, d in zip(spread, denom)
        ]
        grad_pair = [beside(*halves(g)) for g in inner_grad]
        numer_pair, grad_pair, denom = split(numer_pair), split(grad_pair), split(denom)
        query_side, from_later, later_bias = [], [], []
        for (r, h), n, g, d_full in zip(pairs, numer_pair, grad_pair, denom):
            t, k, s = t_ref[r, at[h], :], k_ref[r, at[h], :], before_ref[r, at[h], :]
            t_high, k_high = t[:, :chunk], k[:, :chunk]
            g_high, g_low = g[:, :chunk], g[:, chunk:]
            n_high, n_low = n[:, :dim], n[:, dim:]
            s_high, s_low = s[:, :dim], s[:, 2 * dim : 3 * dim]
            first = beside(n_high, g_high)
            from_later.append(dot(beside(t, t_high), below(first, first, beside(n_low, g_low))))
            grad_t = dot_nt(
                beside(k, k_high, s_high, s_high, s_low),
                beside(g_high, g_high, g_low, n_high, n_low, n_high),
            )
            d_row = d_full.T
            phi = t_high.astype(F32) + t[:, chunk:].astype(F32)
            later_bias.append(jnp.sum(phi * d_row, axis=1, keepdims=True))
            grad_t = grad_t + norm_ref[r, at[h], :] * d_row
            query_side.append(beside(*halves(grad_t * jnp.minimum(phi, 1.0))))
        for h in range(heads):
            left = beside(*[query_side[j * heads + h] for j in range(per)])
            right = below(*[x_ref[r, h] for r in chunks for _ in range(2)])
            sum_q_ref[at[h], :] += dot(left, right)
        later = later_ref[...]
        bias = bias_ref[...]
        key_side = []
        for j, (r, v) in enumerate(zip(chunks, values)):
            own = below(*from_later[j * heads : (j + 1) * heads])
            grad_t = own[:, dim:] + dot_nt(beside(*halves(later)), beside(v, v)) + bias
            pair = k_ref[r]
            slope = jnp.minimum(pair[:, :chunk].astype(F32) + pair[:, chunk:].astype(F32), 1.0)
            key_side.append(beside(*halves(grad_t * slope)))
            later = later + own[:, :dim]
            bias = bias + below(*later_bias[j * heads : (j + 1) * heads])
        sum_k_ref[...] += dot(
            beside(*key_side), below(*[kv_ref[r, 0] for r in chunks for _ in range(2)])
        )
        later_ref[...] = later
        bias_ref[...] = jnp.broadcast_to(bias, bias_ref.shape)
        return carry

    lax.fori_loop(0, blocks // per, gradients, 0)
    grad_ref[pl.ds(heads * both, spare), :] = jnp.zeros((spare, dim), F32)
    for h in range(heads):
        base = h * both
        parts = [
            total[pl.ds(base, features), :] - total[pl.ds(base + features, features), :]
            for total in (sum_q_ref, sum_k_ref)
        ]
        grads = below(*parts)
        top = jnp.max(jnp.abs(grads), axis=0, keepdims=True)
        top = jnp.max(top, axis=1, keepdims=True)
        power = power_of(top)
        grad_ref[at[h], :] = grads * jnp.exp2(-power)
        grad_ref[pl.ds(heads * both + h, 1), :] = jnp.broadcast_to(power, (1, dim))


def student_call(start, x, kv, teacher, map_query, map_key):
    blocks, heads, chunk, dim = x.shape
    features = map_query.shape[1]
    rows = heads * 2 * features
    whole = pl.BlockSpec(memory_space=pltpu.VMEM)
    return pl.pallas_call(
        functools.partial(student_kernel, start, heads),
        in_specs=[whole] * 5,
        out_specs=whole,
        out_shape=jax.ShapeDtypeStruct((rows + (heads + 7) // 8 * 8, dim), F32),
        scratch_shapes=[
            pltpu.VMEM((rows, 2 * dim), BF16),
            pltpu.VMEM((rows, 2 * dim), BF16),
            pltpu.VMEM((blocks, rows, 2 * chunk), BF16),
            pltpu.VMEM((blocks, rows, 2 * chunk), BF16),
            pltpu.VMEM((blocks, rows, 2 * chunk), BF16),
            pltpu.VMEM((blocks, rows, 4 * dim), BF16),
            pltpu.VMEM((blocks, rows, dim), F32),
            pltpu.VMEM((rows, 2 * dim), F32),
            pltpu.VMEM((rows, chunk), F32),
            pltpu.VMEM((rows, dim), F32),
            pltpu.VMEM((rows, dim), F32),
            pltpu.VMEM((rows, dim), F32),
        ],
        compiler_params=pltpu.CompilerParams(vmem_limit_bytes=VMEM_LIMIT),
        cost_estimate=pl.CostEstimate(
            flops=200 * rows * blocks * chunk * dim,
            bytes_accessed=12 * heads * blocks * chunk * dim,
            transcendentals=3 * rows * blocks * chunk,
        ),
    )(in_vmem(x), in_vmem(kv), in_vmem(teacher), map_query, map_key)


def exchange(queries, key_states, value_vector_states, heads, parts):
    places = lax.axis_size("ctx")
    cores = 2 if places % 2 == 0 else 1
    chips = places // cores
    place = lax.axis_index("ctx")
    core, chip = place % cores, place // cores
    tokens, query_heads, dim = queries.shape
    key_heads = key_states.shape[1]
    padding = heads * places - query_heads
    mirrored = chips & (chips - 1) == 0

    def target_of(at, j):
        return at ^ j if mirrored else (at + j) % chips

    def source_of(at, j):
        return at ^ j if mirrored else (at + chips - j) % chips

    def send(a, j):
        return lax.ppermute(
            a, "ctx", [(i, target_of(i // cores, j) * cores + i % cores) for i in range(places)]
        )

    def swap(a):
        return lax.ppermute(a, "ctx", [(i, i ^ 1) for i in range(places)])

    def pick(a, i, axis=0):
        return lax.dynamic_index_in_dim(a, i, axis, False)

    by_head = jnp.pad(queries, ((0, 0), (0, padding), (0, 0))) if padding else queries
    by_head = by_head.transpose(1, 0, 2).reshape(chips, cores, heads, tokens, dim)
    flat = [a.reshape(tokens, key_heads * dim) for a in (key_states, value_vector_states)]
    kv = jnp.stack(
        [jnp.stack([a[:, g * dim : (g + 1) * dim] for a in flat]) for g in range(key_heads)]
    )
    def group_of(at):
        first = jnp.minimum((at * cores + core) * heads, query_heads - 1)
        return first // (query_heads // key_heads)

    mine = [pick(by_head, core, 1)]
    if cores == 2:
        mine.append(swap(pick(by_head, 1 - core, 1)))
    own_keys = [pick(kv, group_of(target_of(chip, j))) for j in range(chips)]
    own_keys = [own_keys[0]] + [send(a, j) for j, a in enumerate(own_keys) if j]
    keys = [jnp.stack(own_keys)]
    arrived = []
    for start, stop in parts:
        pieces = []
        for j in range(chips):
            target = target_of(chip, j)
            pieces.append(jnp.stack([pick(q, target)[start:stop] for q in mine]))
        if arrived and chips > 1:
            pieces = lax.optimization_barrier((*pieces, arrived[-1][1]))[:chips]
        arrived.append([pieces[0]] + [send(a, j) for j, a in enumerate(pieces) if j])
        if cores == 2 and len(keys) == 1:
            ready = lax.optimization_barrier((keys[0], arrived[0][chips > 1]))[0]
            keys.append(swap(ready))
    return arrived, keys, source_of


def on_device(queries, key_states, value_vector_states, map_query, map_key):
    places = lax.axis_size("ctx")
    planes = lax.axis_size("head")
    place = lax.axis_index("ctx")
    tokens, query_heads, dim = queries.shape
    key_heads = key_states.shape[1]
    features = map_query.shape[2]
    group = query_heads // key_heads
    heads = min(d for d in range(1, group + 1) if group % d == 0 and d * places >= query_heads)
    padding = heads * places - query_heads
    half = heads // 2
    parts = [(0, half), (half, heads)] if half else [(0, heads)]
    arrived, keys, source_of = exchange(queries, key_states, value_vector_states, heads, parts)

    def own(weights):
        weights = weights.transpose(0, 2, 1)
        weights = jnp.pad(weights, ((0, padding), (0, 0), (0, 0))) if padding else weights
        return lax.dynamic_slice_in_dim(weights, place * heads, heads, 0)

    own_query, own_key = own(map_query), own(map_key)
    position = place.astype(jnp.int32).reshape(1)
    kv, energy, grads, powers = None, None, [], []
    for (start, stop), pieces in zip(parts, arrived):
        x, *found = teacher_call(position, pieces, kv, keys, energy, places, source_of)
        if kv is None:
            kv = found.pop(0)
        teacher, energy = found
        rows = (stop - start) * 2 * features
        result = student_call(start, x, kv, teacher, own_query, own_key)
        if stop < heads:
            energy, result = lax.optimization_barrier((energy, result))
        grads.append(result[:rows])
        powers.append(result[rows:])
    energy = jnp.where(place * heads < query_heads, energy, 0.0)
    shifted = [
        lax.ppermute(energy, "head", [(i, (i + k) % planes) for i in range(planes)])
        for k in range(1, planes)
    ]
    energy = sum(shifted, energy)
    power = power_of(energy)
    near_one = energy * jnp.exp2(-power)
    first = lax.reduce_precision(near_one, 5, 10)
    row = lax.broadcasted_iota(jnp.int32, energy.shape, 0)
    tail = jnp.where(row == 0, power, jnp.where(row == 1, first, (near_one - first) * 1024.0))
    sent = jnp.concatenate(grads + powers + [tail]).astype(F16)
    used = sent.shape[0]
    gathered = lax.all_gather(jnp.pad(sent, ((0, -used % 16), (0, 0))), "ctx")
    rows = heads * 2 * features
    power, at = [], rows
    for (start, stop), p in zip(parts, powers):
        power.append(gathered[:, at : at + stop - start])
        at += p.shape[0]
    power = jnp.concatenate(power, axis=1).astype(F32)
    tail = gathered[:, at : at + 3].astype(F32)
    energy = jnp.sum((tail[:, 1] + tail[:, 2] * (1.0 / 1024.0)) * jnp.exp2(tail[:, 0]), axis=0)
    factor = (jnp.exp2(power) * (2.0 * query_heads * planes / energy))[:, :, None]

    def unpacked(i):
        part = gathered[:, :rows].reshape(places, heads, 2, features, dim)[:, :, i]
        part = (part.astype(F32) * factor).reshape(places * heads, features, dim)
        return part[:query_heads].transpose(0, 2, 1)

    return (unpacked(0), unpacked(1))


def solution(mesh):
    placed = (
        P("ctx", "head", None),
        P("ctx", "head", None),
        P("ctx", "head", None),
        P("head", None, None),
        P("head", None, None),
    )
    return jax.shard_map(
        on_device,
        mesh=mesh,
        in_specs=placed,
        out_specs=(P("head", None, None), P("head", None, None)),
        check_vma=False,
    )
```

```python
import functools
import math

import jax
import jax.numpy as jnp
from jax import lax
from jax.experimental import pallas as pl
from jax.experimental.pallas import tpu as pltpu
from jax.sharding import PartitionSpec as P

F32 = jnp.float32
BF16 = jnp.bfloat16
F16 = jnp.float16
VMEM_LIMIT = 44 * 1024 * 1024


def dot(a, b):
    return lax.dot_general(a, b, (((1,), (0,)), ((), ())), preferred_element_type=F32)


def dot_nt(a, b):
    return lax.dot_general(a, b, (((1,), (1,)), ((), ())), preferred_element_type=F32)


def halves(x):
    high = x.astype(BF16)
    return high, (x - high.astype(F32)).astype(BF16)


def beside(*parts):
    return jnp.concatenate(parts, axis=1)


def below(*parts):
    return jnp.concatenate(parts, axis=0)


def feature(logit):
    return jnp.where(logit > 0, logit + 1.0, jnp.exp(jnp.minimum(logit, 0.0)))


def power_of(top):
    return jnp.clip(jnp.round(jnp.log2(jnp.maximum(top, 1e-30))), -100.0, 126.0)


def causal(rows, columns, shift):
    row = lax.broadcasted_iota(jnp.int32, (rows, columns), 0)
    column = lax.broadcasted_iota(jnp.int32, (rows, columns), 1)
    return column <= row + shift


def teacher_kernel(shape, rows, scale, source_of, place_ref, *refs):
    places, cores, heads, with_keys = shape
    chips = places // cores
    pieces, refs = refs[:chips], refs[chips:]
    if with_keys:
        keys, refs = refs[:cores], refs[cores:]
        x_ref, kv_ref, out_ref, energy_ref, scores_ref = refs
    else:
        kv_ref, before_ref, x_ref, out_ref, energy_ref, scores_ref = refs
    blocks, _, chunk, dim = x_ref.shape
    per_row = rows // chunk
    steps = blocks // per_row
    power = scale * math.log2(math.e)
    mask = causal(rows, rows, 0)
    place = place_ref[0]
    core = place % cores
    for j, piece in enumerate(pieces):
        base = source_of(place // cores, j) * cores
        for i in range(cores):
            block = base + (core if i == 0 else 1 - core)
            x_ref[block] = piece[i * heads : (i + 1) * heads]
            if with_keys:
                kv_ref[block] = keys[i][j]

    def finish(h, r, weighted, total):
        teacher = weighted / total
        for i in range(per_row):
            out_ref[r * per_row + i, h] = teacher[i * chunk : (i + 1) * chunk]
        return jnp.sum((teacher * teacher).reshape(rows // 8, 8, dim), axis=0)

    def take(h, r):
        return x_ref[pl.ds(r * per_row, per_row), h].reshape(rows, dim)

    def keyed(i, r, count=1):
        return kv_ref[pl.ds(r * per_row, count * per_row), i].reshape(count * rows, dim)

    def one_head(h, energy):
        parts, tops, done = [], [], []
        for r in range(steps):
            scores = dot_nt(take(h, r), keyed(0, 0, r + 1))
            last = jnp.where(mask, scores[:, r * rows :], -1e30)
            scores = beside(scores[:, : r * rows], last) if r else last
            parts.append(scores)
            tops.append(jnp.max(scores, axis=1, keepdims=True))
        for r in range(steps):
            weights = jnp.exp2((parts[r] - tops[r]) * power)
            total = jnp.sum(weights, axis=1, keepdims=True)
            done.append((dot(weights.astype(BF16), keyed(1, 0, r + 1)), total))
        for r in range(steps):
            energy = energy + finish(h, r, *done[r])
        return energy

    def one_long_head(h, energy):
        def one_row(r, energy):
            q = take(h, r)

            def look(j, top):
                scores = dot_nt(q, keyed(0, j))
                scores = jnp.where((j < r) | mask, scores, -1e30)
                scores_ref[j] = scores
                return jnp.maximum(top, jnp.max(scores, axis=1, keepdims=True))

            top = lax.fori_loop(0, r + 1, look, jnp.full((rows, 1), -1e30, F32))

            def add(j, state):
                weighted, total = state
                weights = jnp.exp2((scores_ref[j] - top) * power)
                total = total + jnp.sum(weights, axis=1, keepdims=True)
                return weighted + dot(weights.astype(BF16), keyed(1, j)), total

            weighted, total = lax.fori_loop(
                0, r + 1, add, (jnp.zeros((rows, dim), F32), jnp.zeros((rows, 1), F32))
            )
            return energy + finish(h, r, weighted, total)

        return lax.fori_loop(0, steps, one_row, energy)

    energy = jnp.zeros((8, dim), F32)
    if steps <= 8:
        for h in range(heads):
            energy = one_head(h, energy)
    else:
        energy = lax.fori_loop(0, heads, one_long_head, energy)
    energy = jnp.sum(jnp.sum(energy, axis=0, keepdims=True), axis=1, keepdims=True)
    energy = jnp.broadcast_to(energy, energy_ref.shape)
    energy_ref[...] = energy if with_keys else energy + before_ref[...]


def in_vmem(a):
    return pltpu.with_memory_space_constraint(a, pltpu.VMEM)


def teacher_call(place, pieces, kv, keys, before, places, source_of):
    _, chunk, dim = pieces[0].shape
    cores = len(keys)
    with_keys = kv is None
    heads = pieces[0].shape[0] // cores
    rows = 2 * chunk if places % 2 == 0 else chunk
    steps = places * chunk // rows
    held = (steps, rows, rows) if steps > 8 else (1, 8, 128)
    whole = pl.BlockSpec(memory_space=pltpu.VMEM)
    operands = [in_vmem(p) for p in pieces + (keys if with_keys else [kv])]
    operands += [] if with_keys else [before]
    return pl.pallas_call(
        functools.partial(
            teacher_kernel,
            (places, cores, heads, with_keys),
            rows,
            1.0 / math.sqrt(dim),
            source_of,
        ),
        in_specs=[pl.BlockSpec(memory_space=pltpu.SMEM)] + [whole] * len(operands),
        out_specs=[whole] * (3 + with_keys),
        out_shape=[pltpu.VMEM((places, heads, chunk, dim), BF16)]
        + [pltpu.VMEM((places, 2, chunk, dim), BF16)] * with_keys
        + [
            pltpu.VMEM((places, heads, chunk, dim), F32),
            jax.ShapeDtypeStruct((8, dim), F32),
        ],
        scratch_shapes=[pltpu.VMEM(held, F32)],
        compiler_params=pltpu.CompilerParams(vmem_limit_bytes=VMEM_LIMIT),
        cost_estimate=pl.CostEstimate(
            flops=10 * heads * (places * chunk) ** 2 * dim,
            bytes_accessed=8 * heads * places * chunk * dim,
            transcendentals=heads * (places * chunk) ** 2 // 2,
        ),
    )(place, *operands)


def student_kernel(
    start,
    heads,
    x_ref,
    kv_ref,
    teacher_ref,
    mq_ref,
    mk_ref,
    grad_ref,
    wq_ref,
    wk_ref,
    q_ref,
    t_ref,
    k_ref,
    before_ref,
    norm_ref,
    state_ref,
    bias_ref,
    later_ref,
    sum_q_ref,
    sum_k_ref,
):
    blocks, _, chunk, dim = x_ref.shape
    features = mq_ref.shape[1]
    both = 2 * features
    spare = grad_ref.shape[0] - heads * both
    at = [slice(h * both, (h + 1) * both) for h in range(heads)]
    per = next(p for p in (8, 4, 2, 1) if blocks % p == 0 and (p * heads <= 16 or p == 1))

    for h in range(heads):
        for source, target in ((mq_ref, wq_ref), (mk_ref, wk_ref)):
            high, low = halves(source[start + h])
            target[at[h], :] = below(beside(high, low), beside(-high, -low))
    state_ref[...] = jnp.zeros_like(state_ref)
    sum_q_ref[...] = jnp.zeros_like(sum_q_ref)
    sum_k_ref[...] = jnp.zeros_like(sum_k_ref)
    mask = causal(chunk, chunk, 0)
    mask_all = below(*[mask] * heads)
    ones = jnp.ones((chunk, dim), BF16)

    def features_of(i, carry):
        chunks = [i * per + j for j in range(per)]
        keys = [kv_ref[r, 0] for r in chunks]
        pairs = [
            beside(*halves(feature(dot_nt(wk_ref[...], beside(k, k))))) for k in keys
        ]
        wide = [beside(kv_ref[r, 1], ones) for r in chunks]
        added = [dot(p, below(w, w)) for p, w in zip(pairs, wide)]
        for r in chunks:
            for h in range(heads):
                q = x_ref[r, h]
                high, low = halves(feature(dot_nt(beside(q, q), wq_ref[at[h], :])))
                q_ref[r, at[h], :] = beside(high, low)
                t_ref[r, at[h], :] = beside(high.T, low.T)
        state = state_ref[...]
        for r, p, a in zip(chunks, pairs, added):
            k_ref[r] = p
            before_ref[r] = beside(*halves(state))
            norm_ref[r] = state[:, dim:]
            state = state + a
        state_ref[...] = state
        return carry

    lax.fori_loop(0, blocks // per, features_of, 0)
    bias_ref[...] = jnp.zeros_like(bias_ref)
    later_ref[...] = jnp.zeros_like(later_ref)

    def gradients(i, carry):
        chunks = [blocks - 1 - i * per - j for j in range(per)]
        pairs = [(r, h) for r in chunks for h in range(heads)]

        def stacked(parts):
            return [below(*parts[j * heads : (j + 1) * heads]) for j in range(per)]

        def split(parts):
            return [part[s] for part in parts for s in at]

        def weigh(r, h):
            k = k_ref[r, at[h], :]
            both_ways = dot(q_ref[r, at[h], :], below(k, k))
            return jnp.where(mask, both_ways[:, :chunk] + both_ways[:, chunk:], 0.0)

        def from_before(r, h):
            q = q_ref[r, at[h], :both]
            s = before_ref[r, at[h], :]
            return dot(beside(q, q), below(s[:, : 2 * dim], s[:, 2 * dim :]))

        inner = stacked([weigh(r, h) for r, h in pairs])
        values = [kv_ref[r, 1] for r in chunks]
        wide = [beside(v, ones) for v in values]
        state_part = stacked([from_before(r, h) for r, h in pairs])
        out = [
            dot(beside(*halves(a)), below(w, w)) + b for a, w, b in zip(inner, wide, state_part)
        ]
        inverse = [1.0 / o[:, dim:] for o in out]
        student = [o[:, :dim] * n for o, n in zip(out, inverse)]
        error = [s - below(*[teacher_ref[r, h] for h in range(heads)]) for s, r in zip(student, chunks)]
        numer = [e * n for e, n in zip(error, inverse)]
        denom = [
            -jnp.sum(e * s, axis=1, keepdims=True) * n for e, s, n in zip(error, student, inverse)
        ]
        numer_pair = [beside(*halves(n)) for n in numer]
        spread = [dot_nt(n, beside(v, v)) for n, v in zip(numer_pair, values)]
        inner_grad = [
            jnp.where(mask_all, s + d[:, :chunk], 0.0) for s, d in zip(spread, denom)
        ]
        grad_pair = [beside(*halves(g)) for g in inner_grad]
        numer_pair, grad_pair, denom = split(numer_pair), split(grad_pair), split(denom)
        query_side, from_later, later_bias = [], [], []
        for (r, h), n, g, d_full in zip(pairs, numer_pair, grad_pair, denom):
            t, k, s = t_ref[r, at[h], :], k_ref[r, at[h], :], before_ref[r, at[h], :]
            t_high, k_high = t[:, :chunk], k[:, :chunk]
            g_high, g_low = g[:, :chunk], g[:, chunk:]
            n_high, n_low = n[:, :dim], n[:, dim:]
            s_high, s_low = s[:, :dim], s[:, 2 * dim : 3 * dim]
            first = beside(n_high, g_high)
            from_later.append(dot(beside(t, t_high), below(first, first, beside(n_low, g_low))))
            grad_t = dot_nt(
                beside(k, k_high, s_high, s_high, s_low),
                beside(g_high, g_high, g_low, n_high, n_low, n_high),
            )
            d_row = d_full.T
            phi = t_high.astype(F32) + t[:, chunk:].astype(F32)
            later_bias.append(jnp.sum(phi * d_row, axis=1, keepdims=True))
            grad_t = grad_t + norm_ref[r, at[h], :] * d_row
            query_side.append(beside(*halves(grad_t * jnp.minimum(phi, 1.0))))
        for h in range(heads):
            left = beside(*[query_side[j * heads + h] for j in range(per)])
            right = below(*[x_ref[r, h] for r in chunks for _ in range(2)])
            sum_q_ref[at[h], :] += dot(left, right)
        later = later_ref[...]
        bias = bias_ref[...]
        key_side = []
        for j, (r, v) in enumerate(zip(chunks, values)):
            own = below(*from_later[j * heads : (j + 1) * heads])
            grad_t = own[:, dim:] + dot_nt(beside(*halves(later)), beside(v, v)) + bias
            pair = k_ref[r]
            slope = jnp.minimum(pair[:, :chunk].astype(F32) + pair[:, chunk:].astype(F32), 1.0)
            key_side.append(beside(*halves(grad_t * slope)))
            later = later + own[:, :dim]
            bias = bias + below(*later_bias[j * heads : (j + 1) * heads])
        sum_k_ref[...] += dot(
            beside(*key_side), below(*[kv_ref[r, 0] for r in chunks for _ in range(2)])
        )
        later_ref[...] = later
        bias_ref[...] = jnp.broadcast_to(bias, bias_ref.shape)
        return carry

    lax.fori_loop(0, blocks // per, gradients, 0)
    grad_ref[pl.ds(heads * both, spare), :] = jnp.zeros((spare, dim), F32)
    for h in range(heads):
        base = h * both
        parts = [
            total[pl.ds(base, features), :] - total[pl.ds(base + features, features), :]
            for total in (sum_q_ref, sum_k_ref)
        ]
        grads = below(*parts)
        top = jnp.max(jnp.abs(grads), axis=0, keepdims=True)
        top = jnp.max(top, axis=1, keepdims=True)
        power = power_of(top)
        grad_ref[at[h], :] = grads * jnp.exp2(-power)
        grad_ref[pl.ds(heads * both + h, 1), :] = jnp.broadcast_to(power, (1, dim))


def student_call(start, x, kv, teacher, map_query, map_key):
    blocks, heads, chunk, dim = x.shape
    features = map_query.shape[1]
    rows = heads * 2 * features
    whole = pl.BlockSpec(memory_space=pltpu.VMEM)
    return pl.pallas_call(
        functools.partial(student_kernel, start, heads),
        in_specs=[whole] * 5,
        out_specs=whole,
        out_shape=jax.ShapeDtypeStruct((rows + (heads + 7) // 8 * 8, dim), F32),
        scratch_shapes=[
            pltpu.VMEM((rows, 2 * dim), BF16),
            pltpu.VMEM((rows, 2 * dim), BF16),
            pltpu.VMEM((blocks, rows, 2 * chunk), BF16),
            pltpu.VMEM((blocks, rows, 2 * chunk), BF16),
            pltpu.VMEM((blocks, rows, 2 * chunk), BF16),
            pltpu.VMEM((blocks, rows, 4 * dim), BF16),
            pltpu.VMEM((blocks, rows, dim), F32),
            pltpu.VMEM((rows, 2 * dim), F32),
            pltpu.VMEM((rows, chunk), F32),
            pltpu.VMEM((rows, dim), F32),
            pltpu.VMEM((rows, dim), F32),
            pltpu.VMEM((rows, dim), F32),
        ],
        compiler_params=pltpu.CompilerParams(vmem_limit_bytes=VMEM_LIMIT),
        cost_estimate=pl.CostEstimate(
            flops=200 * rows * blocks * chunk * dim,
            bytes_accessed=12 * heads * blocks * chunk * dim,
            transcendentals=3 * rows * blocks * chunk,
        ),
    )(in_vmem(x), in_vmem(kv), in_vmem(teacher), map_query, map_key)


def exchange(queries, key_states, value_vector_states, heads, parts):
    places = lax.axis_size("ctx")
    cores = 2 if places % 2 == 0 else 1
    chips = places // cores
    place = lax.axis_index("ctx")
    core, chip = place % cores, place // cores
    tokens, query_heads, dim = queries.shape
    key_heads = key_states.shape[1]
    padding = heads * places - query_heads
    mirrored = chips & (chips - 1) == 0

    def target_of(at, j):
        return at ^ j if mirrored else (at + j) % chips

    def source_of(at, j):
        return at ^ j if mirrored else (at + chips - j) % chips

    def send(a, j):
        return lax.ppermute(
            a, "ctx", [(i, target_of(i // cores, j) * cores + i % cores) for i in range(places)]
        )

    def swap(a):
        return lax.ppermute(a, "ctx", [(i, i ^ 1) for i in range(places)])

    def pick(a, i, axis=0):
        return lax.dynamic_index_in_dim(a, i, axis, False)

    by_head = jnp.pad(queries, ((0, 0), (0, padding), (0, 0))) if padding else queries
    by_head = by_head.transpose(1, 0, 2).reshape(chips, cores, heads, tokens, dim)
    *flat, by_head = lax.optimization_barrier((key_states, value_vector_states, by_head))
    flat = [a.reshape(tokens, key_heads * dim) for a in flat]
    kv = jnp.stack(
        [jnp.stack([a[:, g * dim : (g + 1) * dim] for a in flat]) for g in range(key_heads)]
    )
    def group_of(at):
        first = jnp.minimum((at * cores + core) * heads, query_heads - 1)
        return first // (query_heads // key_heads)

    mine = [pick(by_head, core, 1)]
    if cores == 2:
        mine.append(swap(pick(by_head, 1 - core, 1)))
        kv = lax.optimization_barrier((kv, mine[1]))[0]
    to_send = [pick(kv, group_of(target_of(chip, j))) for j in range(chips)]
    arrived = []
    for start, stop in parts:
        pieces = []
        for j in range(chips):
            piece = [pick(q, target_of(chip, j))[start:stop] for q in mine]
            if j == 1 and not arrived:
                piece.append(to_send[j])
            pieces.append(jnp.concatenate(piece))
        if arrived and chips > 1:
            pieces = lax.optimization_barrier((*pieces, arrived[-1][1]))[:chips]
        arrived.append([pieces[0]] + [send(a, j) for j, a in enumerate(pieces) if j])
    own_keys = [send(a, j) if j > 1 else a for j, a in enumerate(to_send)]
    if chips > 1:
        own_keys[1] = arrived[0][1][-2:]
    keys = [jnp.stack(own_keys)]
    if cores == 2:
        keys.append(swap(keys[0]))
    return arrived, keys, source_of


def on_device(queries, key_states, value_vector_states, map_query, map_key):
    places = lax.axis_size("ctx")
    planes = lax.axis_size("head")
    place = lax.axis_index("ctx")
    tokens, query_heads, dim = queries.shape
    key_heads = key_states.shape[1]
    features = map_query.shape[2]
    group = query_heads // key_heads
    heads = min(d for d in range(1, group + 1) if group % d == 0 and d * places >= query_heads)
    padding = heads * places - query_heads
    half = heads // 2
    parts = [(0, half), (half, heads)] if half else [(0, heads)]
    arrived, keys, source_of = exchange(queries, key_states, value_vector_states, heads, parts)

    def own(weights):
        weights = weights.transpose(0, 2, 1)
        weights = jnp.pad(weights, ((0, padding), (0, 0), (0, 0))) if padding else weights
        return lax.dynamic_slice_in_dim(weights, place * heads, heads, 0)

    own_query, own_key = own(map_query), own(map_key)
    position = place.astype(jnp.int32).reshape(1)
    kv, energy, grads, powers = None, None, [], []
    for (start, stop), pieces in zip(parts, arrived):
        x, *found = teacher_call(position, pieces, kv, keys, energy, places, source_of)
        if kv is None:
            kv = found.pop(0)
        teacher, energy = found
        rows = (stop - start) * 2 * features
        result = student_call(start, x, kv, teacher, own_query, own_key)
        if stop < heads:
            energy, result = lax.optimization_barrier((energy, result))
        grads.append(result[:rows])
        powers.append(result[rows:])
    energy = jnp.where(place * heads < query_heads, energy, 0.0)
    shifted = [
        lax.ppermute(energy, "head", [(i, (i + k) % planes) for i in range(planes)])
        for k in range(1, planes)
    ]
    energy = sum(shifted, energy)
    power = power_of(energy)
    near_one = energy * jnp.exp2(-power)
    first = lax.reduce_precision(near_one, 5, 10)
    row = lax.broadcasted_iota(jnp.int32, energy.shape, 0)
    tail = jnp.where(row == 0, power, jnp.where(row == 1, first, (near_one - first) * 1024.0))
    sent = jnp.concatenate(grads + powers + [tail]).astype(F16)
    used = sent.shape[0]
    gathered = lax.all_gather(jnp.pad(sent, ((0, -used % 16), (0, 0))), "ctx")
    rows = heads * 2 * features
    power, at = [], rows
    for (start, stop), p in zip(parts, powers):
        power.append(gathered[:, at : at + stop - start])
        at += p.shape[0]
    power = jnp.concatenate(power, axis=1).astype(F32)
    tail = gathered[:, at : at + 3].astype(F32)
    energy = jnp.sum((tail[:, 1] + tail[:, 2] * (1.0 / 1024.0)) * jnp.exp2(tail[:, 0]), axis=0)
    factor = (jnp.exp2(power) * (2.0 * query_heads * planes / energy))[:, :, None]

    def unpacked(i):
        part = gathered[:, :rows].reshape(places, heads, 2, features, dim)[:, :, i]
        part = (part.astype(F32) * factor).reshape(places * heads, features, dim)
        return part[:query_heads].transpose(0, 2, 1)

    return (unpacked(0), unpacked(1))


def solution(mesh):
    placed = (
        P("ctx", "head", None),
        P("ctx", "head", None),
        P("ctx", "head", None),
        P("head", None, None),
        P("head", None, None),
    )
    return jax.shard_map(
        on_device,
        mesh=mesh,
        in_specs=placed,
        out_specs=(P("head", None, None), P("head", None, None)),
        check_vma=False,
    )
```

```python
import functools
import math

import jax
import jax.numpy as jnp
from jax import lax
from jax.experimental import pallas as pl
from jax.experimental.pallas import tpu as pltpu
from jax.sharding import PartitionSpec as P

F32 = jnp.float32
BF16 = jnp.bfloat16
F16 = jnp.float16
VMEM_LIMIT = 44 * 1024 * 1024


def dot(a, b):
    return lax.dot_general(a, b, (((1,), (0,)), ((), ())), preferred_element_type=F32)


def dot_nt(a, b):
    return lax.dot_general(a, b, (((1,), (1,)), ((), ())), preferred_element_type=F32)


def halves(x):
    high = x.astype(BF16)
    return high, (x - high.astype(F32)).astype(BF16)


def beside(*parts):
    return jnp.concatenate(parts, axis=1)


def below(*parts):
    return jnp.concatenate(parts, axis=0)


def feature(logit):
    return jnp.where(logit > 0, logit + 1.0, jnp.exp(jnp.minimum(logit, 0.0)))


def power_of(top):
    return jnp.clip(jnp.round(jnp.log2(jnp.maximum(top, 1e-30))), -100.0, 126.0)


def causal(rows, columns, shift):
    row = lax.broadcasted_iota(jnp.int32, (rows, columns), 0)
    column = lax.broadcasted_iota(jnp.int32, (rows, columns), 1)
    return column <= row + shift


def teacher_kernel(shape, rows, scale, source_of, place_ref, *refs):
    places, cores, heads, with_keys = shape
    chips = places // cores
    pieces, refs = refs[:chips], refs[chips:]
    if with_keys:
        keys, refs = refs[:cores], refs[cores:]
        x_ref, kv_ref, out_ref, energy_ref, scores_ref = refs
    else:
        kv_ref, before_ref, x_ref, out_ref, energy_ref, scores_ref = refs
    blocks, _, chunk, dim = x_ref.shape
    per_row = rows // chunk
    steps = blocks // per_row
    power = scale * math.log2(math.e)
    mask = causal(rows, rows, 0)
    place = place_ref[0]
    core = place % cores
    for j, piece in enumerate(pieces):
        base = source_of(place // cores, j) * cores
        for i in range(cores):
            block = base + (core if i == 0 else 1 - core)
            x_ref[block] = piece[i * heads : (i + 1) * heads]
            if with_keys:
                kv_ref[block] = keys[i][j]

    def finish(h, r, weighted, total):
        teacher = weighted / total
        for i in range(per_row):
            out_ref[r * per_row + i, h] = teacher[i * chunk : (i + 1) * chunk]
        return jnp.sum((teacher * teacher).reshape(rows // 8, 8, dim), axis=0)

    def take(h, r):
        return x_ref[pl.ds(r * per_row, per_row), h].reshape(rows, dim)

    def keyed(i, r, count=1):
        return kv_ref[pl.ds(r * per_row, count * per_row), i].reshape(count * rows, dim)

    def one_head(h, energy):
        parts, tops, done = [], [], []
        for r in range(steps):
            scores = dot_nt(take(h, r), keyed(0, 0, r + 1))
            last = jnp.where(mask, scores[:, r * rows :], -1e30)
            scores = beside(scores[:, : r * rows], last) if r else last
            parts.append(scores)
            tops.append(jnp.max(scores, axis=1, keepdims=True))
        for r in range(steps):
            weights = jnp.exp2((parts[r] - tops[r]) * power)
            total = jnp.sum(weights, axis=1, keepdims=True)
            done.append((dot(weights.astype(BF16), keyed(1, 0, r + 1)), total))
        for r in range(steps):
            energy = energy + finish(h, r, *done[r])
        return energy

    def one_long_head(h, energy):
        def one_row(r, energy):
            q = take(h, r)

            def look(j, top):
                scores = dot_nt(q, keyed(0, j))
                scores = jnp.where((j < r) | mask, scores, -1e30)
                scores_ref[j] = scores
                return jnp.maximum(top, jnp.max(scores, axis=1, keepdims=True))

            top = lax.fori_loop(0, r + 1, look, jnp.full((rows, 1), -1e30, F32))

            def add(j, state):
                weighted, total = state
                weights = jnp.exp2((scores_ref[j] - top) * power)
                total = total + jnp.sum(weights, axis=1, keepdims=True)
                return weighted + dot(weights.astype(BF16), keyed(1, j)), total

            weighted, total = lax.fori_loop(
                0, r + 1, add, (jnp.zeros((rows, dim), F32), jnp.zeros((rows, 1), F32))
            )
            return energy + finish(h, r, weighted, total)

        return lax.fori_loop(0, steps, one_row, energy)

    energy = jnp.zeros((8, dim), F32)
    if steps <= 8:
        for h in range(heads):
            energy = one_head(h, energy)
    else:
        energy = lax.fori_loop(0, heads, one_long_head, energy)
    energy = jnp.sum(jnp.sum(energy, axis=0, keepdims=True), axis=1, keepdims=True)
    energy = jnp.broadcast_to(energy, energy_ref.shape)
    energy_ref[...] = energy if with_keys else energy + before_ref[...]


def in_vmem(a):
    return pltpu.with_memory_space_constraint(a, pltpu.VMEM)


def teacher_call(place, pieces, kv, keys, before, places, source_of):
    _, chunk, dim = pieces[0].shape
    cores = len(keys)
    with_keys = kv is None
    heads = pieces[0].shape[0] // cores
    rows = 2 * chunk if places % 2 == 0 else chunk
    steps = places * chunk // rows
    held = (steps, rows, rows) if steps > 8 else (1, 8, 128)
    whole = pl.BlockSpec(memory_space=pltpu.VMEM)
    operands = [in_vmem(p) for p in pieces + (keys if with_keys else [kv])]
    operands += [] if with_keys else [before]
    return pl.pallas_call(
        functools.partial(
            teacher_kernel,
            (places, cores, heads, with_keys),
            rows,
            1.0 / math.sqrt(dim),
            source_of,
        ),
        in_specs=[pl.BlockSpec(memory_space=pltpu.SMEM)] + [whole] * len(operands),
        out_specs=[whole] * (3 + with_keys),
        out_shape=[pltpu.VMEM((places, heads, chunk, dim), BF16)]
        + [pltpu.VMEM((places, 2, chunk, dim), BF16)] * with_keys
        + [
            pltpu.VMEM((places, heads, chunk, dim), F32),
            jax.ShapeDtypeStruct((8, dim), F32),
        ],
        scratch_shapes=[pltpu.VMEM(held, F32)],
        compiler_params=pltpu.CompilerParams(vmem_limit_bytes=VMEM_LIMIT),
        cost_estimate=pl.CostEstimate(
            flops=10 * heads * (places * chunk) ** 2 * dim,
            bytes_accessed=8 * heads * places * chunk * dim,
            transcendentals=heads * (places * chunk) ** 2 // 2,
        ),
    )(place, *operands)


def student_kernel(
    start,
    heads,
    x_ref,
    kv_ref,
    teacher_ref,
    mq_ref,
    mk_ref,
    grad_ref,
    wq_ref,
    wk_ref,
    q_ref,
    t_ref,
    k_ref,
    before_ref,
    norm_ref,
    state_ref,
    bias_ref,
    later_ref,
    sum_q_ref,
    sum_k_ref,
):
    blocks, _, chunk, dim = x_ref.shape
    features = mq_ref.shape[1]
    both = 2 * features
    spare = grad_ref.shape[0] - heads * both
    at = [slice(h * both, (h + 1) * both) for h in range(heads)]
    per = next(p for p in (8, 4, 2, 1) if blocks % p == 0 and (p * heads <= 16 or p == 1))

    for h in range(heads):
        for source, target in ((mq_ref, wq_ref), (mk_ref, wk_ref)):
            high, low = halves(source[start + h])
            target[at[h], :] = below(beside(high, low), beside(-high, -low))
    state_ref[...] = jnp.zeros_like(state_ref)
    sum_q_ref[...] = jnp.zeros_like(sum_q_ref)
    sum_k_ref[...] = jnp.zeros_like(sum_k_ref)
    mask = causal(chunk, chunk, 0)
    mask_all = below(*[mask] * heads)
    ones = jnp.ones((chunk, dim), BF16)

    def features_of(i, carry):
        chunks = [i * per + j for j in range(per)]
        keys = [kv_ref[r, 0] for r in chunks]
        pairs = [
            beside(*halves(feature(dot_nt(wk_ref[...], beside(k, k))))) for k in keys
        ]
        wide = [beside(kv_ref[r, 1], ones) for r in chunks]
        added = [dot(p, below(w, w)) for p, w in zip(pairs, wide)]
        for r in chunks:
            for h in range(heads):
                q = x_ref[r, h]
                high, low = halves(feature(dot_nt(beside(q, q), wq_ref[at[h], :])))
                q_ref[r, at[h], :] = beside(high, low)
                t_ref[r, at[h], :] = beside(high.T, low.T)
        state = state_ref[...]
        for r, p, a in zip(chunks, pairs, added):
            k_ref[r] = p
            before_ref[r] = beside(*halves(state))
            norm_ref[r] = state[:, dim:]
            state = state + a
        state_ref[...] = state
        return carry

    lax.fori_loop(0, blocks // per, features_of, 0)
    bias_ref[...] = jnp.zeros_like(bias_ref)
    later_ref[...] = jnp.zeros_like(later_ref)

    def gradients(i, carry):
        chunks = [blocks - 1 - i * per - j for j in range(per)]
        pairs = [(r, h) for r in chunks for h in range(heads)]

        def stacked(parts):
            return [below(*parts[j * heads : (j + 1) * heads]) for j in range(per)]

        def split(parts):
            return [part[s] for part in parts for s in at]

        def weigh(r, h):
            k = k_ref[r, at[h], :]
            both_ways = dot(q_ref[r, at[h], :], below(k, k))
            return jnp.where(mask, both_ways[:, :chunk] + both_ways[:, chunk:], 0.0)

        def from_before(r, h):
            q = q_ref[r, at[h], :both]
            s = before_ref[r, at[h], :]
            return dot(beside(q, q), below(s[:, : 2 * dim], s[:, 2 * dim :]))

        inner = stacked([weigh(r, h) for r, h in pairs])
        values = [kv_ref[r, 1] for r in chunks]
        wide = [beside(v, ones) for v in values]
        state_part = stacked([from_before(r, h) for r, h in pairs])
        out = [
            dot(beside(*halves(a)), below(w, w)) + b for a, w, b in zip(inner, wide, state_part)
        ]
        inverse = [1.0 / o[:, dim:] for o in out]
        student = [o[:, :dim] * n for o, n in zip(out, inverse)]
        error = [s - below(*[teacher_ref[r, h] for h in range(heads)]) for s, r in zip(student, chunks)]
        numer = [e * n for e, n in zip(error, inverse)]
        denom = [
            -jnp.sum(e * s, axis=1, keepdims=True) * n for e, s, n in zip(error, student, inverse)
        ]
        numer_pair = [beside(*halves(n)) for n in numer]
        spread = [dot_nt(n, beside(v, v)) for n, v in zip(numer_pair, values)]
        inner_grad = [
            jnp.where(mask_all, s + d[:, :chunk], 0.0) for s, d in zip(spread, denom)
        ]
        grad_pair = [beside(*halves(g)) for g in inner_grad]
        numer_pair, grad_pair, denom = split(numer_pair), split(grad_pair), split(denom)
        query_side, from_later, later_bias = [], [], []
        for (r, h), n, g, d_full in zip(pairs, numer_pair, grad_pair, denom):
            t, k, s = t_ref[r, at[h], :], k_ref[r, at[h], :], before_ref[r, at[h], :]
            t_high, k_high = t[:, :chunk], k[:, :chunk]
            g_high, g_low = g[:, :chunk], g[:, chunk:]
            n_high, n_low = n[:, :dim], n[:, dim:]
            s_high, s_low = s[:, :dim], s[:, 2 * dim : 3 * dim]
            first = beside(n_high, g_high)
            from_later.append(dot(beside(t, t_high), below(first, first, beside(n_low, g_low))))
            grad_t = dot_nt(
                beside(k, k_high, s_high, s_high, s_low),
                beside(g_high, g_high, g_low, n_high, n_low, n_high),
            )
            d_row = d_full.T
            phi = t_high.astype(F32) + t[:, chunk:].astype(F32)
            later_bias.append(jnp.sum(phi * d_row, axis=1, keepdims=True))
            grad_t = grad_t + norm_ref[r, at[h], :] * d_row
            query_side.append(beside(*halves(grad_t * jnp.minimum(phi, 1.0))))
        for h in range(heads):
            left = beside(*[query_side[j * heads + h] for j in range(per)])
            right = below(*[x_ref[r, h] for r in chunks for _ in range(2)])
            sum_q_ref[at[h], :] += dot(left, right)
        later = later_ref[...]
        bias = bias_ref[...]
        key_side = []
        for j, (r, v) in enumerate(zip(chunks, values)):
            own = below(*from_later[j * heads : (j + 1) * heads])
            grad_t = own[:, dim:] + dot_nt(beside(*halves(later)), beside(v, v)) + bias
            pair = k_ref[r]
            slope = jnp.minimum(pair[:, :chunk].astype(F32) + pair[:, chunk:].astype(F32), 1.0)
            key_side.append(beside(*halves(grad_t * slope)))
            later = later + own[:, :dim]
            bias = bias + below(*later_bias[j * heads : (j + 1) * heads])
        sum_k_ref[...] += dot(
            beside(*key_side), below(*[kv_ref[r, 0] for r in chunks for _ in range(2)])
        )
        later_ref[...] = later
        bias_ref[...] = jnp.broadcast_to(bias, bias_ref.shape)
        return carry

    lax.fori_loop(0, blocks // per, gradients, 0)
    grad_ref[pl.ds(heads * both, spare), :] = jnp.zeros((spare, dim), F32)
    for h in range(heads):
        parts = []
        for total in (sum_q_ref, sum_k_ref):
            both_signs = total[at[h], :]
            parts.append(both_signs[:features] - both_signs[features:])
        top = jnp.max(jnp.abs(below(*parts)), axis=0, keepdims=True)
        power = power_of(jnp.max(top, axis=1, keepdims=True))
        for i, part in enumerate(parts):
            rows = pl.ds((i * heads + h) * features, features)
            grad_ref[rows, :] = part * jnp.exp2(-power)
        grad_ref[pl.ds(heads * both + h, 1), :] = jnp.broadcast_to(power, (1, dim))


def student_scratch(blocks, rows, chunk, dim):
    return [
        pltpu.VMEM((rows, 2 * dim), BF16),
        pltpu.VMEM((rows, 2 * dim), BF16),
        pltpu.VMEM((blocks, rows, 2 * chunk), BF16),
        pltpu.VMEM((blocks, rows, 2 * chunk), BF16),
        pltpu.VMEM((blocks, rows, 2 * chunk), BF16),
        pltpu.VMEM((blocks, rows, 4 * dim), BF16),
        pltpu.VMEM((blocks, rows, dim), F32),
        pltpu.VMEM((rows, 2 * dim), F32),
        pltpu.VMEM((rows, chunk), F32),
        pltpu.VMEM((rows, dim), F32),
        pltpu.VMEM((rows, dim), F32),
        pltpu.VMEM((rows, dim), F32),
    ]


def student_shape(heads, rows, dim):
    return jax.ShapeDtypeStruct((rows + (heads + 7) // 8 * 8, dim), F32)


def student_call(start, x, kv, teacher, map_query, map_key):
    blocks, heads, chunk, dim = x.shape
    features = map_query.shape[1]
    rows = heads * 2 * features
    whole = pl.BlockSpec(memory_space=pltpu.VMEM)
    return pl.pallas_call(
        functools.partial(student_kernel, start, heads),
        in_specs=[whole] * 5,
        out_specs=whole,
        out_shape=student_shape(heads, rows, dim),
        scratch_shapes=student_scratch(blocks, rows, chunk, dim),
        compiler_params=pltpu.CompilerParams(vmem_limit_bytes=VMEM_LIMIT),
        cost_estimate=pl.CostEstimate(
            flops=200 * rows * blocks * chunk * dim,
            bytes_accessed=12 * heads * blocks * chunk * dim,
            transcendentals=3 * rows * blocks * chunk,
        ),
    )(*[in_vmem(a) for a in (x, kv, teacher, map_query, map_key)])


def partner(at, step, count):
    return at ^ step if count & (count - 1) == 0 else (at + step) % count


def both_kernel(shape, rows, scale, source_of, start, place_ref, *refs):
    places, cores, heads, _ = shape
    count = places // cores + cores
    arrived, (mq_ref, mk_ref), refs = refs[:count], refs[count : count + 2], refs[count + 2 :]
    kv_ref, energy_ref, grad_ref, x_ref, out_ref, scores_ref, *scratch = refs
    teacher_kernel(
        shape, rows, scale, source_of, place_ref, *arrived, x_ref, kv_ref, out_ref, energy_ref, scores_ref
    )
    student_kernel(start, heads, x_ref, kv_ref, out_ref, mq_ref, mk_ref, grad_ref, *scratch)


def both_call(start, place, pieces, keys, map_query, map_key, places, source_of):
    _, chunk, dim = pieces[0].shape
    cores = len(keys)
    heads = pieces[0].shape[0] // cores
    rows = 2 * chunk if places % 2 == 0 else chunk
    steps = places * chunk // rows
    held = (steps, rows, rows) if steps > 8 else (1, 8, 128)
    both = heads * 2 * map_query.shape[1]
    whole = pl.BlockSpec(memory_space=pltpu.VMEM)
    operands = [in_vmem(a) for a in pieces + keys + [map_query, map_key]]
    return pl.pallas_call(
        functools.partial(
            both_kernel,
            (places, cores, heads, True),
            rows,
            1.0 / math.sqrt(dim),
            source_of,
            start,
        ),
        in_specs=[pl.BlockSpec(memory_space=pltpu.SMEM)] + [whole] * len(operands),
        out_specs=[whole] * 3,
        out_shape=[
            pltpu.VMEM((places, 2, chunk, dim), BF16),
            jax.ShapeDtypeStruct((8, dim), F32),
            student_shape(heads, both, dim),
        ],
        scratch_shapes=[
            pltpu.VMEM((places, heads, chunk, dim), BF16),
            pltpu.VMEM((places, heads, chunk, dim), F32),
            pltpu.VMEM(held, F32),
        ]
        + student_scratch(places, both, chunk, dim),
        compiler_params=pltpu.CompilerParams(vmem_limit_bytes=VMEM_LIMIT),
        cost_estimate=pl.CostEstimate(
            flops=200 * both * places * chunk * dim + 10 * heads * (places * chunk) ** 2 * dim,
            bytes_accessed=20 * heads * places * chunk * dim,
            transcendentals=heads * (places * chunk) ** 2 // 2,
        ),
    )(place, *operands)


def exchange(queries, key_states, value_vector_states, heads, parts):
    places = lax.axis_size("ctx")
    cores = 2 if places % 2 == 0 else 1
    chips = places // cores
    place = lax.axis_index("ctx")
    core, chip = place % cores, place // cores
    tokens, query_heads, dim = queries.shape
    key_heads = key_states.shape[1]
    padding = heads * places - query_heads
    mirrored = chips & (chips - 1) == 0

    def target_of(at, j):
        return partner(at, j, chips)

    def source_of(at, j):
        return at ^ j if mirrored else (at + chips - j) % chips

    def send(a, j):
        return lax.ppermute(
            a, "ctx", [(i, target_of(i // cores, j) * cores + i % cores) for i in range(places)]
        )

    def swap(a):
        return lax.ppermute(a, "ctx", [(i, i ^ 1) for i in range(places)])

    def pick(a, i, axis=0):
        return lax.dynamic_index_in_dim(a, i, axis, False)

    by_head = jnp.pad(queries, ((0, 0), (0, padding), (0, 0))) if padding else queries
    by_head = by_head.transpose(1, 0, 2).reshape(chips, cores, heads, tokens, dim)
    *flat, by_head = lax.optimization_barrier((key_states, value_vector_states, by_head))
    flat = [a.reshape(tokens, key_heads * dim) for a in flat]
    kv = jnp.stack(
        [jnp.stack([a[:, g * dim : (g + 1) * dim] for a in flat]) for g in range(key_heads)]
    )
    def group_of(at):
        first = jnp.minimum((at * cores + core) * heads, query_heads - 1)
        return first // (query_heads // key_heads)

    mine = [pick(by_head, core, 1)]
    if cores == 2:
        mine.append(swap(pick(by_head, 1 - core, 1)))
        kv = lax.optimization_barrier((kv, mine[1]))[0]
    to_send = [pick(kv, group_of(target_of(chip, j))) for j in range(chips)]
    arrived = []
    for start, stop in parts:
        pieces = []
        for j in range(chips):
            piece = [pick(q, target_of(chip, j))[start:stop] for q in mine]
            if j == 1 and not arrived:
                piece.append(to_send[j])
            pieces.append(jnp.concatenate(piece))
        if arrived and chips > 1:
            pieces = lax.optimization_barrier((*pieces, arrived[-1][1]))[:chips]
        arrived.append([pieces[0]] + [send(a, j) for j, a in enumerate(pieces) if j])
    own_keys = [send(a, j) if j > 1 else a for j, a in enumerate(to_send)]
    if chips > 1:
        own_keys[1] = arrived[0][1][-2:]
    keys = [jnp.stack(own_keys)]
    if cores == 2:
        keys.append(swap(keys[0]))
    return arrived, keys, source_of


def on_device(queries, key_states, value_vector_states, map_query, map_key):
    places = lax.axis_size("ctx")
    planes = lax.axis_size("head")
    place = lax.axis_index("ctx")
    tokens, query_heads, dim = queries.shape
    key_heads = key_states.shape[1]
    features = map_query.shape[2]
    group = query_heads // key_heads
    heads = min(d for d in range(1, group + 1) if group % d == 0 and d * places >= query_heads)
    padding = heads * places - query_heads
    half = heads // 2
    parts = [(0, half), (half, heads)] if half else [(0, heads)]
    arrived, keys, source_of = exchange(queries, key_states, value_vector_states, heads, parts)

    def own(weights):
        weights = weights.transpose(0, 2, 1)
        weights = jnp.pad(weights, ((0, padding), (0, 0), (0, 0))) if padding else weights
        return lax.dynamic_slice_in_dim(weights, place * heads, heads, 0)

    own_query, own_key = own(map_query), own(map_key)
    position = place.astype(jnp.int32).reshape(1)
    kv, energy, grads, powers = None, None, [], []
    for (start, stop), pieces in zip(parts, arrived):
        if stop < heads:
            kv, energy, result = both_call(
                start, position, pieces, keys, own_query, own_key, places, source_of
            )
        else:
            x, *found = teacher_call(position, pieces, kv, keys, energy, places, source_of)
            if kv is None:
                kv = found.pop(0)
            teacher, energy = found
            result = student_call(start, x, kv, teacher, own_query, own_key)
        rows = (stop - start) * features
        grads.append((result[:rows], result[rows : 2 * rows]))
        powers.append(result[2 * rows :])
    energy = jnp.where(place * heads < query_heads, energy, 0.0)
    shifted = [
        lax.ppermute(energy, "head", [(i, partner(i, k, planes)) for i in range(planes)])
        for k in range(1, planes)
    ]
    energy = sum(shifted, energy)
    power = power_of(energy)
    near_one = energy * jnp.exp2(-power)
    first = lax.reduce_precision(near_one, 5, 10)
    row = lax.broadcasted_iota(jnp.int32, energy.shape, 0)
    tail = jnp.where(row == 0, power, jnp.where(row == 1, first, (near_one - first) * 1024.0))
    grads = [part for side in zip(*grads) for part in side]
    sent = jnp.concatenate(grads + powers + [tail]).astype(F16)
    used = sent.shape[0]
    gathered = lax.all_gather(jnp.pad(sent, ((0, -used % 16), (0, 0))), "ctx")
    rows = heads * 2 * features
    power, at = [], rows
    for (start, stop), p in zip(parts, powers):
        power.append(gathered[:, at : at + stop - start])
        at += p.shape[0]
    power = jnp.concatenate(power, axis=1).astype(F32)
    tail = gathered[:, at : at + 3].astype(F32)
    energy = jnp.sum((tail[:, 1] + tail[:, 2] * (1.0 / 1024.0)) * jnp.exp2(tail[:, 0]), axis=0)
    factor = (jnp.exp2(power) * (2.0 * query_heads * planes / energy))[:, :, None]

    def unpacked(i):
        part = gathered[:, i * rows // 2 : (i + 1) * rows // 2].astype(F32)
        part = part.reshape(places, heads, features, dim) * factor
        part = part.reshape(places * heads, features, dim)
        return part[:query_heads].transpose(0, 2, 1)

    return (unpacked(0), unpacked(1))


def solution(mesh):
    placed = (
        P("ctx", "head", None),
        P("ctx", "head", None),
        P("ctx", "head", None),
        P("head", None, None),
        P("head", None, None),
    )
    return jax.shard_map(
        on_device,
        mesh=mesh,
        in_specs=placed,
        out_specs=(P("head", None, None), P("head", None, None)),
        check_vma=False,
    )
```

```python
import functools
import math

import jax
import jax.numpy as jnp
from jax import lax
from jax.experimental import pallas as pl
from jax.experimental.pallas import tpu as pltpu
from jax.sharding import PartitionSpec as P

F32 = jnp.float32
BF16 = jnp.bfloat16
F16 = jnp.float16
VMEM_LIMIT = 44 * 1024 * 1024


def dot(a, b):
    return lax.dot_general(a, b, (((1,), (0,)), ((), ())), preferred_element_type=F32)


def dot_nt(a, b):
    return lax.dot_general(a, b, (((1,), (1,)), ((), ())), preferred_element_type=F32)


def halves(x):
    high = x.astype(BF16)
    return high, (x - high.astype(F32)).astype(BF16)


def beside(*parts):
    return jnp.concatenate(parts, axis=1)


def below(*parts):
    return jnp.concatenate(parts, axis=0)


def feature(logit):
    return jnp.where(logit > 0, logit + 1.0, jnp.exp(jnp.minimum(logit, 0.0)))


def power_of(top):
    return jnp.clip(jnp.round(jnp.log2(jnp.maximum(top, 1e-30))), -100.0, 126.0)


def causal(rows, columns, shift):
    row = lax.broadcasted_iota(jnp.int32, (rows, columns), 0)
    column = lax.broadcasted_iota(jnp.int32, (rows, columns), 1)
    return column <= row + shift


def teacher_kernel(shape, rows, scale, source_of, place_ref, *refs):
    places, cores, heads, with_keys = shape
    chips = places // cores
    pieces, refs = refs[:chips], refs[chips:]
    if with_keys:
        keys, refs = refs[:cores], refs[cores:]
        x_ref, kv_ref, out_ref, energy_ref, scores_ref = refs
    else:
        kv_ref, before_ref, x_ref, out_ref, energy_ref, scores_ref = refs
    blocks, _, chunk, dim = x_ref.shape
    per_row = rows // chunk
    steps = blocks // per_row
    power = scale * math.log2(math.e)
    mask = causal(rows, rows, 0)
    place = place_ref[0]
    core = place % cores
    for j, piece in enumerate(pieces):
        base = source_of(place // cores, j) * cores
        for i in range(cores):
            block = base + (core if i == 0 else 1 - core)
            x_ref[block] = piece[i * heads : (i + 1) * heads]
            if with_keys:
                kv_ref[block] = keys[i][j]

    def finish(h, r, weighted, total):
        teacher = weighted / total
        for i in range(per_row):
            out_ref[r * per_row + i, h] = teacher[i * chunk : (i + 1) * chunk]
        return jnp.sum((teacher * teacher).reshape(rows // 8, 8, dim), axis=0)

    def take(h, r):
        return x_ref[pl.ds(r * per_row, per_row), h].reshape(rows, dim)

    def keyed(i, r, count=1):
        return kv_ref[pl.ds(r * per_row, count * per_row), i].reshape(count * rows, dim)

    def one_head(h, energy):
        parts, tops, done = [], [], []
        for r in range(steps):
            scores = dot_nt(take(h, r), keyed(0, 0, r + 1))
            last = jnp.where(mask, scores[:, r * rows :], -1e30)
            scores = beside(scores[:, : r * rows], last) if r else last
            parts.append(scores)
            tops.append(jnp.max(scores, axis=1, keepdims=True))
        for r in range(steps):
            weights = jnp.exp2((parts[r] - tops[r]) * power)
            total = jnp.sum(weights, axis=1, keepdims=True)
            done.append((dot(weights.astype(BF16), keyed(1, 0, r + 1)), total))
        for r in range(steps):
            energy = energy + finish(h, r, *done[r])
        return energy

    def one_long_head(h, energy):
        def one_row(r, energy):
            q = take(h, r)

            def look(j, top):
                scores = dot_nt(q, keyed(0, j))
                scores = jnp.where((j < r) | mask, scores, -1e30)
                scores_ref[j] = scores
                return jnp.maximum(top, jnp.max(scores, axis=1, keepdims=True))

            top = lax.fori_loop(0, r + 1, look, jnp.full((rows, 1), -1e30, F32))

            def add(j, state):
                weighted, total = state
                weights = jnp.exp2((scores_ref[j] - top) * power)
                total = total + jnp.sum(weights, axis=1, keepdims=True)
                return weighted + dot(weights.astype(BF16), keyed(1, j)), total

            weighted, total = lax.fori_loop(
                0, r + 1, add, (jnp.zeros((rows, dim), F32), jnp.zeros((rows, 1), F32))
            )
            return energy + finish(h, r, weighted, total)

        return lax.fori_loop(0, steps, one_row, energy)

    energy = jnp.zeros((8, dim), F32)
    if steps <= 8:
        for h in range(heads):
            energy = one_head(h, energy)
    else:
        energy = lax.fori_loop(0, heads, one_long_head, energy)
    energy = jnp.sum(jnp.sum(energy, axis=0, keepdims=True), axis=1, keepdims=True)
    energy = jnp.broadcast_to(energy, energy_ref.shape)
    energy_ref[...] = energy if with_keys else energy + before_ref[...]


def in_vmem(a):
    return pltpu.with_memory_space_constraint(a, pltpu.VMEM)


def teacher_call(place, pieces, kv, keys, before, places, source_of):
    _, chunk, dim = pieces[0].shape
    cores = len(keys)
    with_keys = kv is None
    heads = pieces[0].shape[0] // cores
    rows = 2 * chunk if places % 2 == 0 else chunk
    steps = places * chunk // rows
    held = (steps, rows, rows) if steps > 8 else (1, 8, 128)
    whole = pl.BlockSpec(memory_space=pltpu.VMEM)
    operands = [in_vmem(p) for p in pieces + (keys if with_keys else [kv])]
    operands += [] if with_keys else [before]
    return pl.pallas_call(
        functools.partial(
            teacher_kernel,
            (places, cores, heads, with_keys),
            rows,
            1.0 / math.sqrt(dim),
            source_of,
        ),
        in_specs=[pl.BlockSpec(memory_space=pltpu.SMEM)] + [whole] * len(operands),
        out_specs=[whole] * (3 + with_keys),
        out_shape=[pltpu.VMEM((places, heads, chunk, dim), BF16)]
        + [pltpu.VMEM((places, 2, chunk, dim), BF16)] * with_keys
        + [
            pltpu.VMEM((places, heads, chunk, dim), F32),
            jax.ShapeDtypeStruct((8, dim), F32),
        ],
        scratch_shapes=[pltpu.VMEM(held, F32)],
        compiler_params=pltpu.CompilerParams(vmem_limit_bytes=VMEM_LIMIT),
        cost_estimate=pl.CostEstimate(
            flops=10 * heads * (places * chunk) ** 2 * dim,
            bytes_accessed=8 * heads * places * chunk * dim,
            transcendentals=heads * (places * chunk) ** 2 // 2,
        ),
    )(place, *operands)


def student_kernel(
    start,
    heads,
    x_ref,
    kv_ref,
    teacher_ref,
    mq_ref,
    mk_ref,
    grad_ref,
    wq_ref,
    wk_ref,
    q_ref,
    t_ref,
    k_ref,
    before_ref,
    norm_ref,
    state_ref,
    bias_ref,
    later_ref,
    sum_q_ref,
    sum_k_ref,
):
    blocks, _, chunk, dim = x_ref.shape
    features = mq_ref.shape[1]
    both = 2 * features
    spare = grad_ref.shape[0] - heads * both
    at = [slice(h * both, (h + 1) * both) for h in range(heads)]
    per = next(p for p in (8, 4, 2, 1) if blocks % p == 0 and (p * heads <= 16 or p == 1))

    for h in range(heads):
        for source, target in ((mq_ref, wq_ref), (mk_ref, wk_ref)):
            high, low = halves(source[start + h])
            target[at[h], :] = below(beside(high, low), beside(-high, -low))
    state_ref[...] = jnp.zeros_like(state_ref)
    sum_q_ref[...] = jnp.zeros_like(sum_q_ref)
    sum_k_ref[...] = jnp.zeros_like(sum_k_ref)
    mask = causal(chunk, chunk, 0)
    mask_all = below(*[mask] * heads)
    ones = jnp.ones((chunk, dim), BF16)

    def features_of(i, carry):
        chunks = [i * per + j for j in range(per)]
        keys = [kv_ref[r, 0] for r in chunks]
        pairs = [
            beside(*halves(feature(dot_nt(wk_ref[...], beside(k, k))))) for k in keys
        ]
        wide = [beside(kv_ref[r, 1], ones) for r in chunks]
        added = [dot(p, below(w, w)) for p, w in zip(pairs, wide)]
        for r in chunks:
            for h in range(heads):
                q = x_ref[r, h]
                high, low = halves(feature(dot_nt(beside(q, q), wq_ref[at[h], :])))
                q_ref[r, at[h], :] = beside(high, low)
                t_ref[r, at[h], :] = beside(high.T, low.T)
        state = state_ref[...]
        for r, p, a in zip(chunks, pairs, added):
            k_ref[r] = p
            before_ref[r] = beside(*halves(state))
            norm_ref[r] = state[:, dim:]
            state = state + a
        state_ref[...] = state
        return carry

    lax.fori_loop(0, blocks // per, features_of, 0)
    bias_ref[...] = jnp.zeros_like(bias_ref)
    later_ref[...] = jnp.zeros_like(later_ref)

    def gradients(i, carry):
        chunks = [blocks - 1 - i * per - j for j in range(per)]
        pairs = [(r, h) for r in chunks for h in range(heads)]

        def stacked(parts):
            return [below(*parts[j * heads : (j + 1) * heads]) for j in range(per)]

        def split(parts):
            return [part[s] for part in parts for s in at]

        def weigh(r, h):
            k = k_ref[r, at[h], :]
            both_ways = dot(q_ref[r, at[h], :], below(k, k))
            return jnp.where(mask, both_ways[:, :chunk] + both_ways[:, chunk:], 0.0)

        def from_before(r, h):
            q = q_ref[r, at[h], :both]
            s = before_ref[r, at[h], :]
            return dot(beside(q, q), below(s[:, : 2 * dim], s[:, 2 * dim :]))

        inner = stacked([weigh(r, h) for r, h in pairs])
        values = [kv_ref[r, 1] for r in chunks]
        wide = [beside(v, ones) for v in values]
        state_part = stacked([from_before(r, h) for r, h in pairs])
        out = [
            dot(beside(*halves(a)), below(w, w)) + b for a, w, b in zip(inner, wide, state_part)
        ]
        inverse = [1.0 / o[:, dim:] for o in out]
        student = [o[:, :dim] * n for o, n in zip(out, inverse)]
        error = [s - below(*[teacher_ref[r, h] for h in range(heads)]) for s, r in zip(student, chunks)]
        numer = [e * n for e, n in zip(error, inverse)]
        denom = [
            -jnp.sum(e * s, axis=1, keepdims=True) * n for e, s, n in zip(error, student, inverse)
        ]
        numer_pair = [beside(*halves(n)) for n in numer]
        spread = [dot_nt(n, beside(v, v)) for n, v in zip(numer_pair, values)]
        inner_grad = [
            jnp.where(mask_all, s + d[:, :chunk], 0.0) for s, d in zip(spread, denom)
        ]
        grad_pair = [beside(*halves(g)) for g in inner_grad]
        numer_pair, grad_pair, denom = split(numer_pair), split(grad_pair), split(denom)
        query_side, from_later, later_bias = [], [], []
        for (r, h), n, g, d_full in zip(pairs, numer_pair, grad_pair, denom):
            t, k, s = t_ref[r, at[h], :], k_ref[r, at[h], :], before_ref[r, at[h], :]
            t_high, k_high = t[:, :chunk], k[:, :chunk]
            g_high, g_low = g[:, :chunk], g[:, chunk:]
            n_high, n_low = n[:, :dim], n[:, dim:]
            s_high, s_low = s[:, :dim], s[:, 2 * dim : 3 * dim]
            first = beside(n_high, g_high)
            from_later.append(dot(beside(t, t_high), below(first, first, beside(n_low, g_low))))
            grad_t = dot_nt(
                beside(k, k_high, s_high, s_high, s_low),
                beside(g_high, g_high, g_low, n_high, n_low, n_high),
            )
            d_row = d_full.T
            phi = t_high.astype(F32) + t[:, chunk:].astype(F32)
            later_bias.append(jnp.sum(phi * d_row, axis=1, keepdims=True))
            grad_t = grad_t + norm_ref[r, at[h], :] * d_row
            query_side.append(beside(*halves(grad_t * jnp.minimum(phi, 1.0))))
        for h in range(heads):
            left = beside(*[query_side[j * heads + h] for j in range(per)])
            right = below(*[x_ref[r, h] for r in chunks for _ in range(2)])
            sum_q_ref[at[h], :] += dot(left, right)
        later = later_ref[...]
        bias = bias_ref[...]
        key_side = []
        for j, (r, v) in enumerate(zip(chunks, values)):
            own = below(*from_later[j * heads : (j + 1) * heads])
            grad_t = own[:, dim:] + dot_nt(beside(*halves(later)), beside(v, v)) + bias
            pair = k_ref[r]
            slope = jnp.minimum(pair[:, :chunk].astype(F32) + pair[:, chunk:].astype(F32), 1.0)
            key_side.append(beside(*halves(grad_t * slope)))
            later = later + own[:, :dim]
            bias = bias + below(*later_bias[j * heads : (j + 1) * heads])
        sum_k_ref[...] += dot(
            beside(*key_side), below(*[kv_ref[r, 0] for r in chunks for _ in range(2)])
        )
        later_ref[...] = later
        bias_ref[...] = jnp.broadcast_to(bias, bias_ref.shape)
        return carry

    lax.fori_loop(0, blocks // per, gradients, 0)
    grad_ref[pl.ds(heads * both, spare), :] = jnp.zeros((spare, dim), F32)
    for h in range(heads):
        parts = []
        for total in (sum_q_ref, sum_k_ref):
            both_signs = total[at[h], :]
            parts.append(both_signs[:features] - both_signs[features:])
        top = jnp.max(jnp.abs(below(*parts)), axis=0, keepdims=True)
        power = power_of(jnp.max(top, axis=1, keepdims=True))
        for i, part in enumerate(parts):
            rows = pl.ds((i * heads + h) * features, features)
            grad_ref[rows, :] = part * jnp.exp2(-power)
        grad_ref[pl.ds(heads * both + h, 1), :] = jnp.broadcast_to(power, (1, dim))


def student_scratch(blocks, rows, chunk, dim):
    return [
        pltpu.VMEM((rows, 2 * dim), BF16),
        pltpu.VMEM((rows, 2 * dim), BF16),
        pltpu.VMEM((blocks, rows, 2 * chunk), BF16),
        pltpu.VMEM((blocks, rows, 2 * chunk), BF16),
        pltpu.VMEM((blocks, rows, 2 * chunk), BF16),
        pltpu.VMEM((blocks, rows, 4 * dim), BF16),
        pltpu.VMEM((blocks, rows, dim), F32),
        pltpu.VMEM((rows, 2 * dim), F32),
        pltpu.VMEM((rows, chunk), F32),
        pltpu.VMEM((rows, dim), F32),
        pltpu.VMEM((rows, dim), F32),
        pltpu.VMEM((rows, dim), F32),
    ]


def student_shape(heads, rows, dim):
    return jax.ShapeDtypeStruct((rows + (heads + 7) // 8 * 8, dim), F32)


def student_call(start, x, kv, teacher, map_query, map_key):
    blocks, heads, chunk, dim = x.shape
    features = map_query.shape[1]
    rows = heads * 2 * features
    whole = pl.BlockSpec(memory_space=pltpu.VMEM)
    return pl.pallas_call(
        functools.partial(student_kernel, start, heads),
        in_specs=[whole] * 5,
        out_specs=whole,
        out_shape=student_shape(heads, rows, dim),
        scratch_shapes=student_scratch(blocks, rows, chunk, dim),
        compiler_params=pltpu.CompilerParams(vmem_limit_bytes=VMEM_LIMIT),
        cost_estimate=pl.CostEstimate(
            flops=200 * rows * blocks * chunk * dim,
            bytes_accessed=12 * heads * blocks * chunk * dim,
            transcendentals=3 * rows * blocks * chunk,
        ),
    )(*[in_vmem(a) for a in (x, kv, teacher, map_query, map_key)])


def partner(at, step, count):
    return at ^ step if count & (count - 1) == 0 else (at + step) % count


def both_kernel(shape, rows, scale, source_of, start, place_ref, *refs):
    places, cores, heads, _ = shape
    count = places // cores + cores
    arrived, (mq_ref, mk_ref), refs = refs[:count], refs[count : count + 2], refs[count + 2 :]
    kv_ref, energy_ref, grad_ref, x_ref, out_ref, scores_ref, *scratch = refs
    teacher_kernel(
        shape, rows, scale, source_of, place_ref, *arrived, x_ref, kv_ref, out_ref, energy_ref, scores_ref
    )
    student_kernel(start, heads, x_ref, kv_ref, out_ref, mq_ref, mk_ref, grad_ref, *scratch)


def both_call(start, place, pieces, keys, map_query, map_key, places, source_of):
    _, chunk, dim = pieces[0].shape
    cores = len(keys)
    heads = pieces[0].shape[0] // cores
    rows = 2 * chunk if places % 2 == 0 else chunk
    steps = places * chunk // rows
    held = (steps, rows, rows) if steps > 8 else (1, 8, 128)
    both = heads * 2 * map_query.shape[1]
    whole = pl.BlockSpec(memory_space=pltpu.VMEM)
    operands = [in_vmem(a) for a in pieces + keys + [map_query, map_key]]
    return pl.pallas_call(
        functools.partial(
            both_kernel,
            (places, cores, heads, True),
            rows,
            1.0 / math.sqrt(dim),
            source_of,
            start,
        ),
        in_specs=[pl.BlockSpec(memory_space=pltpu.SMEM)] + [whole] * len(operands),
        out_specs=[whole] * 3,
        out_shape=[
            pltpu.VMEM((places, 2, chunk, dim), BF16),
            jax.ShapeDtypeStruct((8, dim), F32),
            student_shape(heads, both, dim),
        ],
        scratch_shapes=[
            pltpu.VMEM((places, heads, chunk, dim), BF16),
            pltpu.VMEM((places, heads, chunk, dim), F32),
            pltpu.VMEM(held, F32),
        ]
        + student_scratch(places, both, chunk, dim),
        compiler_params=pltpu.CompilerParams(vmem_limit_bytes=VMEM_LIMIT),
        cost_estimate=pl.CostEstimate(
            flops=200 * both * places * chunk * dim + 10 * heads * (places * chunk) ** 2 * dim,
            bytes_accessed=20 * heads * places * chunk * dim,
            transcendentals=heads * (places * chunk) ** 2 // 2,
        ),
    )(place, *operands)


def exchange(queries, key_states, value_vector_states, heads, parts):
    places = lax.axis_size("ctx")
    cores = 2 if places % 2 == 0 else 1
    chips = places // cores
    place = lax.axis_index("ctx")
    core, chip = place % cores, place // cores
    tokens, query_heads, dim = queries.shape
    key_heads = key_states.shape[1]
    padding = heads * places - query_heads
    mirrored = chips & (chips - 1) == 0

    def target_of(at, j):
        return partner(at, j, chips)

    def source_of(at, j):
        return at ^ j if mirrored else (at + chips - j) % chips

    def send(a, j):
        return lax.ppermute(
            a, "ctx", [(i, target_of(i // cores, j) * cores + i % cores) for i in range(places)]
        )

    def swap(a):
        return lax.ppermute(a, "ctx", [(i, i ^ 1) for i in range(places)])

    def pick(a, i, axis=0):
        return lax.dynamic_index_in_dim(a, i, axis, False)

    by_head = jnp.pad(queries, ((0, 0), (0, padding), (0, 0))) if padding else queries
    by_head = by_head.transpose(1, 0, 2).reshape(chips, cores, heads, tokens, dim)
    *flat, by_head = lax.optimization_barrier((key_states, value_vector_states, by_head))
    flat = [a.reshape(tokens, key_heads * dim) for a in flat]
    kv = jnp.stack(
        [jnp.stack([a[:, g * dim : (g + 1) * dim] for a in flat]) for g in range(key_heads)]
    )
    def group_of(at):
        first = jnp.minimum((at * cores + core) * heads, query_heads - 1)
        return first // (query_heads // key_heads)

    mine = [pick(by_head, core, 1)]
    if cores == 2:
        mine.append(swap(pick(by_head, 1 - core, 1)))
        kv = lax.optimization_barrier((kv, mine[1]))[0]
    to_send = [pick(kv, group_of(target_of(chip, j))) for j in range(chips)]
    arrived = []
    for start, stop in parts:
        pieces = []
        for j in range(chips):
            piece = [pick(q, target_of(chip, j))[start:stop] for q in mine]
            if j == 1 and not arrived:
                piece.append(to_send[j])
            pieces.append(jnp.concatenate(piece))
        if arrived and chips > 1:
            pieces = lax.optimization_barrier((*pieces, arrived[-1][1]))[:chips]
        arrived.append([pieces[0]] + [send(a, j) for j, a in enumerate(pieces) if j])
    own_keys = [send(a, j) if j > 1 else a for j, a in enumerate(to_send)]
    if chips > 1:
        own_keys[1] = arrived[0][1][-2:]
    keys = [jnp.stack(own_keys)]
    if cores == 2:
        keys.append(swap(keys[0]))
    return arrived, keys, source_of


def unpack_kernel(heads, power_rows, tail_row, scale, gathered_ref, *out_refs):
    places, _, dim = gathered_ref.shape
    features = out_refs[0].shape[1]

    def row(p, i):
        return gathered_ref[p, i : i + 1, :]

    energy = jnp.zeros((1, dim), F32)
    for p in range(places):
        near_one = row(p, tail_row + 1) + row(p, tail_row + 2) * (1.0 / 1024.0)
        energy = energy + near_one * jnp.exp2(row(p, tail_row))
    scale = scale / energy
    for p in range(places):
        for h in range(heads):
            factor = jnp.exp2(row(p, power_rows[h])) * scale
            for i, out_ref in enumerate(out_refs):
                rows = pl.ds((i * heads + h) * features, features)
                out_ref[p * heads + h] = gathered_ref[p, rows, :] * factor


def unpack_call(gathered, heads, features, power_rows, tail_row, scale):
    places, _, dim = gathered.shape
    whole = pl.BlockSpec(memory_space=pltpu.VMEM)
    return pl.pallas_call(
        functools.partial(unpack_kernel, heads, power_rows, tail_row, scale),
        in_specs=[whole],
        out_specs=[whole, whole],
        out_shape=[jax.ShapeDtypeStruct((places * heads, features, dim), F32)] * 2,
        compiler_params=pltpu.CompilerParams(vmem_limit_bytes=VMEM_LIMIT),
    )(gathered)


def on_device(queries, key_states, value_vector_states, map_query, map_key):
    places = lax.axis_size("ctx")
    planes = lax.axis_size("head")
    place = lax.axis_index("ctx")
    tokens, query_heads, dim = queries.shape
    key_heads = key_states.shape[1]
    features = map_query.shape[2]
    group = query_heads // key_heads
    heads = min(d for d in range(1, group + 1) if group % d == 0 and d * places >= query_heads)
    padding = heads * places - query_heads
    half = heads // 2
    parts = [(0, half), (half, heads)] if half else [(0, heads)]
    arrived, keys, source_of = exchange(queries, key_states, value_vector_states, heads, parts)

    def own(weights):
        weights = weights.transpose(0, 2, 1)
        weights = jnp.pad(weights, ((0, padding), (0, 0), (0, 0))) if padding else weights
        return lax.dynamic_slice_in_dim(weights, place * heads, heads, 0)

    own_query, own_key = own(map_query), own(map_key)
    position = place.astype(jnp.int32).reshape(1)
    kv, energy, grads, powers = None, None, [], []
    for (start, stop), pieces in zip(parts, arrived):
        if stop < heads:
            kv, energy, result = both_call(
                start, position, pieces, keys, own_query, own_key, places, source_of
            )
        else:
            x, *found = teacher_call(position, pieces, kv, keys, energy, places, source_of)
            if kv is None:
                kv = found.pop(0)
            teacher, energy = found
            result = student_call(start, x, kv, teacher, own_query, own_key)
        rows = (stop - start) * features
        grads.append((result[:rows], result[rows : 2 * rows]))
        powers.append(result[2 * rows :])
    energy = jnp.where(place * heads < query_heads, energy, 0.0)
    shifted = [
        lax.ppermute(energy, "head", [(i, partner(i, k, planes)) for i in range(planes)])
        for k in range(1, planes)
    ]
    energy = sum(shifted, energy)
    power = power_of(energy)
    near_one = energy * jnp.exp2(-power)
    first = lax.reduce_precision(near_one, 5, 10)
    row = lax.broadcasted_iota(jnp.int32, energy.shape, 0)
    tail = jnp.where(row == 0, power, jnp.where(row == 1, first, (near_one - first) * 1024.0))
    grads = [part for side in zip(*grads) for part in side]
    sent = jnp.concatenate(grads + powers + [tail]).astype(F16)
    used = sent.shape[0]
    gathered = lax.all_gather(jnp.pad(sent, ((0, -used % 16), (0, 0))), "ctx").astype(F32)
    power_rows, at = [], heads * 2 * features
    for (start, stop), p in zip(parts, powers):
        power_rows += [at + h for h in range(stop - start)]
        at += p.shape[0]
    scale = 2.0 * query_heads * planes
    unpacked = unpack_call(in_vmem(gathered), heads, features, power_rows, at, scale)
    return tuple(a[:query_heads].transpose(0, 2, 1) for a in unpacked)


def solution(mesh):
    placed = (
        P("ctx", "head", None),
        P("ctx", "head", None),
        P("ctx", "head", None),
        P("head", None, None),
        P("head", None, None),
    )
    return jax.shard_map(
        on_device,
        mesh=mesh,
        in_specs=placed,
        out_specs=(P("head", None, None), P("head", None, None)),
        check_vma=False,
    )
```

```python
import functools
import math

import jax
import jax.numpy as jnp
from jax import lax
from jax.experimental import pallas as pl
from jax.experimental.pallas import tpu as pltpu
from jax.sharding import PartitionSpec as P

F32 = jnp.float32
BF16 = jnp.bfloat16
F16 = jnp.float16
VMEM_LIMIT = 44 * 1024 * 1024


def dot(a, b):
    return lax.dot_general(a, b, (((1,), (0,)), ((), ())), preferred_element_type=F32)


def dot_nt(a, b):
    return lax.dot_general(a, b, (((1,), (1,)), ((), ())), preferred_element_type=F32)


def halves(x):
    high = x.astype(BF16)
    return high, (x - high.astype(F32)).astype(BF16)


def beside(*parts):
    return jnp.concatenate(parts, axis=1)


def below(*parts):
    return jnp.concatenate(parts, axis=0)


def feature(logit):
    return jnp.where(logit > 0, logit + 1.0, jnp.exp(jnp.minimum(logit, 0.0)))


def power_of(top):
    return jnp.clip(jnp.round(jnp.log2(jnp.maximum(top, 1e-30))), -100.0, 126.0)


def causal(rows, columns, shift):
    row = lax.broadcasted_iota(jnp.int32, (rows, columns), 0)
    column = lax.broadcasted_iota(jnp.int32, (rows, columns), 1)
    return column <= row + shift


def teacher_kernel(shape, rows, scale, source_of, place_ref, *refs):
    places, cores, heads, with_keys = shape
    chips = places // cores
    pieces, refs = refs[:chips], refs[chips:]
    if with_keys:
        keys, refs = refs[:cores], refs[cores:]
        x_ref, kv_ref, out_ref, energy_ref, scores_ref = refs
    else:
        kv_ref, before_ref, x_ref, out_ref, energy_ref, scores_ref = refs
    blocks, _, chunk, dim = x_ref.shape
    per_row = rows // chunk
    steps = blocks // per_row
    power = scale * math.log2(math.e)
    mask = causal(rows, rows, 0)
    place = place_ref[0]
    core = place % cores
    for j, piece in enumerate(pieces):
        base = source_of(place // cores, j) * cores
        for i in range(cores):
            block = base + (core if i == 0 else 1 - core)
            x_ref[block] = piece[i * heads : (i + 1) * heads]
            if with_keys:
                kv_ref[block] = keys[i][j]

    def finish(h, r, weighted, total):
        teacher = weighted / total
        for i in range(per_row):
            out_ref[r * per_row + i, h] = teacher[i * chunk : (i + 1) * chunk]
        return jnp.sum((teacher * teacher).reshape(rows // 8, 8, dim), axis=0)

    def take(h, r):
        return x_ref[pl.ds(r * per_row, per_row), h].reshape(rows, dim)

    def keyed(i, r, count=1):
        return kv_ref[pl.ds(r * per_row, count * per_row), i].reshape(count * rows, dim)

    def one_head(h, energy):
        parts, tops, done = [], [], []
        for r in range(steps):
            scores = dot_nt(take(h, r), keyed(0, 0, r + 1))
            last = jnp.where(mask, scores[:, r * rows :], -1e30)
            scores = beside(scores[:, : r * rows], last) if r else last
            parts.append(scores)
            tops.append(jnp.max(scores, axis=1, keepdims=True))
        for r in range(steps):
            weights = jnp.exp2((parts[r] - tops[r]) * power)
            total = jnp.sum(weights, axis=1, keepdims=True)
            done.append((dot(weights.astype(BF16), keyed(1, 0, r + 1)), total))
        for r in range(steps):
            energy = energy + finish(h, r, *done[r])
        return energy

    def one_long_head(h, energy):
        def one_row(r, energy):
            q = take(h, r)

            def look(j, top):
                scores = dot_nt(q, keyed(0, j))
                scores = jnp.where((j < r) | mask, scores, -1e30)
                scores_ref[j] = scores
                return jnp.maximum(top, jnp.max(scores, axis=1, keepdims=True))

            top = lax.fori_loop(0, r + 1, look, jnp.full((rows, 1), -1e30, F32))

            def add(j, state):
                weighted, total = state
                weights = jnp.exp2((scores_ref[j] - top) * power)
                total = total + jnp.sum(weights, axis=1, keepdims=True)
                return weighted + dot(weights.astype(BF16), keyed(1, j)), total

            weighted, total = lax.fori_loop(
                0, r + 1, add, (jnp.zeros((rows, dim), F32), jnp.zeros((rows, 1), F32))
            )
            return energy + finish(h, r, weighted, total)

        return lax.fori_loop(0, steps, one_row, energy)

    energy = jnp.zeros((8, dim), F32)
    if steps <= 8:
        for h in range(heads):
            energy = one_head(h, energy)
    else:
        energy = lax.fori_loop(0, heads, one_long_head, energy)
    energy = jnp.sum(jnp.sum(energy, axis=0, keepdims=True), axis=1, keepdims=True)
    energy = jnp.broadcast_to(energy, energy_ref.shape)
    energy_ref[...] = energy if with_keys else energy + before_ref[...]


def in_vmem(a):
    return pltpu.with_memory_space_constraint(a, pltpu.VMEM)


def teacher_call(place, pieces, kv, keys, before, places, source_of):
    _, chunk, dim = pieces[0].shape
    cores = len(keys)
    with_keys = kv is None
    heads = pieces[0].shape[0] // cores
    rows = 2 * chunk if places % 2 == 0 else chunk
    steps = places * chunk // rows
    held = (steps, rows, rows) if steps > 8 else (1, 8, 128)
    whole = pl.BlockSpec(memory_space=pltpu.VMEM)
    operands = [in_vmem(p) for p in pieces + (keys if with_keys else [kv])]
    operands += [] if with_keys else [before]
    return pl.pallas_call(
        functools.partial(
            teacher_kernel,
            (places, cores, heads, with_keys),
            rows,
            1.0 / math.sqrt(dim),
            source_of,
        ),
        in_specs=[pl.BlockSpec(memory_space=pltpu.SMEM)] + [whole] * len(operands),
        out_specs=[whole] * (3 + with_keys),
        out_shape=[pltpu.VMEM((places, heads, chunk, dim), BF16)]
        + [pltpu.VMEM((places, 2, chunk, dim), BF16)] * with_keys
        + [
            pltpu.VMEM((places, heads, chunk, dim), F32),
            jax.ShapeDtypeStruct((8, dim), F32),
        ],
        scratch_shapes=[pltpu.VMEM(held, F32)],
        compiler_params=pltpu.CompilerParams(vmem_limit_bytes=VMEM_LIMIT),
        cost_estimate=pl.CostEstimate(
            flops=10 * heads * (places * chunk) ** 2 * dim,
            bytes_accessed=8 * heads * places * chunk * dim,
            transcendentals=heads * (places * chunk) ** 2 // 2,
        ),
    )(place, *operands)


def student_kernel(
    start,
    heads,
    x_ref,
    kv_ref,
    teacher_ref,
    mq_ref,
    mk_ref,
    grad_ref,
    wq_ref,
    wk_ref,
    q_ref,
    t_ref,
    k_ref,
    before_ref,
    norm_ref,
    state_ref,
    bias_ref,
    later_ref,
    sum_q_ref,
    sum_k_ref,
):
    blocks, _, chunk, dim = x_ref.shape
    features = mq_ref.shape[1]
    both = 2 * features
    spare = grad_ref.shape[0] - heads * both
    at = [slice(h * both, (h + 1) * both) for h in range(heads)]
    per = next(p for p in (8, 4, 2, 1) if blocks % p == 0 and (p * heads <= 16 or p == 1))

    for h in range(heads):
        for source, target in ((mq_ref, wq_ref), (mk_ref, wk_ref)):
            high, low = halves(source[start + h])
            target[at[h], :] = below(beside(high, low), beside(-high, -low))
    state_ref[...] = jnp.zeros_like(state_ref)
    sum_q_ref[...] = jnp.zeros_like(sum_q_ref)
    sum_k_ref[...] = jnp.zeros_like(sum_k_ref)
    mask = causal(chunk, chunk, 0)
    mask_all = below(*[mask] * heads)
    ones = jnp.ones((chunk, dim), BF16)

    def features_of(i, carry):
        chunks = [i * per + j for j in range(per)]
        keys = [kv_ref[r, 0] for r in chunks]
        pairs = [
            beside(*halves(feature(dot_nt(wk_ref[...], beside(k, k))))) for k in keys
        ]
        wide = [beside(kv_ref[r, 1], ones) for r in chunks]
        added = [dot(p, below(w, w)) for p, w in zip(pairs, wide)]
        for r in chunks:
            for h in range(heads):
                q = x_ref[r, h]
                high, low = halves(feature(dot_nt(beside(q, q), wq_ref[at[h], :])))
                q_ref[r, at[h], :] = beside(high, low)
                t_ref[r, at[h], :] = beside(high.T, low.T)
        state = state_ref[...]
        for r, p, a in zip(chunks, pairs, added):
            k_ref[r] = p
            before_ref[r] = beside(*halves(state))
            norm_ref[r] = state[:, dim:]
            state = state + a
        state_ref[...] = state
        return carry

    lax.fori_loop(0, blocks // per, features_of, 0)
    bias_ref[...] = jnp.zeros_like(bias_ref)
    later_ref[...] = jnp.zeros_like(later_ref)

    def gradients(i, carry):
        chunks = [blocks - 1 - i * per - j for j in range(per)]
        pairs = [(r, h) for r in chunks for h in range(heads)]

        def stacked(parts):
            return [below(*parts[j * heads : (j + 1) * heads]) for j in range(per)]

        def split(parts):
            return [part[s] for part in parts for s in at]

        def weigh(r, h):
            k = k_ref[r, at[h], :]
            both_ways = dot(q_ref[r, at[h], :], below(k, k))
            return jnp.where(mask, both_ways[:, :chunk] + both_ways[:, chunk:], 0.0)

        def from_before(r, h):
            q = q_ref[r, at[h], :both]
            s = before_ref[r, at[h], :]
            return dot(beside(q, q), below(s[:, : 2 * dim], s[:, 2 * dim :]))

        inner = stacked([weigh(r, h) for r, h in pairs])
        values = [kv_ref[r, 1] for r in chunks]
        wide = [beside(v, ones) for v in values]
        state_part = stacked([from_before(r, h) for r, h in pairs])
        out = [
            dot(beside(*halves(a)), below(w, w)) + b for a, w, b in zip(inner, wide, state_part)
        ]
        inverse = [1.0 / o[:, dim:] for o in out]
        student = [o[:, :dim] * n for o, n in zip(out, inverse)]
        error = [s - below(*[teacher_ref[r, h] for h in range(heads)]) for s, r in zip(student, chunks)]
        numer = [e * n for e, n in zip(error, inverse)]
        denom = [
            -jnp.sum(e * s, axis=1, keepdims=True) * n for e, s, n in zip(error, student, inverse)
        ]
        numer_pair = [beside(*halves(n)) for n in numer]
        spread = [dot_nt(n, beside(v, v)) for n, v in zip(numer_pair, values)]
        inner_grad = [
            jnp.where(mask_all, s + d[:, :chunk], 0.0) for s, d in zip(spread, denom)
        ]
        grad_pair = [beside(*halves(g)) for g in inner_grad]
        numer_pair, grad_pair, denom = split(numer_pair), split(grad_pair), split(denom)
        query_side, from_later, later_bias = [], [], []
        for (r, h), n, g, d_full in zip(pairs, numer_pair, grad_pair, denom):
            t, k, s = t_ref[r, at[h], :], k_ref[r, at[h], :], before_ref[r, at[h], :]
            t_high, k_high = t[:, :chunk], k[:, :chunk]
            g_high, g_low = g[:, :chunk], g[:, chunk:]
            n_high, n_low = n[:, :dim], n[:, dim:]
            s_high, s_low = s[:, :dim], s[:, 2 * dim : 3 * dim]
            first = beside(n_high, g_high)
            from_later.append(dot(beside(t, t_high), below(first, first, beside(n_low, g_low))))
            grad_t = dot_nt(
                beside(k, k_high, s_high, s_high, s_low),
                beside(g_high, g_high, g_low, n_high, n_low, n_high),
            )
            d_row = d_full.T
            phi = t_high.astype(F32) + t[:, chunk:].astype(F32)
            later_bias.append(jnp.sum(phi * d_row, axis=1, keepdims=True))
            grad_t = grad_t + norm_ref[r, at[h], :] * d_row
            query_side.append(beside(*halves(grad_t * jnp.minimum(phi, 1.0))))
        for h in range(heads):
            left = beside(*[query_side[j * heads + h] for j in range(per)])
            right = below(*[x_ref[r, h] for r in chunks for _ in range(2)])
            sum_q_ref[at[h], :] += dot(left, right)
        later = later_ref[...]
        bias = bias_ref[...]
        key_side = []
        for j, (r, v) in enumerate(zip(chunks, values)):
            own = below(*from_later[j * heads : (j + 1) * heads])
            grad_t = own[:, dim:] + dot_nt(beside(*halves(later)), beside(v, v)) + bias
            pair = k_ref[r]
            slope = jnp.minimum(pair[:, :chunk].astype(F32) + pair[:, chunk:].astype(F32), 1.0)
            key_side.append(beside(*halves(grad_t * slope)))
            later = later + own[:, :dim]
            bias = bias + below(*later_bias[j * heads : (j + 1) * heads])
        sum_k_ref[...] += dot(
            beside(*key_side), below(*[kv_ref[r, 0] for r in chunks for _ in range(2)])
        )
        later_ref[...] = later
        bias_ref[...] = jnp.broadcast_to(bias, bias_ref.shape)
        return carry

    lax.fori_loop(0, blocks // per, gradients, 0)
    grad_ref[pl.ds(heads * both, spare), :] = jnp.zeros((spare, dim), F32)
    for h in range(heads):
        parts = []
        for total in (sum_q_ref, sum_k_ref):
            both_signs = total[at[h], :]
            parts.append(both_signs[:features] - both_signs[features:])
        top = jnp.max(jnp.abs(below(*parts)), axis=0, keepdims=True)
        power = power_of(jnp.max(top, axis=1, keepdims=True))
        for i, part in enumerate(parts):
            rows = pl.ds((i * heads + h) * features, features)
            grad_ref[rows, :] = part * jnp.exp2(-power)
        grad_ref[pl.ds(heads * both + h, 1), :] = jnp.broadcast_to(power, (1, dim))


def student_scratch(blocks, rows, chunk, dim):
    return [
        pltpu.VMEM((rows, 2 * dim), BF16),
        pltpu.VMEM((rows, 2 * dim), BF16),
        pltpu.VMEM((blocks, rows, 2 * chunk), BF16),
        pltpu.VMEM((blocks, rows, 2 * chunk), BF16),
        pltpu.VMEM((blocks, rows, 2 * chunk), BF16),
        pltpu.VMEM((blocks, rows, 4 * dim), BF16),
        pltpu.VMEM((blocks, rows, dim), F32),
        pltpu.VMEM((rows, 2 * dim), F32),
        pltpu.VMEM((rows, chunk), F32),
        pltpu.VMEM((rows, dim), F32),
        pltpu.VMEM((rows, dim), F32),
        pltpu.VMEM((rows, dim), F32),
    ]


def student_shape(heads, rows, dim):
    return jax.ShapeDtypeStruct((rows + (heads + 7) // 8 * 8, dim), F32)


def student_call(start, x, kv, teacher, map_query, map_key):
    blocks, heads, chunk, dim = x.shape
    features = map_query.shape[1]
    rows = heads * 2 * features
    whole = pl.BlockSpec(memory_space=pltpu.VMEM)
    return pl.pallas_call(
        functools.partial(student_kernel, start, heads),
        in_specs=[whole] * 5,
        out_specs=whole,
        out_shape=student_shape(heads, rows, dim),
        scratch_shapes=student_scratch(blocks, rows, chunk, dim),
        compiler_params=pltpu.CompilerParams(vmem_limit_bytes=VMEM_LIMIT),
        cost_estimate=pl.CostEstimate(
            flops=200 * rows * blocks * chunk * dim,
            bytes_accessed=12 * heads * blocks * chunk * dim,
            transcendentals=3 * rows * blocks * chunk,
        ),
    )(*[in_vmem(a) for a in (x, kv, teacher, map_query, map_key)])


def partner(at, step, count):
    return at ^ step if count & (count - 1) == 0 else (at + step) % count


def both_kernel(shape, rows, scale, source_of, start, place_ref, *refs):
    places, cores, heads, _ = shape
    count = places // cores + cores
    arrived, (mq_ref, mk_ref), refs = refs[:count], refs[count : count + 2], refs[count + 2 :]
    kv_ref, energy_ref, grad_ref, x_ref, out_ref, scores_ref, *scratch = refs
    teacher_kernel(
        shape, rows, scale, source_of, place_ref, *arrived, x_ref, kv_ref, out_ref, energy_ref, scores_ref
    )
    student_kernel(start, heads, x_ref, kv_ref, out_ref, mq_ref, mk_ref, grad_ref, *scratch)


def both_call(start, place, pieces, keys, map_query, map_key, places, source_of):
    _, chunk, dim = pieces[0].shape
    cores = len(keys)
    heads = pieces[0].shape[0] // cores
    rows = 2 * chunk if places % 2 == 0 else chunk
    steps = places * chunk // rows
    held = (steps, rows, rows) if steps > 8 else (1, 8, 128)
    both = heads * 2 * map_query.shape[1]
    whole = pl.BlockSpec(memory_space=pltpu.VMEM)
    operands = [in_vmem(a) for a in pieces + keys + [map_query, map_key]]
    return pl.pallas_call(
        functools.partial(
            both_kernel,
            (places, cores, heads, True),
            rows,
            1.0 / math.sqrt(dim),
            source_of,
            start,
        ),
        in_specs=[pl.BlockSpec(memory_space=pltpu.SMEM)] + [whole] * len(operands),
        out_specs=[whole] * 3,
        out_shape=[
            pltpu.VMEM((places, 2, chunk, dim), BF16),
            jax.ShapeDtypeStruct((8, dim), F32),
            student_shape(heads, both, dim),
        ],
        scratch_shapes=[
            pltpu.VMEM((places, heads, chunk, dim), BF16),
            pltpu.VMEM((places, heads, chunk, dim), F32),
            pltpu.VMEM(held, F32),
        ]
        + student_scratch(places, both, chunk, dim),
        compiler_params=pltpu.CompilerParams(vmem_limit_bytes=VMEM_LIMIT),
        cost_estimate=pl.CostEstimate(
            flops=200 * both * places * chunk * dim + 10 * heads * (places * chunk) ** 2 * dim,
            bytes_accessed=20 * heads * places * chunk * dim,
            transcendentals=heads * (places * chunk) ** 2 // 2,
        ),
    )(place, *operands)


def exchange(queries, key_states, value_vector_states, heads, parts):
    places = lax.axis_size("ctx")
    cores = 2 if places % 2 == 0 else 1
    chips = places // cores
    place = lax.axis_index("ctx")
    core, chip = place % cores, place // cores
    tokens, query_heads, dim = queries.shape
    key_heads = key_states.shape[1]
    padding = heads * places - query_heads
    mirrored = chips & (chips - 1) == 0

    def target_of(at, j):
        return partner(at, j, chips)

    def source_of(at, j):
        return at ^ j if mirrored else (at + chips - j) % chips

    def send(a, j):
        return lax.ppermute(
            a, "ctx", [(i, target_of(i // cores, j) * cores + i % cores) for i in range(places)]
        )

    def swap(a):
        return lax.ppermute(a, "ctx", [(i, i ^ 1) for i in range(places)])

    def pick(a, i, axis=0):
        return lax.dynamic_index_in_dim(a, i, axis, False)

    by_head = jnp.pad(queries, ((0, 0), (0, padding), (0, 0))) if padding else queries
    by_head = by_head.transpose(1, 0, 2).reshape(chips, cores, heads, tokens, dim)
    *flat, by_head = lax.optimization_barrier((key_states, value_vector_states, by_head))
    flat = [a.reshape(tokens, key_heads * dim) for a in flat]
    kv = jnp.stack(
        [jnp.stack([a[:, g * dim : (g + 1) * dim] for a in flat]) for g in range(key_heads)]
    )
    def group_of(at):
        first = jnp.minimum((at * cores + core) * heads, query_heads - 1)
        return first // (query_heads // key_heads)

    mine = [pick(by_head, core, 1)]
    if cores == 2:
        mine.append(swap(pick(by_head, 1 - core, 1)))
        kv = lax.optimization_barrier((kv, mine[1]))[0]
    to_send = [pick(kv, group_of(target_of(chip, j))) for j in range(chips)]
    arrived = []
    for start, stop in parts:
        pieces = []
        for j in range(chips):
            piece = [pick(q, target_of(chip, j))[start:stop] for q in mine]
            if j == 1 and not arrived:
                piece.append(to_send[j])
            pieces.append(jnp.concatenate(piece))
        if arrived and chips > 1:
            pieces = lax.optimization_barrier((*pieces, arrived[-1][1]))[:chips]
        arrived.append([pieces[0]] + [send(a, j) for j, a in enumerate(pieces) if j])
    own_keys = [send(a, j) if j > 1 else a for j, a in enumerate(to_send)]
    if chips > 1:
        own_keys[1] = arrived[0][1][-2:]
    keys = [jnp.stack(own_keys)]
    if cores == 2:
        keys.append(swap(keys[0]))
    return arrived, keys, source_of


def unpack_kernel(heads, power_rows, tail_row, scale, gathered_ref, *refs):
    *out_refs, held_ref, sems = refs
    places, _, dim = gathered_ref.shape
    features = out_refs[0].shape[1]
    runs = sems.shape[1]
    per = places // runs
    copies = []

    def row(p, i):
        return gathered_ref[p, i : i + 1, :]

    energy = jnp.zeros((1, dim), F32)
    for p in range(places):
        near_one = row(p, tail_row + 1) + row(p, tail_row + 2) * (1.0 / 1024.0)
        energy = energy + near_one * jnp.exp2(row(p, tail_row))
    scale = scale / energy
    for run in range(runs):
        for p in range(run * per, (run + 1) * per):
            for h in range(heads):
                factor = jnp.exp2(row(p, power_rows[h])) * scale
                for i in range(2):
                    rows = pl.ds((i * heads + h) * features, features)
                    held_ref[i, p * heads + h] = gathered_ref[p, rows, :] * factor
        done = pl.ds(run * per * heads, per * heads)
        for i, out_ref in enumerate(out_refs):
            copy = pltpu.make_async_copy(held_ref.at[i, done], out_ref.at[done], sems.at[i, run])
            copy.start()
            copies.append(copy)
    for copy in copies:
        copy.wait()


def unpack_call(gathered, heads, features, power_rows, tail_row, scale):
    places, _, dim = gathered.shape
    runs = 4 if places % 4 == 0 else 1
    whole = pl.BlockSpec(memory_space=pltpu.VMEM)
    return pl.pallas_call(
        functools.partial(unpack_kernel, heads, power_rows, tail_row, scale),
        in_specs=[whole],
        out_specs=[pl.BlockSpec(memory_space=pl.ANY)] * 2,
        out_shape=[jax.ShapeDtypeStruct((places * heads, features, dim), F32)] * 2,
        scratch_shapes=[
            pltpu.VMEM((2, places * heads, features, dim), F32),
            pltpu.SemaphoreType.DMA((2, runs)),
        ],
        compiler_params=pltpu.CompilerParams(vmem_limit_bytes=VMEM_LIMIT),
    )(gathered)


def on_device(queries, key_states, value_vector_states, map_query, map_key):
    places = lax.axis_size("ctx")
    planes = lax.axis_size("head")
    place = lax.axis_index("ctx")
    tokens, query_heads, dim = queries.shape
    key_heads = key_states.shape[1]
    features = map_query.shape[2]
    group = query_heads // key_heads
    heads = min(d for d in range(1, group + 1) if group % d == 0 and d * places >= query_heads)
    padding = heads * places - query_heads
    half = heads // 2
    parts = [(0, half), (half, heads)] if half else [(0, heads)]
    arrived, keys, source_of = exchange(queries, key_states, value_vector_states, heads, parts)

    def own(weights):
        weights = weights.transpose(0, 2, 1)
        weights = jnp.pad(weights, ((0, padding), (0, 0), (0, 0))) if padding else weights
        return lax.dynamic_slice_in_dim(weights, place * heads, heads, 0)

    own_query, own_key = own(map_query), own(map_key)
    position = place.astype(jnp.int32).reshape(1)
    kv, energy, grads, powers = None, None, [], []
    for (start, stop), pieces in zip(parts, arrived):
        if stop < heads:
            kv, energy, result = both_call(
                start, position, pieces, keys, own_query, own_key, places, source_of
            )
        else:
            x, *found = teacher_call(position, pieces, kv, keys, energy, places, source_of)
            if kv is None:
                kv = found.pop(0)
            teacher, energy = found
            result = student_call(start, x, kv, teacher, own_query, own_key)
        rows = (stop - start) * features
        grads.append((result[:rows], result[rows : 2 * rows]))
        powers.append(result[2 * rows :])
    energy = jnp.where(place * heads < query_heads, energy, 0.0)
    shifted = [
        lax.ppermute(energy, "head", [(i, partner(i, k, planes)) for i in range(planes)])
        for k in range(1, planes)
    ]
    energy = sum(shifted, energy)
    power = power_of(energy)
    near_one = energy * jnp.exp2(-power)
    first = lax.reduce_precision(near_one, 5, 10)
    row = lax.broadcasted_iota(jnp.int32, energy.shape, 0)
    tail = jnp.where(row == 0, power, jnp.where(row == 1, first, (near_one - first) * 1024.0))
    grads = [part for side in zip(*grads) for part in side]
    sent = jnp.concatenate(grads + powers + [tail]).astype(F16)
    used = sent.shape[0]
    gathered = lax.all_gather(jnp.pad(sent, ((0, -used % 16), (0, 0))), "ctx").astype(F32)
    power_rows, at = [], heads * 2 * features
    for (start, stop), p in zip(parts, powers):
        power_rows += [at + h for h in range(stop - start)]
        at += p.shape[0]
    scale = 2.0 * query_heads * planes
    unpacked = unpack_call(in_vmem(gathered), heads, features, power_rows, at, scale)
    return tuple(a[:query_heads].transpose(0, 2, 1) for a in unpacked)


def solution(mesh):
    placed = (
        P("ctx", "head", None),
        P("ctx", "head", None),
        P("ctx", "head", None),
        P("head", None, None),
        P("head", None, None),
    )
    return jax.shard_map(
        on_device,
        mesh=mesh,
        in_specs=placed,
        out_specs=(P("head", None, None), P("head", None, None)),
        check_vma=False,
    )
```

```python
import functools
import math

import jax
import jax.numpy as jnp
from jax import lax
from jax.experimental import pallas as pl
from jax.experimental.pallas import tpu as pltpu
from jax.sharding import PartitionSpec as P

F32 = jnp.float32
BF16 = jnp.bfloat16
F16 = jnp.float16
VMEM_LIMIT = 44 * 1024 * 1024


def dot(a, b):
    return lax.dot_general(a, b, (((1,), (0,)), ((), ())), preferred_element_type=F32)


def dot_nt(a, b):
    return lax.dot_general(a, b, (((1,), (1,)), ((), ())), preferred_element_type=F32)


def halves(x):
    high = x.astype(BF16)
    return high, (x - high.astype(F32)).astype(BF16)


def beside(*parts):
    return jnp.concatenate(parts, axis=1)


def below(*parts):
    return jnp.concatenate(parts, axis=0)


def feature(logit):
    return jnp.where(logit > 0, logit + 1.0, jnp.exp(jnp.minimum(logit, 0.0)))


def power_of(top):
    return jnp.clip(jnp.round(jnp.log2(jnp.maximum(top, 1e-30))), -100.0, 126.0)


def causal(rows, columns, shift):
    row = lax.broadcasted_iota(jnp.int32, (rows, columns), 0)
    column = lax.broadcasted_iota(jnp.int32, (rows, columns), 1)
    return column <= row + shift


def teacher_kernel(shape, rows, scale, source_of, place_ref, *refs):
    places, cores, heads, with_keys = shape
    chips = places // cores
    pieces, refs = refs[:chips], refs[chips:]
    if with_keys:
        keys, refs = refs[:cores], refs[cores:]
        x_ref, kv_ref, out_ref, energy_ref, scores_ref = refs
    else:
        kv_ref, before_ref, x_ref, out_ref, energy_ref, scores_ref = refs
    blocks, _, chunk, dim = x_ref.shape
    per_row = rows // chunk
    steps = blocks // per_row
    power = scale * math.log2(math.e)
    mask = causal(rows, rows, 0)
    place = place_ref[0]
    core = place % cores
    for j, piece in enumerate(pieces):
        base = source_of(place // cores, j) * cores
        for i in range(cores):
            block = base + (core if i == 0 else 1 - core)
            x_ref[block] = piece[i * heads : (i + 1) * heads]
            if with_keys:
                kv_ref[block] = keys[i][j]

    def finish(h, r, weighted, total):
        teacher = weighted / total
        for i in range(per_row):
            out_ref[r * per_row + i, h] = teacher[i * chunk : (i + 1) * chunk]
        return jnp.sum((teacher * teacher).reshape(rows // 8, 8, dim), axis=0)

    def take(h, r):
        return x_ref[pl.ds(r * per_row, per_row), h].reshape(rows, dim)

    def keyed(i, r, count=1):
        return kv_ref[pl.ds(r * per_row, count * per_row), i].reshape(count * rows, dim)

    def one_head(h, energy):
        parts, tops, done = [], [], []
        for r in range(steps):
            scores = dot_nt(take(h, r), keyed(0, 0, r + 1))
            last = jnp.where(mask, scores[:, r * rows :], -1e30)
            scores = beside(scores[:, : r * rows], last) if r else last
            parts.append(scores)
            tops.append(jnp.max(scores, axis=1, keepdims=True))
        for r in range(steps):
            weights = jnp.exp2((parts[r] - tops[r]) * power)
            total = jnp.sum(weights, axis=1, keepdims=True)
            done.append((dot(weights.astype(BF16), keyed(1, 0, r + 1)), total))
        for r in range(steps):
            energy = energy + finish(h, r, *done[r])
        return energy

    def one_long_head(h, energy):
        def one_row(r, energy):
            q = take(h, r)

            def look(j, top):
                scores = dot_nt(q, keyed(0, j))
                scores = jnp.where((j < r) | mask, scores, -1e30)
                scores_ref[j] = scores
                return jnp.maximum(top, jnp.max(scores, axis=1, keepdims=True))

            top = lax.fori_loop(0, r + 1, look, jnp.full((rows, 1), -1e30, F32))

            def add(j, state):
                weighted, total = state
                weights = jnp.exp2((scores_ref[j] - top) * power)
                total = total + jnp.sum(weights, axis=1, keepdims=True)
                return weighted + dot(weights.astype(BF16), keyed(1, j)), total

            weighted, total = lax.fori_loop(
                0, r + 1, add, (jnp.zeros((rows, dim), F32), jnp.zeros((rows, 1), F32))
            )
            return energy + finish(h, r, weighted, total)

        return lax.fori_loop(0, steps, one_row, energy)

    energy = jnp.zeros((8, dim), F32)
    if steps <= 8:
        for h in range(heads):
            energy = one_head(h, energy)
    else:
        energy = lax.fori_loop(0, heads, one_long_head, energy)
    energy = jnp.sum(jnp.sum(energy, axis=0, keepdims=True), axis=1, keepdims=True)
    energy = jnp.broadcast_to(energy, energy_ref.shape)
    energy_ref[...] = energy if with_keys else energy + before_ref[...]


def in_vmem(a):
    return pltpu.with_memory_space_constraint(a, pltpu.VMEM)


def teacher_call(place, pieces, kv, keys, before, places, source_of):
    _, chunk, dim = pieces[0].shape
    cores = len(keys)
    with_keys = kv is None
    heads = pieces[0].shape[0] // cores
    rows = 2 * chunk if places % 2 == 0 else chunk
    steps = places * chunk // rows
    held = (steps, rows, rows) if steps > 8 else (1, 8, 128)
    whole = pl.BlockSpec(memory_space=pltpu.VMEM)
    operands = [in_vmem(p) for p in pieces + (keys if with_keys else [kv])]
    operands += [] if with_keys else [before]
    return pl.pallas_call(
        functools.partial(
            teacher_kernel,
            (places, cores, heads, with_keys),
            rows,
            1.0 / math.sqrt(dim),
            source_of,
        ),
        in_specs=[pl.BlockSpec(memory_space=pltpu.SMEM)] + [whole] * len(operands),
        out_specs=[whole] * (3 + with_keys),
        out_shape=[pltpu.VMEM((places, heads, chunk, dim), BF16)]
        + [pltpu.VMEM((places, 2, chunk, dim), BF16)] * with_keys
        + [
            pltpu.VMEM((places, heads, chunk, dim), F32),
            jax.ShapeDtypeStruct((8, dim), F32),
        ],
        scratch_shapes=[pltpu.VMEM(held, F32)],
        compiler_params=pltpu.CompilerParams(vmem_limit_bytes=VMEM_LIMIT),
        cost_estimate=pl.CostEstimate(
            flops=10 * heads * (places * chunk) ** 2 * dim,
            bytes_accessed=8 * heads * places * chunk * dim,
            transcendentals=heads * (places * chunk) ** 2 // 2,
        ),
    )(place, *operands)


def student_kernel(
    start,
    heads,
    x_ref,
    kv_ref,
    teacher_ref,
    mq_ref,
    mk_ref,
    grad_ref,
    wq_ref,
    wk_ref,
    q_ref,
    t_ref,
    k_ref,
    before_ref,
    norm_ref,
    state_ref,
    bias_ref,
    later_ref,
    sum_q_ref,
    sum_k_ref,
):
    blocks, _, chunk, dim = x_ref.shape
    features = mq_ref.shape[1]
    both = 2 * features
    spare = grad_ref.shape[0] - heads * both
    at = [slice(h * both, (h + 1) * both) for h in range(heads)]
    per = next(p for p in (8, 4, 2, 1) if blocks % p == 0 and (p * heads <= 16 or p == 1))

    for h in range(heads):
        for source, target in ((mq_ref, wq_ref), (mk_ref, wk_ref)):
            high, low = halves(source[start + h])
            target[at[h], :] = below(beside(high, low), beside(-high, -low))
    state_ref[...] = jnp.zeros_like(state_ref)
    sum_q_ref[...] = jnp.zeros_like(sum_q_ref)
    sum_k_ref[...] = jnp.zeros_like(sum_k_ref)
    mask = causal(chunk, chunk, 0)
    mask_all = below(*[mask] * heads)
    ones = jnp.ones((chunk, dim), BF16)

    def features_of(i, carry):
        chunks = [i * per + j for j in range(per)]
        keys = [kv_ref[r, 0] for r in chunks]
        pairs = [
            beside(*halves(feature(dot_nt(wk_ref[...], beside(k, k))))) for k in keys
        ]
        wide = [beside(kv_ref[r, 1], ones) for r in chunks]
        added = [dot(p, below(w, w)) for p, w in zip(pairs, wide)]
        for r in chunks:
            for h in range(heads):
                q = x_ref[r, h]
                high, low = halves(feature(dot_nt(beside(q, q), wq_ref[at[h], :])))
                q_ref[r, at[h], :] = beside(high, low)
                t_ref[r, at[h], :] = beside(high.T, low.T)
        state = state_ref[...]
        for r, p, a in zip(chunks, pairs, added):
            k_ref[r] = p
            before_ref[r] = beside(*halves(state))
            norm_ref[r] = state[:, dim:]
            state = state + a
        state_ref[...] = state
        return carry

    lax.fori_loop(0, blocks // per, features_of, 0)
    bias_ref[...] = jnp.zeros_like(bias_ref)
    later_ref[...] = jnp.zeros_like(later_ref)

    def gradients(i, carry):
        chunks = [blocks - 1 - i * per - j for j in range(per)]
        pairs = [(r, h) for r in chunks for h in range(heads)]

        def stacked(parts):
            return [below(*parts[j * heads : (j + 1) * heads]) for j in range(per)]

        def split(parts):
            return [part[s] for part in parts for s in at]

        def weigh(r, h):
            k = k_ref[r, at[h], :]
            both_ways = dot(q_ref[r, at[h], :], below(k, k))
            return jnp.where(mask, both_ways[:, :chunk] + both_ways[:, chunk:], 0.0)

        def from_before(r, h):
            q = q_ref[r, at[h], :both]
            s = before_ref[r, at[h], :]
            return dot(beside(q, q), below(s[:, : 2 * dim], s[:, 2 * dim :]))

        inner = stacked([weigh(r, h) for r, h in pairs])
        values = [kv_ref[r, 1] for r in chunks]
        wide = [beside(v, ones) for v in values]
        state_part = stacked([from_before(r, h) for r, h in pairs])
        out = [
            dot(beside(*halves(a)), below(w, w)) + b for a, w, b in zip(inner, wide, state_part)
        ]
        inverse = [1.0 / o[:, dim:] for o in out]
        student = [o[:, :dim] * n for o, n in zip(out, inverse)]
        error = [s - below(*[teacher_ref[r, h] for h in range(heads)]) for s, r in zip(student, chunks)]
        numer = [e * n for e, n in zip(error, inverse)]
        denom = [
            -jnp.sum(e * s, axis=1, keepdims=True) * n for e, s, n in zip(error, student, inverse)
        ]
        numer_pair = [beside(*halves(n)) for n in numer]
        spread = [dot_nt(n, beside(v, v)) for n, v in zip(numer_pair, values)]
        inner_grad = [
            jnp.where(mask_all, s + d[:, :chunk], 0.0) for s, d in zip(spread, denom)
        ]
        grad_pair = [beside(*halves(g)) for g in inner_grad]
        numer_pair, grad_pair, denom = split(numer_pair), split(grad_pair), split(denom)
        query_side, from_later, later_bias = [], [], []
        for (r, h), n, g, d_full in zip(pairs, numer_pair, grad_pair, denom):
            t, k, s = t_ref[r, at[h], :], k_ref[r, at[h], :], before_ref[r, at[h], :]
            t_high, k_high = t[:, :chunk], k[:, :chunk]
            g_high, g_low = g[:, :chunk], g[:, chunk:]
            n_high, n_low = n[:, :dim], n[:, dim:]
            s_high, s_low = s[:, :dim], s[:, 2 * dim : 3 * dim]
            first = beside(n_high, g_high)
            from_later.append(dot(beside(t, t_high), below(first, first, beside(n_low, g_low))))
            grad_t = dot_nt(
                beside(k, k_high, s_high, s_high, s_low),
                beside(g_high, g_high, g_low, n_high, n_low, n_high),
            )
            d_row = d_full.T
            phi = t_high.astype(F32) + t[:, chunk:].astype(F32)
            later_bias.append(jnp.sum(phi * d_row, axis=1, keepdims=True))
            grad_t = grad_t + norm_ref[r, at[h], :] * d_row
            query_side.append(beside(*halves(grad_t * jnp.minimum(phi, 1.0))))
        for h in range(heads):
            left = beside(*[query_side[j * heads + h] for j in range(per)])
            right = below(*[x_ref[r, h] for r in chunks for _ in range(2)])
            sum_q_ref[at[h], :] += dot(left, right)
        later = later_ref[...]
        bias = bias_ref[...]
        key_side = []
        for j, (r, v) in enumerate(zip(chunks, values)):
            own = below(*from_later[j * heads : (j + 1) * heads])
            grad_t = own[:, dim:] + dot_nt(beside(*halves(later)), beside(v, v)) + bias
            pair = k_ref[r]
            slope = jnp.minimum(pair[:, :chunk].astype(F32) + pair[:, chunk:].astype(F32), 1.0)
            key_side.append(beside(*halves(grad_t * slope)))
            later = later + own[:, :dim]
            bias = bias + below(*later_bias[j * heads : (j + 1) * heads])
        sum_k_ref[...] += dot(
            beside(*key_side), below(*[kv_ref[r, 0] for r in chunks for _ in range(2)])
        )
        later_ref[...] = later
        bias_ref[...] = jnp.broadcast_to(bias, bias_ref.shape)
        return carry

    lax.fori_loop(0, blocks // per, gradients, 0)
    grad_ref[pl.ds(heads * both, spare), :] = jnp.zeros((spare, dim), F32)
    for h in range(heads):
        parts = []
        for total in (sum_q_ref, sum_k_ref):
            both_signs = total[at[h], :]
            parts.append(both_signs[:features] - both_signs[features:])
        top = jnp.max(jnp.abs(below(*parts)), axis=0, keepdims=True)
        power = power_of(jnp.max(top, axis=1, keepdims=True))
        for i, part in enumerate(parts):
            rows = pl.ds((i * heads + h) * features, features)
            grad_ref[rows, :] = part * jnp.exp2(-power)
        grad_ref[pl.ds(heads * both + h, 1), :] = jnp.broadcast_to(power, (1, dim))


def student_scratch(blocks, rows, chunk, dim):
    return [
        pltpu.VMEM((rows, 2 * dim), BF16),
        pltpu.VMEM((rows, 2 * dim), BF16),
        pltpu.VMEM((blocks, rows, 2 * chunk), BF16),
        pltpu.VMEM((blocks, rows, 2 * chunk), BF16),
        pltpu.VMEM((blocks, rows, 2 * chunk), BF16),
        pltpu.VMEM((blocks, rows, 4 * dim), BF16),
        pltpu.VMEM((blocks, rows, dim), F32),
        pltpu.VMEM((rows, 2 * dim), F32),
        pltpu.VMEM((rows, chunk), F32),
        pltpu.VMEM((rows, dim), F32),
        pltpu.VMEM((rows, dim), F32),
        pltpu.VMEM((rows, dim), F32),
    ]


def student_shape(heads, rows, dim):
    return jax.ShapeDtypeStruct((rows + (heads + 7) // 8 * 8, dim), F32)


def student_call(start, x, kv, teacher, map_query, map_key):
    blocks, heads, chunk, dim = x.shape
    features = map_query.shape[1]
    rows = heads * 2 * features
    whole = pl.BlockSpec(memory_space=pltpu.VMEM)
    return pl.pallas_call(
        functools.partial(student_kernel, start, heads),
        in_specs=[whole] * 5,
        out_specs=whole,
        out_shape=student_shape(heads, rows, dim),
        scratch_shapes=student_scratch(blocks, rows, chunk, dim),
        compiler_params=pltpu.CompilerParams(vmem_limit_bytes=VMEM_LIMIT),
        cost_estimate=pl.CostEstimate(
            flops=200 * rows * blocks * chunk * dim,
            bytes_accessed=12 * heads * blocks * chunk * dim,
            transcendentals=3 * rows * blocks * chunk,
        ),
    )(*[in_vmem(a) for a in (x, kv, teacher, map_query, map_key)])


def partner(at, step, count):
    return at ^ step if count & (count - 1) == 0 else (at + step) % count


def both_kernel(shape, rows, scale, source_of, start, place_ref, *refs):
    places, cores, heads, _ = shape
    count = places // cores + cores
    arrived, (mq_ref, mk_ref), refs = refs[:count], refs[count : count + 2], refs[count + 2 :]
    kv_ref, energy_ref, grad_ref, x_ref, out_ref, scores_ref, *scratch = refs
    teacher_kernel(
        shape, rows, scale, source_of, place_ref, *arrived, x_ref, kv_ref, out_ref, energy_ref, scores_ref
    )
    student_kernel(start, heads, x_ref, kv_ref, out_ref, mq_ref, mk_ref, grad_ref, *scratch)


def both_call(start, place, pieces, keys, map_query, map_key, places, source_of):
    _, chunk, dim = pieces[0].shape
    cores = len(keys)
    heads = pieces[0].shape[0] // cores
    rows = 2 * chunk if places % 2 == 0 else chunk
    steps = places * chunk // rows
    held = (steps, rows, rows) if steps > 8 else (1, 8, 128)
    both = heads * 2 * map_query.shape[1]
    whole = pl.BlockSpec(memory_space=pltpu.VMEM)
    operands = [in_vmem(a) for a in pieces + keys + [map_query, map_key]]
    return pl.pallas_call(
        functools.partial(
            both_kernel,
            (places, cores, heads, True),
            rows,
            1.0 / math.sqrt(dim),
            source_of,
            start,
        ),
        in_specs=[pl.BlockSpec(memory_space=pltpu.SMEM)] + [whole] * len(operands),
        out_specs=[whole] * 3,
        out_shape=[
            pltpu.VMEM((places, 2, chunk, dim), BF16),
            jax.ShapeDtypeStruct((8, dim), F32),
            student_shape(heads, both, dim),
        ],
        scratch_shapes=[
            pltpu.VMEM((places, heads, chunk, dim), BF16),
            pltpu.VMEM((places, heads, chunk, dim), F32),
            pltpu.VMEM(held, F32),
        ]
        + student_scratch(places, both, chunk, dim),
        compiler_params=pltpu.CompilerParams(vmem_limit_bytes=VMEM_LIMIT),
        cost_estimate=pl.CostEstimate(
            flops=200 * both * places * chunk * dim + 10 * heads * (places * chunk) ** 2 * dim,
            bytes_accessed=20 * heads * places * chunk * dim,
            transcendentals=heads * (places * chunk) ** 2 // 2,
        ),
    )(place, *operands)


def exchange(queries, key_states, value_vector_states, heads, parts):
    places = lax.axis_size("ctx")
    cores = 2 if places % 2 == 0 else 1
    chips = places // cores
    place = lax.axis_index("ctx")
    core, chip = place % cores, place // cores
    tokens, query_heads, dim = queries.shape
    key_heads = key_states.shape[1]
    padding = heads * places - query_heads
    mirrored = chips & (chips - 1) == 0

    def target_of(at, j):
        return partner(at, j, chips)

    def source_of(at, j):
        return at ^ j if mirrored else (at + chips - j) % chips

    def send(a, j):
        return lax.ppermute(
            a, "ctx", [(i, target_of(i // cores, j) * cores + i % cores) for i in range(places)]
        )

    def swap(a):
        return lax.ppermute(a, "ctx", [(i, i ^ 1) for i in range(places)])

    def pick(a, i, axis=0):
        return lax.dynamic_index_in_dim(a, i, axis, False)

    by_head = jnp.pad(queries, ((0, 0), (0, padding), (0, 0))) if padding else queries
    by_head = by_head.transpose(1, 0, 2).reshape(chips, cores, heads, tokens, dim)
    *flat, by_head = lax.optimization_barrier((key_states, value_vector_states, by_head))
    flat = [a.reshape(tokens, key_heads * dim) for a in flat]
    kv = jnp.stack(
        [jnp.stack([a[:, g * dim : (g + 1) * dim] for a in flat]) for g in range(key_heads)]
    )
    def group_of(at):
        first = jnp.minimum((at * cores + core) * heads, query_heads - 1)
        return first // (query_heads // key_heads)

    mine = [pick(by_head, core, 1)]
    if cores == 2:
        mine.append(swap(pick(by_head, 1 - core, 1)))
        kv = lax.optimization_barrier((kv, mine[1]))[0]
    to_send = [pick(kv, group_of(target_of(chip, j))) for j in range(chips)]
    arrived = []
    for start, stop in parts:
        pieces = []
        for j in range(chips):
            piece = [pick(q, target_of(chip, j))[start:stop] for q in mine]
            if j == 1 and not arrived:
                piece.append(to_send[j])
            pieces.append(jnp.concatenate(piece))
        if arrived and chips > 1:
            pieces = lax.optimization_barrier((*pieces, arrived[-1][1]))[:chips]
        arrived.append([pieces[0]] + [send(a, j) for j, a in enumerate(pieces) if j])
    own_keys = [send(a, j) if j > 1 else a for j, a in enumerate(to_send)]
    if chips > 1:
        own_keys[1] = arrived[0][1][-2:]
    keys = [jnp.stack(own_keys)]
    if cores == 2:
        keys.append(swap(keys[0]))
    return arrived, keys, source_of


def unpack_kernel(heads, power_rows, tail_row, scale, gathered_ref, *refs):
    *out_refs, held_ref, sems = refs
    places, _, dim = gathered_ref.shape
    features = out_refs[0].shape[1]
    runs = sems.shape[1]
    per = places // runs
    copies = []

    def row(p, i):
        return gathered_ref[p, i : i + 1, :]

    energy = jnp.zeros((1, dim), F32)
    for p in range(places):
        near_one = row(p, tail_row + 1) + row(p, tail_row + 2) * (1.0 / 1024.0)
        energy = energy + near_one * jnp.exp2(row(p, tail_row))
    scale = scale / energy
    for run in range(runs):
        for p in range(run * per, (run + 1) * per):
            for h in range(heads):
                factor = jnp.exp2(row(p, power_rows[h])) * scale
                for i in range(2):
                    rows = pl.ds((i * heads + h) * features, features)
                    held_ref[i, p * heads + h] = gathered_ref[p, rows, :] * factor
        done = pl.ds(run * per * heads, per * heads)
        for i, out_ref in enumerate(out_refs):
            copy = pltpu.make_async_copy(held_ref.at[i, done], out_ref.at[done], sems.at[i, run])
            copy.start()
            copies.append(copy)
    for copy in copies:
        copy.wait()


def unpack_call(gathered, heads, features, power_rows, tail_row, scale):
    places, _, dim = gathered.shape
    runs = 4 if places % 4 == 0 else 1
    whole = pl.BlockSpec(memory_space=pltpu.VMEM)
    return pl.pallas_call(
        functools.partial(unpack_kernel, heads, power_rows, tail_row, scale),
        in_specs=[whole],
        out_specs=[pl.BlockSpec(memory_space=pl.ANY)] * 2,
        out_shape=[jax.ShapeDtypeStruct((places * heads, features, dim), F32)] * 2,
        scratch_shapes=[
            pltpu.VMEM((2, places * heads, features, dim), F32),
            pltpu.SemaphoreType.DMA((2, runs)),
        ],
        compiler_params=pltpu.CompilerParams(vmem_limit_bytes=VMEM_LIMIT),
    )(gathered)


def on_device(queries, key_states, value_vector_states, map_query, map_key):
    places = lax.axis_size("ctx")
    planes = lax.axis_size("head")
    place = lax.axis_index("ctx")
    tokens, query_heads, dim = queries.shape
    key_heads = key_states.shape[1]
    features = map_query.shape[2]
    group = query_heads // key_heads
    heads = min(d for d in range(1, group + 1) if group % d == 0 and d * places >= query_heads)
    padding = heads * places - query_heads
    half = heads // 2
    parts = [(0, half), (half, heads)] if half else [(0, heads)]
    arrived, keys, source_of = exchange(queries, key_states, value_vector_states, heads, parts)

    def own(weights):
        weights = weights.transpose(0, 2, 1)
        weights = jnp.pad(weights, ((0, padding), (0, 0), (0, 0))) if padding else weights
        return lax.dynamic_slice_in_dim(weights, place * heads, heads, 0)

    own_query, own_key = own(map_query), own(map_key)
    position = place.astype(jnp.int32).reshape(1)
    kv, energy, grads, powers = None, None, [], []
    for (start, stop), pieces in zip(parts, arrived):
        if stop < heads:
            kv, energy, result = both_call(
                start, position, pieces, keys, own_query, own_key, places, source_of
            )
        else:
            x, *found = teacher_call(position, pieces, kv, keys, energy, places, source_of)
            if kv is None:
                kv = found.pop(0)
            teacher, energy = found
            result = student_call(start, x, kv, teacher, own_query, own_key)
        rows = (stop - start) * features
        grads.append((result[:rows], result[rows : 2 * rows]))
        powers.append(result[2 * rows :])
    if padding:
        energy = jnp.where(place * heads < query_heads, energy, 0.0)
    shifted = [
        lax.ppermute(energy, "head", [(i, partner(i, k, planes)) for i in range(planes)])
        for k in range(1, planes)
    ]
    energy = sum(shifted, energy)
    power = power_of(energy)
    near_one = energy * jnp.exp2(-power)
    first = lax.reduce_precision(near_one, 5, 10)
    row = lax.broadcasted_iota(jnp.int32, energy.shape, 0)
    tail = jnp.where(row == 0, power, jnp.where(row == 1, first, (near_one - first) * 1024.0))
    grads = [part for side in zip(*grads) for part in side]
    sent = jnp.concatenate(grads + powers + [tail]).astype(F16)
    used = sent.shape[0]
    gathered = lax.all_gather(jnp.pad(sent, ((0, -used % 16), (0, 0))), "ctx").astype(F32)
    power_rows, at = [], heads * 2 * features
    for (start, stop), p in zip(parts, powers):
        power_rows += [at + h for h in range(stop - start)]
        at += p.shape[0]
    scale = 2.0 * query_heads * planes
    unpacked = unpack_call(in_vmem(gathered), heads, features, power_rows, at, scale)
    return tuple(a[:query_heads].transpose(0, 2, 1) for a in unpacked)


def solution(mesh):
    placed = (
        P("ctx", "head", None),
        P("ctx", "head", None),
        P("ctx", "head", None),
        P("head", None, None),
        P("head", None, None),
    )
    return jax.shard_map(
        on_device,
        mesh=mesh,
        in_specs=placed,
        out_specs=(P("head", None, None), P("head", None, None)),
        check_vma=False,
    )
```
